32 devices in a mesh: ctx: 2 (over x), vocab: 4 (over z), rep: 4 (over y, core).
Axes of the slice: x: 2, y: 2, z: 4, core: 2. Of those that a mesh axis runs over, the one named last changes fastest.
Arguments:
- queries: bfloat16 [8, 512, 8192], P('rep', 'ctx', 'vocab'), may hold values from -10 to 10
- key_value: bfloat16 [2, 8, 512, 512], P(None, 'rep', 'ctx'), may hold values from -10 to 10
- residual: bfloat16 [8, 512, 4096], P('rep', ('ctx', 'vocab')), may hold values from -6 to 6
- out_weight: bfloat16 [8192, 4096], P('vocab', ('ctx', 'rep')), may hold values from -0.5 to 0.5
- moe_gain: float32 [4096], replicated, may hold values from 0.1 to 1.9
- expert_ids: int32 [8, 512, 8], P('rep', ('ctx', 'vocab')), may hold values from 0 to 127, as said below
- route_gate: float32 [8, 512, 8], P('rep', ('ctx', 'vocab')), may hold values from 0.25 to 2.5
- gate_weight: bfloat16 [4, 1536, 4096], P('vocab', 'ctx'), may hold values from -0.09375 to 0.09375
- up_weight: bfloat16 [4, 1536, 4096], P('vocab', 'ctx'), may hold values from -0.09375 to 0.09375
- down_weight: bfloat16 [4, 1536, 4096], P('vocab', 'ctx'), may hold values from -0.15625 to 0.15625
- final_gain: float32 [4096], replicated, may hold values from 0.5 to 1.5
- teacher_head: bfloat16 [1536, 4096], P('vocab'), may hold values from -6 to 6
- learner_hidden: bfloat16 [8, 512, 4096], P('rep', ('ctx', 'vocab')), may hold values from -6 to 6
- learner_head: bfloat16 [1536, 4096], P('vocab', ('ctx', 'rep')), may hold values from -6 to 6
- lengths: int32 [8], P('rep'), may hold values from 128 to 512
Outputs:
- hidden_grad: bfloat16 [8, 512, 4096], P('rep', ('ctx', 'vocab'))
- head_grad: bfloat16 [1536, 4096], P('vocab', ('ctx', 'rep'))
- row_kl: float32 [8, 512], P('rep', ('ctx', 'vocab'))
The draws below stay inside these ranges and needn't reach their ends.
Inputs may be any that keep to these rules, and one draw needn't show every extreme that they name: `expert_ids`: each token names 8 different experts. In the rows of one device (one index of every axis) every token names exactly one expert below 4, and each expert below 4 is named by exactly 32 of those tokens.
All inputs are finite; a program needn't handle non-finite values.
Results may differ from the reference program's by a relative error of at most 0.017.
Values may be sent and summed in bfloat16 or wider, within the bound.
No kernel may reach another device: no remote copies, remote signals or barrier semaphores. Data moves between devices by JAX's collectives and lax.ppermute only.
A program may use at most 128 MiB of HBM per device.

```python
import math
import jax
import jax.numpy as jnp
from jax import lax

D = 4096
QH = 64
KVH = 4
HD = 128
FFE = 1536
EXPERTS = 128
TOPK = 8
VOC_DEV = 384
SLAB = 512
SEQ_DEV = 2
SEQS = 8
VOCAB = 1536
EXP_WIN = 4
N_CTX = 2
N_VOCAB = 4
N_REP = 4


def block_order(block_key):
    return jax.random.permutation(block_key, SEQ_DEV * (SLAB // (N_CTX * N_VOCAB)))


def draw_expert_ids(key, part):
    key = jax.random.fold_in(key, 11)
    block_count = N_REP * N_CTX * N_VOCAB
    pos_dev = SLAB // (N_CTX * N_VOCAB)
    block_keys = jax.random.split(jax.random.fold_in(key, 1), block_count)
    orders = jax.vmap(block_order)(block_keys)
    window = (orders % N_VOCAB).astype(jnp.int32)
    window = window.reshape(N_REP, N_CTX * N_VOCAB, SEQ_DEV, pos_dev)
    window = jnp.transpose(window, (0, 2, 1, 3)).reshape(SEQS, SLAB)
    remaining = EXPERTS - N_VOCAB
    scores = jax.random.randint(jax.random.fold_in(key, 2), (SEQS, SLAB, remaining), 0, 1 << 20, dtype=jnp.int32)
    scores = scores * 128 + jnp.arange(remaining, dtype=jnp.int32)
    others = jnp.argsort(scores, axis=-1, stable=True)[..., :TOPK - 1].astype(jnp.int32) + N_VOCAB
    placement = jax.random.randint(jax.random.fold_in(key, 3), (SEQS, SLAB, 1), 0, TOPK, dtype=jnp.int32)
    columns = jnp.arange(TOPK, dtype=jnp.int32)[None, None, :]
    source = jnp.clip(columns - (columns > placement).astype(jnp.int32), 0, TOPK - 2)
    source = jnp.broadcast_to(source, (SEQS, SLAB, TOPK))
    picked = jnp.take_along_axis(others, source, axis=-1)
    return jnp.where(columns == placement, window[..., None], picked).astype(jnp.int32)


def draw_queries(key, part):
    key = jax.random.fold_in(key, 21)
    values = jnp.clip(jax.random.normal(key, (SEQS, SLAB, QH * HD), jnp.float32), -6.0, 6.0)
    return values.astype(jnp.bfloat16)


def draw_key_value(key, part):
    key = jax.random.fold_in(key, 22)
    values = jnp.clip(jax.random.normal(key, (2, SEQS, SLAB, KVH * HD), jnp.float32), -6.0, 6.0)
    return values.astype(jnp.bfloat16)


def draw_residual(key, part):
    key = jax.random.fold_in(key, 23)
    values = jnp.clip(jax.random.normal(key, (SEQS, SLAB, D), jnp.float32), -6.0, 6.0)
    return values.astype(jnp.bfloat16)


def draw_learner_hidden(key, part):
    key = jax.random.fold_in(key, 24)
    values = jnp.clip(jax.random.normal(key, (SEQS, SLAB, D), jnp.float32), -6.0, 6.0)
    return values.astype(jnp.bfloat16)


def draw_teacher_head(key, part):
    key = jax.random.fold_in(key, 25)
    values = jnp.clip(jax.random.normal(key, (VOCAB, D), jnp.float32), -6.0, 6.0) * (D // 9) ** (-0.5)
    return values.astype(jnp.bfloat16)


def draw_learner_head(key, part):
    key = jax.random.fold_in(key, 26)
    values = jnp.clip(jax.random.normal(key, (VOCAB, D), jnp.float32), -6.0, 6.0) * (D // 9) ** (-0.5)
    return values.astype(jnp.bfloat16)


def touch_ends(values, own_key, least, top_value):
    longest = values.shape.index(max(values.shape))
    spots = []
    for shift in (0, 1):
        where = [jax.random.randint(jax.random.fold_in(own_key, axis), (), 0, length) for axis, length in enumerate(values.shape)]
        where[longest] = (where[longest] + shift) % values.shape[longest]
        spots.append(tuple(where))
    return values.at[spots[0]].set(least).at[spots[1]].set(top_value)


def block_levels(rng, dims, shards, smallest, top_value):
    loudness = 1.0
    for position, shards_of in shards:
        draws = jax.random.uniform(jax.random.fold_in(jax.random.fold_in(rng, 6), position), (shards_of,), jnp.float32, smallest / len(shards), top_value / len(shards))
        loudness = loudness * jnp.repeat(jnp.exp(draws), dims[position] // shards_of).reshape((-1,) + (1,) * (len(dims) - 1 - position))
    return loudness


def bell_draw(stream_key, dims, spread, most, cuts=(), kind=jnp.bfloat16):
    array = jax.random.normal(stream_key, dims, jnp.float32) * spread
    if len(cuts) > 0:
        array = block_levels(stream_key, dims, cuts, -0.22, 0.18) * array
    return jnp.clip(array, min=-most, max=most).astype(kind)


def setup_inputs(seed: int = 0) -> dict:
    key_of = jax.random.split(jax.random.key(seed), 16)
    queries = draw_queries(jax.random.fold_in(key_of[15], 71), 0)
    key_value = draw_key_value(jax.random.fold_in(key_of[15], 71), 0)
    residual = draw_residual(jax.random.fold_in(key_of[15], 71), 0)
    out_weight = bell_draw(key_of[3], (QH * HD, D), (QH * HD // 64) ** -0.5, 0.5, ((0, 4), (1, 8)))
    moe_gain = jnp.clip(1.0 + 0.18 * jax.random.normal(key_of[4], (D,), jnp.float32), 0.1, 1.9)
    expert_ids = draw_expert_ids(jax.random.fold_in(key_of[15], 71), 0)
    route_gate = jnp.clip(jnp.exp(math.log(2.5) - 2.3025851 * jax.random.uniform(key_of[6], (SEQS, SLAB, TOPK), jnp.float32) ** block_levels(key_of[6], (SEQS, SLAB, TOPK), ((0, 4), (1, 8)), -0.2, 0.2)), 0.25, 2.5)
    gate_weight = bell_draw(key_of[7], (EXP_WIN, FFE, D), D ** -0.5, 0.09375, ((0, 4), (1, 2)))
    up_weight = bell_draw(key_of[8], (EXP_WIN, FFE, D), D ** -0.5, 0.09375, ((0, 4), (1, 2)))
    down_weight = bell_draw(key_of[9], (EXP_WIN, FFE, D), FFE ** -0.5, 0.15625, ((0, 4), (1, 2)))
    final_gain = jnp.clip(1.0 + 0.1 * jax.random.normal(key_of[10], (D,), jnp.float32), 0.5, 1.5)
    teacher_head = draw_teacher_head(jax.random.fold_in(key_of[15], 71), 0)
    learner_hidden = draw_learner_hidden(jax.random.fold_in(key_of[15], 71), 0)
    learner_head = draw_learner_head(jax.random.fold_in(key_of[15], 71), 0)
    lengths = touch_ends(jax.random.randint(key_of[14], (SEQS,), SLAB // 4, SLAB + 1), jax.random.fold_in(key_of[14], 1), SLAB // 4, SLAB).astype(jnp.int32)
    return {"queries": queries, "key_value": key_value, "residual": residual, "out_weight": out_weight, "moe_gain": moe_gain, "expert_ids": expert_ids, "route_gate": route_gate, "gate_weight": gate_weight, "up_weight": up_weight, "down_weight": down_weight, "final_gain": final_gain, "teacher_head": teacher_head, "learner_hidden": learner_hidden, "learner_head": learner_head, "lengths": lengths}


EPSILON = 1e-06
MASKED = -1e+30

def rms_scale(values, gain):
    mean_square = lax.optimization_barrier(jnp.mean(values * values, axis=-1, keepdims=True))
    return values * lax.rsqrt(mean_square + EPSILON) * gain

def attend_sequence(inputs):
    query_seq, key_seq, value_seq, length = inputs
    positions = jnp.arange(SLAB)
    query_heads = query_seq.astype(jnp.float32).reshape(SLAB, QH, HD)
    key_heads = jnp.repeat(key_seq.astype(jnp.float32).reshape(SLAB, KVH, HD), QH // KVH, axis=1)
    value_heads = jnp.repeat(value_seq.astype(jnp.float32).reshape(SLAB, KVH, HD), QH // KVH, axis=1)
    scores = jnp.einsum('qhd,khd->hqk', query_heads, key_heads) * HD ** (-0.5)
    allowed = (positions[None, :] <= positions[:, None]) & (positions[None, :] < length)
    scores = jnp.where(allowed[None], scores, MASKED)
    row_peak = lax.optimization_barrier(jnp.max(scores, axis=-1, keepdims=True))
    exponent = jnp.where(allowed[None], jnp.exp(scores - row_peak), 0.0)
    exp_total = lax.optimization_barrier(jnp.sum(exponent, axis=-1))
    rounded = lax.optimization_barrier(exponent.astype(jnp.bfloat16)).astype(jnp.float32)
    attended = jnp.einsum('hqk,khd->qhd', rounded, value_heads) / jnp.transpose(exp_total)[:, :, None]
    return attended.reshape(SLAB, QH * HD).astype(jnp.bfloat16)

def run_expert(inputs):
    rows_in, gate_rows, up_rows, down_rows = inputs
    gate_pre = jnp.dot(rows_in, gate_rows.T, preferred_element_type=jnp.float32)
    up_pre = jnp.dot(rows_in, up_rows.T, preferred_element_type=jnp.float32)
    activated = (jax.nn.silu(gate_pre) * up_pre).astype(jnp.bfloat16)
    slice_width = FFE // N_CTX
    summed = jnp.zeros((rows_in.shape[0], rows_in.shape[1]), jnp.float32)
    for column_part in range(N_CTX):
        lower = column_part * slice_width
        piece_out = jnp.dot(activated[:, lower:lower + slice_width], down_rows[lower:lower + slice_width], preferred_element_type=jnp.float32)
        summed = summed + lax.optimization_barrier(piece_out.astype(jnp.bfloat16)).astype(jnp.float32)
    return summed.astype(jnp.bfloat16)

def reference(queries, key_value, residual, out_weight, moe_gain, expert_ids, route_gate, gate_weight, up_weight, down_weight, final_gain, teacher_head, learner_hidden, learner_head, lengths):
    attended = lax.map(attend_sequence, (queries, key_value[0], key_value[1], lengths))
    row_total = SEQS * SLAB
    width = residual.shape[2]
    flat_heads = attended.reshape(row_total, QH * HD)
    head_part = QH * HD // N_VOCAB
    attn_rows = jnp.zeros((row_total, width), jnp.float32)
    for section in range(N_VOCAB):
        lower = section * head_part
        partial_rows = jnp.dot(flat_heads[:, lower:lower + head_part], out_weight[lower:lower + head_part], preferred_element_type=jnp.float32)
        attn_rows = attn_rows + lax.optimization_barrier(partial_rows.astype(jnp.bfloat16)).astype(jnp.float32)
    hidden_one = residual.reshape(row_total, width).astype(jnp.float32) + attn_rows
    normed = rms_scale(hidden_one, moe_gain).astype(jnp.bfloat16)
    route_ids = expert_ids.reshape(row_total, TOPK)
    inside = route_ids < N_VOCAB
    chosen = lax.optimization_barrier(jnp.sum(jnp.where(inside, route_ids, 0), axis=1)).astype(jnp.int32)
    route_weight = lax.optimization_barrier(jnp.sum(jnp.where(inside, route_gate.reshape(row_total, TOPK), 0.0), axis=1))
    order = jnp.argsort(chosen, stable=True).astype(jnp.int32)
    grouped = normed[order].reshape(N_VOCAB, row_total // N_VOCAB, width)
    expert_out = lax.map(run_expert, (grouped, gate_weight, up_weight, down_weight))
    inverse = jnp.argsort(order).astype(jnp.int32)
    moe_rows = expert_out.reshape(row_total, width)[inverse].astype(jnp.float32)
    hidden_two = hidden_one + route_weight[:, None] * moe_rows
    final_rows = rms_scale(hidden_two, final_gain).astype(jnp.bfloat16)
    learner_flat = learner_hidden.reshape(row_total, width)
    teacher_logits = jnp.dot(final_rows, teacher_head.T, preferred_element_type=jnp.float32)
    learner_logits = jnp.dot(learner_flat, learner_head.T, preferred_element_type=jnp.float32)
    learner_peak = lax.optimization_barrier(jnp.max(learner_logits, axis=1, keepdims=True))
    learner_lse = learner_peak + jnp.log(lax.optimization_barrier(jnp.sum(jnp.exp(learner_logits - learner_peak), axis=1, keepdims=True)))
    teacher_peak = lax.optimization_barrier(jnp.max(teacher_logits, axis=1, keepdims=True))
    teacher_lse = teacher_peak + jnp.log(lax.optimization_barrier(jnp.sum(jnp.exp(teacher_logits - teacher_peak), axis=1, keepdims=True)))
    learner_prob = jnp.exp(learner_logits - learner_lse)
    logit_gap = learner_logits - teacher_logits
    mean_gap = lax.optimization_barrier(jnp.sum(learner_prob * logit_gap, axis=1, keepdims=True))
    divergence = mean_gap - learner_lse + teacher_lse
    positions = jnp.arange(SLAB)
    live_rows = (positions[None, :] < lengths[:, None]).reshape(row_total, 1)
    row_kl = jnp.where(live_rows, divergence, 0.0).reshape(SEQS, SLAB)
    dlogits = jnp.where(live_rows, learner_prob * (logit_gap - mean_gap), 0.0).astype(jnp.bfloat16)
    grad_total = jnp.zeros((row_total, width), jnp.float32)
    for section in range(N_VOCAB):
        lower = section * VOC_DEV
        grad_part = jnp.dot(dlogits[:, lower:lower + VOC_DEV], learner_head[lower:lower + VOC_DEV], preferred_element_type=jnp.float32)
        grad_total = grad_total + lax.optimization_barrier(grad_part.astype(jnp.bfloat16)).astype(jnp.float32)
    hidden_grad = grad_total.astype(jnp.bfloat16).reshape(SEQS, SLAB, width)
    head_grad = lax.dot_general(dlogits, learner_flat, (((0,), (0,)), ((), ())), preferred_element_type=jnp.float32).astype(jnp.bfloat16)
    return (hidden_grad, head_grad, row_kl)
```

```python
import jax
import jax.numpy as jnp
from jax import lax
from jax.sharding import PartitionSpec as P

QH = 64
KVH = 4
HD = 128

EPSILON = 1e-06
MASKED = -1e30
PLANE = ("ctx", "rep")
LAST = (((1,), (1,)), ((), ()))
FIRST = (((0,), (0,)), ((), ()))
F32 = jnp.float32
BF16 = jnp.bfloat16


def matmul(left, right, dims=(((1,), (0,)), ((), ()))):
    return lax.dot_general(left, right, dims, preferred_element_type=F32)


def rms_scale(values, gain):
    mean_square = jnp.mean(values * values, axis=-1, keepdims=True)
    return values * lax.rsqrt(mean_square + EPSILON) * gain


def after(value, *earlier):
    return lax.optimization_barrier((value, *earlier))[0]


def plane_index():
    return lax.axis_index("ctx") * lax.axis_size("rep") + lax.axis_index("rep")


def is_square():
    return lax.axis_size("ctx") == 2 and lax.axis_size("rep") == 4


def plane_swap(value, offset):
    ranks = lax.axis_size("ctx") * lax.axis_size("rep")
    return lax.ppermute(value, PLANE, [(i, i ^ offset) for i in range(ranks)])


def plane_gather(own):
    if not is_square():
        gathered = lax.all_gather(own, PLANE, axis=0, tiled=False)
        index = plane_index()
        return [
            lax.dynamic_index_in_dim(gathered, index ^ r, 0, keepdims=False)
            for r in range(gathered.shape[0])
        ]
    core = plane_swap(own, 1)
    along_x = plane_swap(own, 4)
    along_y = plane_swap(own, 2)
    half = own.shape[0] // 2
    corner = jnp.concatenate([plane_swap(along_y[:half], 4), plane_swap(along_x[half:], 2)], axis=0)
    return [
        own,
        core,
        along_y,
        plane_swap(along_y, 1),
        along_x,
        plane_swap(along_x, 1),
        corner,
        plane_swap(corner, 1),
    ]


def plane_exchange(blocks):
    return [blocks[0]] + [plane_swap(blocks[r], r) for r in range(1, len(blocks))]


def pick(value, index, size, axis):
    return lax.dynamic_slice_in_dim(value, index * size, size, axis)


def split_relative(value, index, count, axis):
    size = value.shape[axis] // count
    return [pick(value, index ^ r, size, axis) for r in range(count)]


def join_absolute(blocks, index, axis):
    stacked = jnp.stack(blocks)
    return jnp.concatenate(
        [
            lax.dynamic_index_in_dim(stacked, index ^ j, 0, keepdims=False)
            for j in range(len(blocks))
        ],
        axis=axis,
    )


def line_exchange(value):
    count = lax.axis_size("vocab")
    index = lax.axis_index("vocab")
    blocks = split_relative(value, index, count, 0)
    received = [blocks[0]] + [
        lax.ppermute(blocks[r], "vocab", [(i, i ^ r) for i in range(count)])
        for r in range(1, count)
    ]
    return join_absolute(received, index, 0)


def line_gather(own):
    count = lax.axis_size("vocab")
    index = lax.axis_index("vocab")
    from_left, from_right = [own], [own]
    for _ in range(count - 1):
        from_left.append(
            lax.ppermute(from_left[-1], "vocab", [(i, i + 1) for i in range(count - 1)])
        )
        from_right.append(
            lax.ppermute(from_right[-1], "vocab", [(i + 1, i) for i in range(count - 1)])
        )
    blocks = []
    for j in range(count):
        block = own
        for distance in range(1, count):
            if j + distance < count:
                block = jnp.where(index == j + distance, from_left[distance], block)
            if j - distance >= 0:
                block = jnp.where(index == j - distance, from_right[distance], block)
        blocks.append(block)
    return jnp.stack(blocks)


def line_reduce(partial):
    count = lax.axis_size("vocab")
    index = lax.axis_index("vocab")
    size = partial.shape[0] // count
    to_right = to_left = None
    for step in range(1, count):
        ahead = count - step
        right = pick(partial, jnp.minimum(index + ahead, count - 1), size, 0)
        left = pick(partial, jnp.maximum(index - ahead, 0), size, 0)
        if to_right is not None:
            right = (right.astype(F32) + to_right.astype(F32)).astype(BF16)
            left = (left.astype(F32) + to_left.astype(F32)).astype(BF16)
        to_right = lax.ppermute(right, "vocab", [(i, i + 1) for i in range(min(step, count - 1))])
        to_left = lax.ppermute(
            left, "vocab", [(i, i - 1) for i in range(max(count - step, 1), count)]
        )
    own = pick(partial, index, size, 0).astype(F32)
    return own + to_right.astype(F32) + to_left.astype(F32)


def attend(queries, key_value, lengths):
    seq_dev, pos_ctx, head_cols = queries.shape
    heads_dev = head_cols // HD
    ctx_index = lax.axis_index("ctx")
    shared_head = lax.axis_index("vocab") * heads_dev // (QH // KVH)
    own_rows = lax.dynamic_slice_in_dim(key_value, shared_head * HD, HD, 3)
    query_heads = queries.reshape(seq_dev, pos_ctx, heads_dev, HD)
    query_pos = ctx_index * pos_ctx + jnp.arange(pos_ctx)
    if lax.axis_size("ctx") == 2:
        earlier = lax.ppermute(own_rows, "ctx", [(0, 1)])
        rows = jnp.concatenate([earlier, own_rows], axis=2)
        key_pos = jnp.arange(2 * pos_ctx) + (ctx_index - 1) * pos_ctx
    else:
        rows = lax.all_gather(own_rows, "ctx", axis=2, tiled=True)
        key_pos = jnp.arange(rows.shape[2])
    scores = jnp.einsum("sqhd,skd->sqhk", query_heads, rows[0], preferred_element_type=F32) * HD ** (
        -0.5
    )
    allowed = (
        (key_pos[None, None, :] <= query_pos[None, :, None])
        & (key_pos[None, None, :] < lengths[:, None, None])
        & (key_pos[None, None, :] >= 0)
    )
    allowed = allowed[:, :, None, :]
    scores = jnp.where(allowed, scores, MASKED)
    peak = jnp.max(scores, axis=-1)
    exponent = jnp.where(allowed, jnp.exp(scores - peak[..., None]), 0.0)
    total = jnp.sum(exponent, axis=-1)
    weighted = jnp.einsum(
        "sqhk,skd->sqhd", exponent.astype(BF16), rows[1], preferred_element_type=F32
    )
    return (weighted / total[..., None]).astype(BF16).reshape(seq_dev * pos_ctx, head_cols)


def per_device(
    queries,
    key_value,
    residual,
    out_weight,
    moe_gain,
    expert_ids,
    route_gate,
    gate_weight,
    up_weight,
    down_weight,
    final_gain,
    teacher_head,
    learner_hidden,
    learner_head,
    lengths,
):
    seq_dev, pos_ctx, _ = queries.shape
    pos_dev, width = residual.shape[1:]
    own_count = seq_dev * pos_dev
    vocab_count = lax.axis_size("vocab")
    plane_count = lax.axis_size("ctx") * lax.axis_size("rep")
    ctx_index = lax.axis_index("ctx")
    vocab_index = lax.axis_index("vocab")
    plane = plane_index()
    per_expert = own_count // vocab_count

    route_ids = expert_ids.reshape(own_count, -1)
    inside = route_ids < vocab_count
    chosen = jnp.sum(jnp.where(inside, route_ids, 0), axis=1)
    route_weight = jnp.sum(jnp.where(inside, route_gate.reshape(own_count, -1), 0.0), axis=1)
    member = (chosen[:, None] == jnp.arange(vocab_count)[None, :]).astype(jnp.int32)
    slot_rank = jnp.sum((jnp.cumsum(member, axis=0) - 1) * member, axis=1)
    target = chosen * per_expert + slot_rank
    placed = target[None, :] == jnp.arange(own_count)[:, None]
    placer = placed.astype(BF16)

    line_target = chosen * own_count + vocab_index * per_expert + slot_rank
    line_facts = line_gather(jnp.stack([line_target.astype(F32), route_weight]))
    line_target = line_facts[:, 0].astype(jnp.int32)
    line_weight = line_facts[:, 1]
    line_tokens = (
        jnp.swapaxes(line_target.reshape(vocab_count, seq_dev, pos_dev), 0, 1).reshape(-1)
    )
    line_placer = (line_tokens[None, :] == jnp.arange(seq_dev * pos_ctx)[:, None]).astype(BF16)
    mine = vocab_index * own_count + jnp.arange(own_count)
    my_weight = jnp.sum(
        jnp.where(line_target.reshape(1, -1) == mine[:, None], line_weight.reshape(1, -1), 0.0),
        axis=1,
    )

    residual_rows = line_exchange(
        matmul(placer, residual.reshape(own_count, width)).astype(BF16)
    )

    weight_blocks = plane_gather(out_weight)
    heads_out = attend(queries, key_value, lengths)
    heads_sorted = matmul(line_placer, heads_out).astype(BF16)

    teacher_line = line_gather(pick(teacher_head, plane, width // plane_count, 1))
    learner_line = line_gather(learner_head)

    attn_blocks = [None] * plane_count
    group = 2 if plane_count % 2 == 0 else 1
    order = [0, 2, 1, 3] if plane_count == 8 else range(plane_count // group)
    for start in order:
        members = range(start * group, start * group + group)
        part = jnp.concatenate(
            [matmul(heads_sorted, weight_blocks[r]).astype(BF16) for r in members], axis=1
        )
        for r, piece in zip(members, jnp.split(line_reduce(part), group, axis=1)):
            attn_blocks[r] = piece
    attn_rows = join_absolute(attn_blocks, plane, 1)

    vocab = vocab_count * teacher_head.shape[0]
    teacher_line = after(teacher_line, weight_blocks[-1])
    learner_line = after(learner_line, weight_blocks[-1])
    teacher_blocks = plane_gather(teacher_line.reshape(vocab, -1))
    learner_blocks = plane_gather(learner_line.reshape(vocab, -1))

    learner_rows = matmul(placer, learner_hidden.reshape(own_count, width)).astype(BF16)
    learner_columns = split_relative(learner_rows, plane, plane_count, 1)
    learner_logits = sum(
        matmul(rows, block, LAST) for rows, block in zip(learner_columns, learner_blocks)
    )
    learner_peak = jnp.max(learner_logits, axis=1, keepdims=True)
    learner_exp = jnp.exp(learner_logits - learner_peak)
    learner_total = jnp.sum(learner_exp, axis=1, keepdims=True)
    learner_lse = learner_peak + jnp.log(learner_total)
    plane_columns = jnp.concatenate(plane_exchange(learner_columns), axis=0)

    hidden_one = residual_rows.astype(F32) + attn_rows
    normed = rms_scale(hidden_one, moe_gain).astype(BF16)
    pair = lax.axis_size("ctx") == 2
    if pair:
        other = lax.ppermute(normed, "ctx", [(0, 1), (1, 0)])
        rows = jnp.concatenate([normed, other], axis=0)
    else:
        rows = lax.all_gather(normed, "ctx", axis=0, tiled=True)
    gate_pre = matmul(rows, gate_weight[0], LAST)
    up_pre = matmul(rows, up_weight[0], LAST)
    activated = (jax.nn.silu(gate_pre) * up_pre).astype(BF16)
    if pair:
        theirs = matmul(activated[own_count:], down_weight[0]).astype(BF16)
        theirs = lax.ppermute(theirs, "ctx", [(0, 1), (1, 0)])
        ours = matmul(activated[:own_count], down_weight[0]).astype(BF16)
        expert_out = (ours.astype(F32) + theirs.astype(F32)).astype(BF16)
    else:
        terms = matmul(activated, down_weight[0]).astype(BF16)
        expert_out = lax.psum_scatter(terms, "ctx", scatter_dimension=0, tiled=True)
    hidden_two = hidden_one + my_weight[:, None] * expert_out.astype(F32)
    final_rows = rms_scale(hidden_two, final_gain).astype(BF16)
    teacher_logits = sum(
        matmul(rows, block, LAST)
        for rows, block in zip(split_relative(final_rows, plane, plane_count, 1), teacher_blocks)
    )
    teacher_logits = line_exchange(teacher_logits)

    teacher_peak = jnp.max(teacher_logits, axis=1, keepdims=True)
    teacher_lse = teacher_peak + jnp.log(
        jnp.sum(jnp.exp(teacher_logits - teacher_peak), axis=1, keepdims=True)
    )
    logit_gap = learner_logits - teacher_logits
    mean_gap = jnp.sum(learner_exp * logit_gap, axis=1, keepdims=True) / learner_total
    divergence = mean_gap - learner_lse + teacher_lse
    row_pos = ctx_index * pos_ctx + vocab_index * pos_dev + jnp.arange(pos_dev)
    live = row_pos[None, :] < lengths[:, None]
    live_sorted = jnp.any(placed & live.reshape(1, -1), axis=1)
    kl_rows = jnp.sum(jnp.where(placed, divergence, 0.0), axis=0).reshape(seq_dev, pos_dev)
    row_kl = jnp.where(live, kl_rows, 0.0)
    learner_prob = jnp.exp(learner_logits - learner_lse)
    dlogits = jnp.where(
        live_sorted[:, None], learner_prob * (logit_gap - mean_gap), 0.0
    ).astype(BF16)

    plane_dlogits = jnp.concatenate(plane_gather(dlogits), axis=0)
    head_part = matmul(plane_dlogits, plane_columns, FIRST).astype(BF16)
    head_grad = line_reduce(head_part).astype(BF16)

    restored = matmul(placer, dlogits, FIRST).astype(BF16)
    hidden_grad = join_absolute(
        [matmul(restored, block).astype(BF16) for block in learner_blocks], plane, 1
    ).reshape(seq_dev, pos_dev, width)
    return (hidden_grad, head_grad, row_kl)


def solution(mesh):
    placed = (
        P("rep", "ctx", "vocab"),
        P(None, "rep", "ctx", None),
        P("rep", ("ctx", "vocab"), None),
        P("vocab", ("ctx", "rep")),
        P(),
        P("rep", ("ctx", "vocab"), None),
        P("rep", ("ctx", "vocab"), None),
        P("vocab", "ctx", None),
        P("vocab", "ctx", None),
        P("vocab", "ctx", None),
        P(),
        P("vocab", None),
        P("rep", ("ctx", "vocab"), None),
        P("vocab", ("ctx", "rep")),
        P("rep"),
    )
    return jax.shard_map(
        per_device,
        mesh=mesh,
        in_specs=placed,
        out_specs=(
            P("rep", ("ctx", "vocab"), None),
            P("vocab", ("ctx", "rep")),
            P("rep", ("ctx", "vocab")),
        ),
        check_vma=False,
    )
```

```python
import jax
import jax.numpy as jnp
from jax import lax
from jax.experimental import pallas as pl
from jax.experimental.pallas import tpu as pltpu
from jax.sharding import PartitionSpec as P

QH = 64
KVH = 4
HD = 128

EPSILON = 1e-06
MASKED = -1e30
PLANE = ("ctx", "rep")
LAST = (((1,), (1,)), ((), ()))
FIRST = (((0,), (0,)), ((), ()))
F32 = jnp.float32
BF16 = jnp.bfloat16


def matmul(left, right, dims=(((1,), (0,)), ((), ()))):
    return lax.dot_general(left, right, dims, preferred_element_type=F32)


def rms_scale(values, gain):
    mean_square = jnp.mean(values * values, axis=-1, keepdims=True)
    return values * lax.rsqrt(mean_square + EPSILON) * gain


def after(value, *earlier):
    return lax.optimization_barrier((value, *earlier))[0]


def plane_index():
    return lax.axis_index("ctx") * lax.axis_size("rep") + lax.axis_index("rep")


def is_square():
    return lax.axis_size("ctx") == 2 and lax.axis_size("rep") == 4


def plane_swap(value, offset):
    ranks = lax.axis_size("ctx") * lax.axis_size("rep")
    return lax.ppermute(value, PLANE, [(i, i ^ offset) for i in range(ranks)])


def relative(gathered, index):
    return [
        lax.dynamic_index_in_dim(gathered, index ^ r, 0, keepdims=False)
        for r in range(gathered.shape[0])
    ]


def plane_gather(own):
    if not is_square():
        return relative(lax.all_gather(own, PLANE, axis=0, tiled=False), plane_index())
    along_x = plane_swap(own, 4)
    along_y = plane_swap(own, 2)
    core = plane_swap(own, 1)
    corner = plane_swap(along_y, 4)
    return [
        own,
        core,
        along_y,
        plane_swap(along_y, 1),
        along_x,
        plane_swap(along_x, 1),
        corner,
        plane_swap(corner, 1),
    ]


def rep_gather(own):
    if not is_square():
        return relative(
            lax.all_gather(own, "rep", axis=0, tiled=False), lax.axis_index("rep")
        )
    along_y = plane_swap(own, 2)
    return [own, plane_swap(own, 1), along_y, plane_swap(along_y, 1)]


def plane_rows(own):
    if not is_square():
        return jnp.concatenate(plane_gather(own), axis=0)
    half = own.shape[0] // 2
    along_x = plane_swap(own, 4)
    along_y = plane_swap(own, 2)
    near = plane_swap(along_y[:half], 4)
    far = plane_swap(along_x[half:], 2)
    mine = jnp.concatenate([own, along_y, along_x, near, far], axis=0)
    return jnp.concatenate([mine, plane_swap(mine, 1)], axis=0)


def plane_exchange(rows, count):
    blocks = split_relative(rows, plane_index(), count, 1)
    if not is_square():
        return jnp.concatenate(
            [blocks[0]] + [plane_swap(blocks[r], r) for r in range(1, count)], axis=0
        )
    there = plane_swap(jnp.concatenate(blocks[4:], axis=1), 4)
    size = blocks[0].shape[1]
    here = jnp.concatenate([jnp.concatenate(blocks[:4], axis=1), there], axis=0)
    there = plane_swap(here[:, 2 * size :], 2)
    own = rows.shape[0]
    here = here[:, : 2 * size]
    here = jnp.concatenate([here[:own], there[:own], here[own:], there[own:]], axis=0)
    return jnp.concatenate([here[:, :size], plane_swap(here[:, size:], 1)], axis=0)


def pick(value, index, size, axis):
    return lax.dynamic_slice_in_dim(value, index * size, size, axis)


def split_relative(value, index, count, axis):
    size = value.shape[axis] // count
    return [pick(value, index ^ r, size, axis) for r in range(count)]


def join_absolute(blocks, index, axis):
    while len(blocks) > 4:
        bit = index % 2 == 1
        index = index // 2
        blocks = [
            jnp.concatenate([jnp.where(bit, b, a), jnp.where(bit, a, b)], axis=axis)
            for a, b in zip(blocks[::2], blocks[1::2])
        ]
    count = len(blocks)
    return jnp.concatenate(
        [
            lax.select_n(index, *[blocks[j ^ i] for i in range(count)])
            for j in range(count)
        ],
        axis=axis,
    )


def line_swap(value, offset):
    count = lax.axis_size("vocab")
    return lax.ppermute(value, "vocab", [(i, i ^ offset) for i in range(count)])


def line_exchange(value):
    count = lax.axis_size("vocab")
    index = lax.axis_index("vocab")
    blocks = split_relative(value, index, count, 0)
    received = [blocks[0]] + [line_swap(blocks[r], r) for r in range(1, count)]
    return join_absolute(received, index, 0)


def line_gather(own):
    if lax.axis_size("vocab") != 4:
        return lax.all_gather(own, "vocab", axis=0, tiled=False)
    index = lax.axis_index("vocab")
    odd = index % 2 == 1
    beside = line_swap(own, 1)
    near = jnp.stack([jnp.where(odd, beside, own), jnp.where(odd, own, beside)])
    middle = lax.ppermute(near, "vocab", [(1, 2), (2, 1)])
    passed = lax.ppermute(middle, "vocab", [(1, 0), (2, 3)])
    far = jnp.where((index == 1) | (index == 2), middle, passed)
    high = index >= 2
    return jnp.concatenate([jnp.where(high, far, near), jnp.where(high, near, far)], axis=0)


def line_reduce(partial):
    if lax.axis_size("vocab") != 4:
        return lax.psum_scatter(
            partial, "vocab", scatter_dimension=0, tiled=True
        ).astype(F32)
    index = lax.axis_index("vocab")
    size = partial.shape[0] // 4
    far = pick(partial, 1 - index // 2, 2 * size, 0)
    near = pick(partial, index // 2, 2 * size, 0)
    outer = lax.ppermute(far, "vocab", [(0, 1), (3, 2)])
    far = (far.astype(F32) + outer.astype(F32)).astype(BF16)
    inner = lax.ppermute(far, "vocab", [(1, 2), (2, 1)])
    near = near.astype(F32) + inner.astype(F32)
    beside = line_swap(pick(near, 1 - index % 2, size, 0).astype(BF16), 1)
    return pick(near, index % 2, size, 0) + beside.astype(F32)


def line_sum(partial):
    if lax.axis_size("vocab") != 4:
        return line_reduce(partial)
    index = lax.axis_index("vocab")
    blocks = split_relative(partial, index, 4, 0)
    received = [line_swap(blocks[r], r) for r in (3, 2, 1)]
    return sum((block.astype(F32) for block in received), blocks[0].astype(F32))


HEADS_STEP = 4


def attend_kernel(facts, query, rows, out):
    pos_ctx = query.shape[1]
    keys = rows.shape[2]
    length = facts[pl.program_id(0)]
    query_pos = facts[pl.num_programs(0)] + lax.broadcasted_iota(jnp.int32, (pos_ctx, keys), 0)
    key_pos = facts[pl.num_programs(0) + 1] + lax.broadcasted_iota(jnp.int32, (pos_ctx, keys), 1)
    allowed = (key_pos <= query_pos) & (key_pos < length) & (key_pos >= 0)
    bias = jnp.where(allowed, 0.0, MASKED)
    for head in range(query.shape[2] // HD):
        cols = slice(head * HD, (head + 1) * HD)
        scores = matmul(query[0, :, cols], rows[0, 0], LAST) * HD ** (-0.5) + bias
        peak = jnp.max(scores, axis=-1, keepdims=True)
        exponent = jnp.exp(scores - peak)
        total = jnp.sum(exponent, axis=-1, keepdims=True)
        weighted = matmul(exponent.astype(BF16), rows[1, 0])
        out[:, cols] = (weighted / total).astype(BF16)


def attend(queries, key_value, lengths):
    seq_dev, pos_ctx, head_cols = queries.shape
    heads_dev = head_cols // HD
    ctx_index = lax.axis_index("ctx")
    shared_head = lax.axis_index("vocab") * heads_dev // (QH // KVH)
    own_rows = lax.dynamic_slice_in_dim(key_value, shared_head * HD, HD, 3)
    if lax.axis_size("ctx") == 2:
        other = lax.ppermute(own_rows, "ctx", [(0, 1), (1, 0)])
        rows = jnp.concatenate([other, own_rows], axis=2)
        first_key = (ctx_index - 1) * pos_ctx
    else:
        rows = lax.all_gather(own_rows, "ctx", axis=2, tiled=True)
        first_key = 0 * ctx_index
    facts = jnp.concatenate([lengths, jnp.stack([ctx_index * pos_ctx, first_key])])
    step_cols = HEADS_STEP * HD
    return pl.pallas_call(
        attend_kernel,
        out_shape=jax.ShapeDtypeStruct((seq_dev * pos_ctx, head_cols), BF16),
        grid_spec=pltpu.PrefetchScalarGridSpec(
            num_scalar_prefetch=1,
            grid=(seq_dev, head_cols // step_cols),
            in_specs=[
                pl.BlockSpec((1, pos_ctx, step_cols), lambda s, h, facts: (s, 0, h)),
                pl.BlockSpec((2, 1, rows.shape[2], HD), lambda s, h, facts: (0, s, 0, 0)),
            ],
            out_specs=pl.BlockSpec((pos_ctx, step_cols), lambda s, h, facts: (s, h)),
        ),
        cost_estimate=pl.CostEstimate(
            flops=4 * seq_dev * pos_ctx * rows.shape[2] * head_cols,
            bytes_accessed=4 * queries.size,
            transcendentals=seq_dev * heads_dev * pos_ctx * rows.shape[2],
        ),
        compiler_params=pltpu.CompilerParams(vmem_limit_bytes=32 * 2**20),
        name="attend",
    )(facts, queries, rows)


def per_device(
    queries,
    key_value,
    residual,
    out_weight,
    moe_gain,
    expert_ids,
    route_gate,
    gate_weight,
    up_weight,
    down_weight,
    final_gain,
    teacher_head,
    learner_hidden,
    learner_head,
    lengths,
):
    seq_dev, pos_ctx, _ = queries.shape
    pos_dev, width = residual.shape[1:]
    own_count = seq_dev * pos_dev
    vocab_count = lax.axis_size("vocab")
    plane_count = lax.axis_size("ctx") * lax.axis_size("rep")
    ctx_index = lax.axis_index("ctx")
    vocab_index = lax.axis_index("vocab")
    plane = plane_index()
    per_expert = own_count // vocab_count

    route_ids = expert_ids.reshape(own_count, -1)
    inside = route_ids < vocab_count
    chosen = jnp.sum(jnp.where(inside, route_ids, 0), axis=1)
    route_weight = jnp.sum(jnp.where(inside, route_gate.reshape(own_count, -1), 0.0), axis=1)
    member = (chosen[:, None] == jnp.arange(vocab_count)[None, :]).astype(jnp.int32)
    slot_rank = jnp.sum((jnp.cumsum(member, axis=0) - 1) * member, axis=1)
    target = chosen * per_expert + slot_rank
    placed = target[None, :] == jnp.arange(own_count)[:, None]
    placer = placed.astype(BF16)

    line_target = chosen * own_count + vocab_index * per_expert + slot_rank
    line_facts = lax.all_gather(jnp.stack([line_target.astype(F32), route_weight]), "vocab")
    line_target = line_facts[:, 0].astype(jnp.int32)
    line_weight = line_facts[:, 1]
    line_tokens = (
        jnp.swapaxes(line_target.reshape(vocab_count, seq_dev, pos_dev), 0, 1).reshape(-1)
    )
    line_placer = (line_tokens[None, :] == jnp.arange(seq_dev * pos_ctx)[:, None]).astype(BF16)
    mine = vocab_index * own_count + jnp.arange(own_count)
    my_weight = jnp.sum(
        jnp.where(line_target.reshape(1, -1) == mine[:, None], line_weight.reshape(1, -1), 0.0),
        axis=1,
    )

    heads_out = attend(queries, key_value, lengths)
    weight_blocks = plane_gather(out_weight)
    residual_rows = line_exchange(
        matmul(placer, residual.reshape(own_count, width)).astype(BF16)
    )
    heads_sorted = matmul(line_placer, heads_out).astype(BF16)

    rep_count = lax.axis_size("rep")
    rep_index = lax.axis_index("rep")
    vocab = vocab_count * teacher_head.shape[0]
    teacher_line = line_gather(pick(teacher_head, rep_index, width // rep_count, 1))
    learner_line = line_gather(learner_head)

    attn_blocks = [None] * plane_count
    order = ([0, 1], [4, 5], [2, 3], [6, 7]) if is_square() else ([r] for r in range(plane_count))
    for members in order:
        part = jnp.concatenate(
            [matmul(heads_sorted, weight_blocks[r]).astype(BF16) for r in members], axis=1
        )
        for r, piece in zip(members, jnp.split(line_reduce(part), len(members), axis=1)):
            attn_blocks[r] = piece
    attn_rows = join_absolute(attn_blocks, plane, 1)

    teacher_line = after(teacher_line.reshape(vocab, -1), weight_blocks[2])
    teacher_blocks = rep_gather(teacher_line)
    learner_line = after(learner_line.reshape(vocab, -1), weight_blocks[6], teacher_blocks[2])
    learner_blocks = plane_gather(learner_line)

    learner_rows = matmul(placer, learner_hidden.reshape(own_count, width)).astype(BF16)
    plane_columns = plane_exchange(learner_rows, plane_count)
    learner_logits = sum(
        matmul(rows, block, LAST)
        for rows, block in zip(split_relative(learner_rows, plane, plane_count, 1), learner_blocks)
    )
    learner_peak = jnp.max(learner_logits, axis=1, keepdims=True)
    learner_exp = jnp.exp(learner_logits - learner_peak)
    learner_total = jnp.sum(learner_exp, axis=1, keepdims=True)
    learner_lse = learner_peak + jnp.log(learner_total)

    hidden_one = residual_rows.astype(F32) + attn_rows
    normed = rms_scale(hidden_one, moe_gain).astype(BF16)
    pair = lax.axis_size("ctx") == 2
    if pair:
        other = lax.ppermute(normed, "ctx", [(0, 1), (1, 0)])
        rows = jnp.concatenate([normed, other], axis=0)
    else:
        rows = lax.all_gather(normed, "ctx", axis=0, tiled=True)
    gate_pre = matmul(rows, gate_weight[0], LAST)
    up_pre = matmul(rows, up_weight[0], LAST)
    activated = (jax.nn.silu(gate_pre) * up_pre).astype(BF16)
    if pair:
        theirs = matmul(activated[own_count:], down_weight[0]).astype(BF16)
        theirs = lax.ppermute(theirs, "ctx", [(0, 1), (1, 0)])
        ours = matmul(activated[:own_count], down_weight[0]).astype(BF16)
        expert_out = (ours.astype(F32) + theirs.astype(F32)).astype(BF16)
    else:
        terms = matmul(activated, down_weight[0]).astype(BF16)
        expert_out = lax.psum_scatter(terms, "ctx", scatter_dimension=0, tiled=True)
    hidden_two = hidden_one + my_weight[:, None] * expert_out.astype(F32)
    final_rows = rms_scale(hidden_two, final_gain).astype(BF16)
    teacher_logits = sum(
        matmul(rows, block, LAST)
        for rows, block in zip(split_relative(final_rows, rep_index, rep_count, 1), teacher_blocks)
    )
    teacher_logits = line_exchange(teacher_logits)

    teacher_peak = jnp.max(teacher_logits, axis=1, keepdims=True)
    teacher_lse = teacher_peak + jnp.log(
        jnp.sum(jnp.exp(teacher_logits - teacher_peak), axis=1, keepdims=True)
    )
    logit_gap = learner_logits - teacher_logits
    mean_gap = jnp.sum(learner_exp * logit_gap, axis=1, keepdims=True) / learner_total
    divergence = mean_gap - learner_lse + teacher_lse
    row_pos = ctx_index * pos_ctx + vocab_index * pos_dev + jnp.arange(pos_dev)
    live = row_pos[None, :] < lengths[:, None]
    live_sorted = jnp.any(placed & live.reshape(1, -1), axis=1)
    kl_rows = jnp.sum(jnp.where(placed, divergence, 0.0), axis=0).reshape(seq_dev, pos_dev)
    row_kl = jnp.where(live, kl_rows, 0.0)
    learner_prob = jnp.exp(learner_logits - learner_lse)
    dlogits = jnp.where(
        live_sorted[:, None], learner_prob * (logit_gap - mean_gap), 0.0
    ).astype(BF16)

    head_part = matmul(plane_rows(dlogits), plane_columns, FIRST).astype(BF16)
    head_grad = line_sum(head_part).astype(BF16)

    restored = matmul(placer, dlogits, FIRST).astype(BF16)
    hidden_grad = join_absolute(
        [matmul(restored, block).astype(BF16) for block in learner_blocks], plane, 1
    ).reshape(seq_dev, pos_dev, width)
    return (hidden_grad, head_grad, row_kl)


def solution(mesh):
    placed = (
        P("rep", "ctx", "vocab"),
        P(None, "rep", "ctx", None),
        P("rep", ("ctx", "vocab"), None),
        P("vocab", ("ctx", "rep")),
        P(),
        P("rep", ("ctx", "vocab"), None),
        P("rep", ("ctx", "vocab"), None),
        P("vocab", "ctx", None),
        P("vocab", "ctx", None),
        P("vocab", "ctx", None),
        P(),
        P("vocab", None),
        P("rep", ("ctx", "vocab"), None),
        P("vocab", ("ctx", "rep")),
        P("rep"),
    )
    return jax.shard_map(
        per_device,
        mesh=mesh,
        in_specs=placed,
        out_specs=(
            P("rep", ("ctx", "vocab"), None),
            P("vocab", ("ctx", "rep")),
            P("rep", ("ctx", "vocab")),
        ),
        check_vma=False,
    )
```

```python
import jax
import jax.numpy as jnp
from jax import lax
from jax.experimental import pallas as pl
from jax.experimental.pallas import tpu as pltpu
from jax.sharding import PartitionSpec as P

QH = 64
KVH = 4
HD = 128

EPSILON = 1e-06
MASKED = -1e30
PLANE = ("ctx", "rep")
LAST = (((1,), (1,)), ((), ()))
FIRST = (((0,), (0,)), ((), ()))
F32 = jnp.float32
BF16 = jnp.bfloat16


def matmul(left, right, dims=(((1,), (0,)), ((), ()))):
    return lax.dot_general(left, right, dims, preferred_element_type=F32)


def rms_scale(values, gain):
    mean_square = jnp.mean(values * values, axis=-1, keepdims=True)
    return values * lax.rsqrt(mean_square + EPSILON) * gain


def after(value, *earlier):
    return lax.optimization_barrier((value, *earlier))[0]


def swap_x(value):
    return lax.ppermute(value, "ctx", [(0, 1), (1, 0)])


def swap_rep(value, offset):
    return lax.ppermute(value, "rep", [(i, i ^ offset) for i in range(4)])


def swap_z(value, offset):
    return lax.ppermute(value, "vocab", [(i, i ^ offset) for i in range(4)])


def pick(value, index, size, axis):
    return lax.dynamic_slice_in_dim(value, index * size, size, axis)


def split_relative(value, index, count, axis):
    size = value.shape[axis] // count
    return [pick(value, index ^ r, size, axis) for r in range(count)]


def join_absolute(blocks, index, axis):
    count = len(blocks)
    return jnp.concatenate(
        [
            lax.select_n(index, *[blocks[j ^ i] for i in range(count)])
            for j in range(count)
        ],
        axis=axis,
    )


def rep_gather(own):
    along_y = swap_rep(own, 2)
    return [own, swap_rep(own, 1), along_y, swap_rep(along_y, 1)]


def line_gather(own):
    received = [own] + [swap_z(own, r) for r in (1, 2, 3)]
    return join_absolute(received, lax.axis_index("vocab"), 0)


def line_exchange(value):
    index = lax.axis_index("vocab")
    blocks = split_relative(value, index, 4, 0)
    received = [blocks[0]] + [swap_z(blocks[r], r) for r in (1, 2, 3)]
    return join_absolute(received, index, 0)


def line_sum(partial):
    blocks = split_relative(partial, lax.axis_index("vocab"), 4, 0)
    received = [swap_z(blocks[r], r) for r in (3, 2, 1)]
    return sum((block.astype(F32) for block in received), blocks[0].astype(F32))


def line_reduce(far, near):
    index = lax.axis_index("vocab")
    size = near.shape[0] // 2
    outer = lax.ppermute(far, "vocab", [(0, 1), (3, 2)])
    far = (far.astype(F32) + outer.astype(F32)).astype(BF16)
    inner = lax.ppermute(far, "vocab", [(1, 2), (2, 1)])
    near = near.astype(F32) + inner.astype(F32)
    beside = swap_z(pick(near, 1 - index % 2, size, 0).astype(BF16), 1)
    return pick(near, index % 2, size, 0) + beside.astype(F32)


def plane_rows(own):
    half = own.shape[0] // 2
    along_x = swap_x(own)
    along_y = swap_rep(own, 2)
    near = swap_x(along_y[:half])
    far = swap_rep(along_x[half:], 2)
    mine = jnp.concatenate([own, along_y, along_x, near, far], axis=0)
    return jnp.concatenate([mine, swap_rep(mine, 1)], axis=0), along_x


def plane_exchange(rows):
    plane = lax.axis_index("ctx") * 4 + lax.axis_index("rep")
    blocks = split_relative(rows, plane, 8, 1)
    count, size = blocks[0].shape
    there = swap_x(jnp.concatenate(blocks[4:], axis=1))
    here = jnp.concatenate([jnp.concatenate(blocks[:4], axis=1), there], axis=0)
    there = swap_rep(here[:, 2 * size :], 2)
    here = here[:, : 2 * size]
    here = jnp.concatenate([here[:count], there[:count], here[count:], there[count:]], axis=0)
    return jnp.concatenate([here[:, :size], swap_rep(here[:, size:], 1)], axis=0)


HEADS_STEP = 4


def attend_kernel(facts, query, rows, out):
    pos_ctx = query.shape[1]
    keys = rows.shape[2]
    length = facts[pl.program_id(0)]
    query_pos = facts[pl.num_programs(0)] + lax.broadcasted_iota(jnp.int32, (pos_ctx, keys), 0)
    key_pos = facts[pl.num_programs(0) + 1] + lax.broadcasted_iota(jnp.int32, (pos_ctx, keys), 1)
    allowed = (key_pos <= query_pos) & (key_pos < length) & (key_pos >= 0)
    bias = jnp.where(allowed, 0.0, MASKED)
    for head in range(query.shape[2] // HD):
        cols = slice(head * HD, (head + 1) * HD)
        scores = matmul(query[0, :, cols], rows[0, 0], LAST) * HD ** (-0.5) + bias
        peak = jnp.max(scores, axis=-1, keepdims=True)
        exponent = jnp.exp(scores - peak)
        total = jnp.sum(exponent, axis=-1, keepdims=True)
        weighted = matmul(exponent.astype(BF16), rows[1, 0])
        out[:, cols] = (weighted / total).astype(BF16)


def attend(queries, key_value, lengths):
    seq_dev, pos_ctx, head_cols = queries.shape
    heads_dev = head_cols // HD
    ctx_index = lax.axis_index("ctx")
    shared_head = lax.axis_index("vocab") * heads_dev // (QH // KVH)
    own_rows = lax.dynamic_slice_in_dim(key_value, shared_head * HD, HD, 3)
    other = swap_x(own_rows)
    rows = jnp.concatenate([other, own_rows], axis=2)
    facts = jnp.concatenate([lengths, jnp.stack([ctx_index * pos_ctx, (ctx_index - 1) * pos_ctx])])
    step_cols = HEADS_STEP * HD
    heads_out = pl.pallas_call(
        attend_kernel,
        out_shape=jax.ShapeDtypeStruct((seq_dev * pos_ctx, head_cols), BF16),
        grid_spec=pltpu.PrefetchScalarGridSpec(
            num_scalar_prefetch=1,
            grid=(seq_dev, head_cols // step_cols),
            in_specs=[
                pl.BlockSpec((1, pos_ctx, step_cols), lambda s, h, facts: (s, 0, h)),
                pl.BlockSpec((2, 1, rows.shape[2], HD), lambda s, h, facts: (0, s, 0, 0)),
            ],
            out_specs=pl.BlockSpec((pos_ctx, step_cols), lambda s, h, facts: (s, h)),
        ),
        cost_estimate=pl.CostEstimate(
            flops=4 * seq_dev * pos_ctx * rows.shape[2] * head_cols,
            bytes_accessed=4 * queries.size,
            transcendentals=seq_dev * heads_dev * pos_ctx * rows.shape[2],
        ),
        compiler_params=pltpu.CompilerParams(vmem_limit_bytes=32 * 2**20),
        name="attend",
    )(facts, queries, rows)
    return heads_out, other


def per_device(
    queries,
    key_value,
    residual,
    out_weight,
    moe_gain,
    expert_ids,
    route_gate,
    gate_weight,
    up_weight,
    down_weight,
    final_gain,
    teacher_head,
    learner_hidden,
    learner_head,
    lengths,
):
    seq_dev, pos_ctx, _ = queries.shape
    pos_dev, width = residual.shape[1:]
    own_count = seq_dev * pos_dev
    half = width // 2
    ctx_index = lax.axis_index("ctx")
    vocab_index = lax.axis_index("vocab")
    rep_index = lax.axis_index("rep")
    per_expert = own_count // 4
    vocab = 4 * teacher_head.shape[0]

    route_ids = expert_ids.reshape(own_count, -1)
    inside = route_ids < 4
    chosen = jnp.sum(jnp.where(inside, route_ids, 0), axis=1)
    route_weight = jnp.sum(jnp.where(inside, route_gate.reshape(own_count, -1), 0.0), axis=1)
    member = (chosen[:, None] == jnp.arange(4)[None, :]).astype(jnp.int32)
    slot_rank = jnp.sum((jnp.cumsum(member, axis=0) - 1) * member, axis=1)
    target = chosen * per_expert + slot_rank
    placed = target[None, :] == jnp.arange(own_count)[:, None]
    placer = placed.astype(BF16)

    line_target = chosen * own_count + vocab_index * per_expert + slot_rank
    pair_facts = jnp.stack([line_target.astype(F32), route_weight])[None]
    beside = swap_z(pair_facts, 1)
    pair_facts = join_absolute([pair_facts, beside], vocab_index % 2, 0)
    line_facts = join_absolute([pair_facts, swap_z(pair_facts, 2)], vocab_index // 2, 0)
    line_target = line_facts[:, 0].astype(jnp.int32)
    line_weight = line_facts[:, 1]
    line_tokens = jnp.swapaxes(line_target.reshape(4, seq_dev, pos_dev), 0, 1).reshape(-1)
    line_placer = (line_tokens[None, :] == jnp.arange(seq_dev * pos_ctx)[:, None]).astype(BF16)
    mine = vocab_index * own_count + jnp.arange(own_count)
    my_weight = jnp.sum(
        jnp.where(line_target.reshape(1, -1) == mine[:, None], line_weight.reshape(1, -1), 0.0),
        axis=1,
        keepdims=True,
    )

    heads_out, keys = attend(queries, key_value, lengths)
    weight_blocks = rep_gather(out_weight)
    residual_rows = matmul(placer, residual.reshape(own_count, width)).astype(BF16)
    other_residual = swap_x(after(pick(residual_rows, 1 - ctx_index, half, 1), keys))
    both_residual = (pick(residual_rows, ctx_index, half, 1), other_residual)
    other_weight = swap_x(my_weight)

    learner_line = line_gather(learner_head)
    learner_line = after(learner_line, weight_blocks[2])
    learner_blocks = rep_gather(learner_line)

    heads_sorted = matmul(line_placer, heads_out).astype(BF16)
    far_pair, near_pair = 1 - vocab_index // 2, vocab_index // 2
    pair_rows = 2 * own_count
    own_far = pick(heads_sorted, far_pair, pair_rows, 0)
    own_near = pick(heads_sorted, near_pair, pair_rows, 0)
    other_far = swap_x(own_far)
    other_near = swap_x(after(own_near, other_far))
    owner = (jnp.arange(4) == vocab_index).reshape(1, 4, 1, 1)

    def project(rows, weight, residual_part, pair, block):
        added = pick(residual_part, pair, 2 * per_expert, 0)
        added = pick(added, rep_index ^ block, weight.shape[1], 1).astype(F32)
        added = jnp.where(owner, added.reshape(2, 1, per_expert, -1), 0.0)
        added = added.reshape(pair_rows, -1)
        return (matmul(rows, weight) + added).astype(BF16)

    def projected(far, near, residual_part, members):
        parts = [
            jnp.concatenate(
                [project(rows, weight_blocks[r], residual_part, pair, r) for r in members], axis=1
            )
            for rows, pair in ((far, far_pair), (near, near_pair))
        ]
        return jnp.split(line_reduce(*parts), 2, axis=1)

    own_blocks = projected(own_far, own_near, both_residual[0], (0, 1))
    own_blocks += projected(own_far, own_near, both_residual[0], (2, 3))
    other_blocks = projected(other_far, other_near, both_residual[1], (0, 1))
    other_blocks += projected(other_far, other_near, both_residual[1], (2, 3))

    hidden_one = jnp.concatenate(
        [join_absolute(own_blocks, rep_index, 1), join_absolute(other_blocks, rep_index, 1)], axis=0
    )
    sent = hidden_one.astype(BF16)
    got = swap_x(sent)
    got = jnp.concatenate([got[own_count:], got[:own_count]], axis=0)
    rows = join_absolute([sent, got], ctx_index, 1).astype(F32)
    normed = rms_scale(rows, moe_gain).astype(BF16)

    learner_own = learner_hidden.reshape(own_count, width)
    learner_rows = matmul(placer, learner_own).astype(BF16)
    other_rows = swap_x(after(pick(learner_rows, 1 - ctx_index, half, 1), other_near))
    both_rows = jnp.concatenate([pick(learner_rows, ctx_index, half, 1), other_rows], axis=0)
    learner_part = sum(
        matmul(part, block, LAST)
        for part, block in zip(split_relative(both_rows, rep_index, 4, 1), learner_blocks)
    )
    learner_logits = learner_part[:own_count] + swap_x(learner_part[own_count:])
    learner_peak = jnp.max(learner_logits, axis=1, keepdims=True)
    learner_exp = jnp.exp(learner_logits - learner_peak)
    learner_total = jnp.sum(learner_exp, axis=1, keepdims=True)
    learner_lse = learner_peak + jnp.log(learner_total)
    plane_columns = plane_exchange(after(learner_own, learner_logits))

    teacher_slice = pick(teacher_head, ctx_index * 4 + rep_index, width // 8, 1)
    teacher_line = line_gather(after(teacher_slice, other_blocks[0], other_blocks[2]))
    teacher_blocks = rep_gather(teacher_line)

    gate_pre = matmul(normed, gate_weight[0], LAST)
    up_pre = matmul(normed, up_weight[0], LAST)
    activated = (jax.nn.silu(gate_pre) * up_pre).astype(BF16)
    theirs = matmul(activated, pick(down_weight[0], 1 - ctx_index, half, 1)).astype(BF16)
    theirs = swap_x(theirs)
    theirs = jnp.concatenate([theirs[own_count:], theirs[:own_count]], axis=0)
    ours = matmul(activated, pick(down_weight[0], ctx_index, half, 1)).astype(BF16)
    expert_out = (ours.astype(F32) + theirs.astype(F32)).astype(BF16).astype(F32)
    both_weight = jnp.concatenate([my_weight, other_weight], axis=0)
    hidden_two = hidden_one + both_weight * expert_out

    squares = jnp.sum(hidden_two * hidden_two, axis=1, keepdims=True)
    own_squares = squares[:own_count] + swap_x(squares[own_count:])
    scale = lax.rsqrt(own_squares / width + EPSILON)
    final_rows = (hidden_two * pick(final_gain, ctx_index, half, 0)).astype(BF16)
    teacher_part = sum(
        matmul(part, block, LAST)
        for part, block in zip(split_relative(final_rows, rep_index, 4, 1), teacher_blocks)
    )
    teacher_logits = (teacher_part[:own_count] + swap_x(teacher_part[own_count:])) * scale
    teacher_logits = line_exchange(teacher_logits)

    teacher_peak = jnp.max(teacher_logits, axis=1, keepdims=True)
    teacher_lse = teacher_peak + jnp.log(
        jnp.sum(jnp.exp(teacher_logits - teacher_peak), axis=1, keepdims=True)
    )
    logit_gap = learner_logits - teacher_logits
    mean_gap = jnp.sum(learner_exp * logit_gap, axis=1, keepdims=True) / learner_total
    divergence = mean_gap - learner_lse + teacher_lse
    row_pos = ctx_index * pos_ctx + vocab_index * pos_dev + jnp.arange(pos_dev)
    live = row_pos[None, :] < lengths[:, None]
    live_sorted = jnp.any(placed & live.reshape(1, -1), axis=1)
    kl_rows = jnp.sum(jnp.where(placed, divergence, 0.0), axis=0).reshape(seq_dev, pos_dev)
    row_kl = jnp.where(live, kl_rows, 0.0)
    learner_prob = jnp.exp(learner_logits - learner_lse)
    dlogits = jnp.where(
        live_sorted[:, None], learner_prob * (logit_gap - mean_gap), 0.0
    ).astype(BF16)
    dlogits = matmul(placer, dlogits, FIRST).astype(BF16)

    plane_dlogits, other_dlogits = plane_rows(dlogits)
    head_part = matmul(plane_dlogits, plane_columns, FIRST).astype(BF16)
    head_grad = line_sum(head_part).astype(BF16)

    other_grad = swap_x(
        join_absolute(
            [matmul(other_dlogits, block).astype(BF16) for block in learner_blocks], rep_index, 1
        )
    )
    own_grad = join_absolute(
        [matmul(dlogits, block).astype(BF16) for block in learner_blocks], rep_index, 1
    )
    hidden_grad = join_absolute([own_grad, other_grad], ctx_index, 1)
    return (hidden_grad.reshape(seq_dev, pos_dev, width), head_grad, row_kl)


def per_device_general(
    queries,
    key_value,
    residual,
    out_weight,
    moe_gain,
    expert_ids,
    route_gate,
    gate_weight,
    up_weight,
    down_weight,
    final_gain,
    teacher_head,
    learner_hidden,
    learner_head,
    lengths,
):
    seq_dev, pos_ctx, head_cols = queries.shape
    pos_dev = residual.shape[1]
    width = residual.shape[2]
    vocab_count = lax.axis_size("vocab")
    ctx_index = lax.axis_index("ctx")
    vocab_index = lax.axis_index("vocab")
    heads_dev = head_cols // HD
    shared_head = vocab_index * heads_dev // (QH // KVH)
    key_rows = lax.dynamic_slice_in_dim(key_value, shared_head * HD, HD, 3)
    query_heads = queries.reshape(seq_dev, pos_ctx, heads_dev, HD)
    query_pos = ctx_index * pos_ctx + jnp.arange(pos_ctx)
    score_scale = HD ** (-0.5)
    shard_rows = lax.all_gather(key_rows, "ctx", axis=2, tiled=True)
    running_max = jnp.full((seq_dev, pos_ctx, heads_dev), MASKED, jnp.float32)
    key_pos = jnp.arange(shard_rows.shape[2])
    scores = (
        jnp.einsum("sqhd,skd->sqhk", query_heads, shard_rows[0], preferred_element_type=jnp.float32)
        * score_scale
    )
    allowed = (key_pos[None, None, :] <= query_pos[None, :, None]) & (
        key_pos[None, None, :] < lengths[:, None, None]
    )
    allowed = allowed[:, :, None, :]
    scores = jnp.where(allowed, scores, MASKED)
    new_max = jnp.maximum(running_max, jnp.max(scores, axis=-1))
    exponent = jnp.where(allowed, jnp.exp(scores - new_max[..., None]), 0.0)
    running_sum = jnp.sum(exponent, axis=-1)
    weighted = jnp.einsum(
        "sqhk,skd->sqhd",
        exponent.astype(jnp.bfloat16),
        shard_rows[1],
        preferred_element_type=jnp.float32,
    )
    final_max, final_sum, weighted = (new_max, running_sum, weighted)
    heads_out = (
        (weighted / final_sum[..., None]).astype(jnp.bfloat16).reshape(seq_dev * pos_ctx, head_cols)
    )
    mixed = jnp.dot(
        heads_out,
        lax.all_gather(out_weight, ("ctx", "rep"), axis=1, tiled=True),
        preferred_element_type=jnp.float32,
    )
    attn_rows = lax.psum_scatter(
        mixed.reshape(seq_dev, pos_ctx, width).astype(jnp.bfloat16),
        "vocab",
        scatter_dimension=1,
        tiled=True,
    ).astype(jnp.float32)
    hidden_one = residual.astype(jnp.float32) + attn_rows
    own_count = seq_dev * pos_dev
    normed = rms_scale(hidden_one, moe_gain).astype(jnp.bfloat16).reshape(own_count, width)
    route_ids = expert_ids.reshape(own_count, -1)
    inside = route_ids < vocab_count
    chosen = jnp.sum(jnp.where(inside, route_ids, 0), axis=1)
    route_weight = jnp.sum(jnp.where(inside, route_gate.reshape(own_count, -1), 0.0), axis=1)
    per_expert = own_count // vocab_count
    member = (chosen[:, None] == jnp.arange(vocab_count)[None, :]).astype(jnp.int32)
    slot_rank = jnp.sum((jnp.cumsum(member, axis=0) - 1) * member, axis=1)
    target = chosen * per_expert + slot_rank
    placer = (target[None, :] == jnp.arange(own_count)[:, None]).astype(jnp.bfloat16)
    outgoing = jnp.dot(placer, normed, preferred_element_type=jnp.float32).astype(jnp.bfloat16)
    arrived = lax.all_to_all(
        outgoing.reshape(vocab_count, per_expert, width),
        "vocab",
        split_axis=0,
        concat_axis=0,
        tiled=True,
    )
    arrived = arrived.reshape(own_count, width)
    gate_slice = gate_weight[0]
    up_slice = up_weight[0]
    down_slice = down_weight[0]
    contract_last = (((1,), (1,)), ((), ()))
    shard_rows = lax.all_gather(arrived, "ctx", axis=0, tiled=True)
    gate_pre = lax.dot_general(
        shard_rows, gate_slice, contract_last, preferred_element_type=jnp.float32
    )
    up_pre = lax.dot_general(
        shard_rows, up_slice, contract_last, preferred_element_type=jnp.float32
    )
    activated = (jax.nn.silu(gate_pre) * up_pre).astype(jnp.bfloat16)
    expert_terms = jnp.dot(activated, down_slice, preferred_element_type=jnp.float32)
    expert_out = lax.psum_scatter(
        expert_terms.astype(jnp.bfloat16), "ctx", scatter_dimension=0, tiled=True
    )
    returned_rows = lax.all_to_all(
        expert_out.reshape(vocab_count, per_expert, width),
        "vocab",
        split_axis=0,
        concat_axis=0,
        tiled=True,
    )
    restored = lax.dot_general(
        placer,
        returned_rows.reshape(own_count, width),
        (((0,), (0,)), ((), ())),
        preferred_element_type=jnp.float32,
    )
    hidden_two = hidden_one.reshape(own_count, width) + route_weight[:, None] * restored
    final_rows = (
        rms_scale(hidden_two, final_gain).astype(jnp.bfloat16).reshape(seq_dev, pos_dev, width)
    )
    teacher_rows, learner_rows = (
        lax.all_gather(final_rows, "vocab", axis=1, tiled=True),
        lax.all_gather(learner_hidden, "vocab", axis=1, tiled=True),
    )
    learner_full = lax.all_gather(learner_head, ("ctx", "rep"), axis=1, tiled=True)
    teacher_flat = teacher_rows.reshape(-1, width)
    learner_flat = learner_rows.reshape(-1, width)
    teacher_logits = lax.dot_general(
        teacher_flat, teacher_head, contract_last, preferred_element_type=jnp.float32
    )
    learner_logits = lax.dot_general(
        learner_flat, learner_full, contract_last, preferred_element_type=jnp.float32
    )
    logit_gap = learner_logits - teacher_logits
    learner_peak = jnp.max(learner_logits, axis=1)
    teacher_peak = jnp.max(teacher_logits, axis=1)
    learner_peak, teacher_peak = lax.pmax((learner_peak, teacher_peak), "vocab")
    learner_exp = jnp.exp(learner_logits - learner_peak[:, None])
    learner_total, cross_total, teacher_total = lax.psum(
        (
            jnp.sum(learner_exp, axis=1),
            jnp.sum(learner_exp * logit_gap, axis=1),
            jnp.sum(jnp.exp(teacher_logits - teacher_peak[:, None]), axis=1),
        ),
        "vocab",
    )
    learner_lse = learner_peak + jnp.log(learner_total)
    teacher_lse = teacher_peak + jnp.log(teacher_total)
    mean_gap = cross_total / learner_total
    divergence = mean_gap - learner_lse + teacher_lse
    row_pos = ctx_index * pos_ctx + jnp.arange(pos_ctx)
    live_rows = (row_pos[None, :] < lengths[:, None]).reshape(-1)
    learner_prob = jnp.exp(learner_logits - learner_lse[:, None])
    dlogits = jnp.where(
        live_rows[:, None], learner_prob * (logit_gap - mean_gap[:, None]), 0.0
    ).astype(jnp.bfloat16)
    kl_block = jnp.where(live_rows, divergence, 0.0).reshape(seq_dev, pos_ctx)
    row_kl = lax.dynamic_slice_in_dim(kl_block, vocab_index * pos_dev, pos_dev, 1)
    by_position = jnp.swapaxes(dlogits.reshape(seq_dev, pos_ctx, -1), 0, 1)
    shard_rows = by_position
    grad_rows = lax.psum_scatter(
        jnp.einsum(
            "psv,vd->psd", shard_rows, learner_full, preferred_element_type=jnp.float32
        ).astype(jnp.bfloat16),
        "vocab",
        scatter_dimension=0,
        tiled=True,
    ).astype(jnp.float32)
    hidden_grad = jnp.swapaxes(grad_rows, 0, 1).astype(jnp.bfloat16)
    head_sum = lax.psum_scatter(
        lax.dot_general(
            learner_flat, dlogits, (((0,), (0,)), ((), ())), preferred_element_type=jnp.float32
        ).astype(jnp.bfloat16),
        ("ctx", "rep"),
        scatter_dimension=0,
        tiled=True,
    ).astype(jnp.float32)
    head_grad = jnp.transpose(head_sum).astype(jnp.bfloat16)
    return (hidden_grad, head_grad, row_kl)


def solution(mesh):
    placed = (
        P("rep", "ctx", "vocab"),
        P(None, "rep", "ctx", None),
        P("rep", ("ctx", "vocab"), None),
        P("vocab", ("ctx", "rep")),
        P(),
        P("rep", ("ctx", "vocab"), None),
        P("rep", ("ctx", "vocab"), None),
        P("vocab", "ctx", None),
        P("vocab", "ctx", None),
        P("vocab", "ctx", None),
        P(),
        P("vocab", None),
        P("rep", ("ctx", "vocab"), None),
        P("vocab", ("ctx", "rep")),
        P("rep"),
    )
    shape = dict(mesh.shape)
    swaps = (shape["ctx"], shape["vocab"], shape["rep"]) == (2, 4, 4)
    return jax.shard_map(
        per_device if swaps else per_device_general,
        mesh=mesh,
        in_specs=placed,
        out_specs=(
            P("rep", ("ctx", "vocab"), None),
            P("vocab", ("ctx", "rep")),
            P("rep", ("ctx", "vocab")),
        ),
        check_vma=False,
    )
```

```python
import jax
import jax.numpy as jnp
from jax import lax
from jax.experimental import pallas as pl
from jax.experimental.pallas import tpu as pltpu
from jax.sharding import PartitionSpec as P

QH = 64
KVH = 4
HD = 128

EPSILON = 1e-06
MASKED = -1e30
PLANE = ("ctx", "rep")
LAST = (((1,), (1,)), ((), ()))
FIRST = (((0,), (0,)), ((), ()))
F32 = jnp.float32
BF16 = jnp.bfloat16


def matmul(left, right, dims=(((1,), (0,)), ((), ()))):
    return lax.dot_general(left, right, dims, preferred_element_type=F32)


def rms_scale(values, gain):
    mean_square = jnp.mean(values * values, axis=-1, keepdims=True)
    return values * lax.rsqrt(mean_square + EPSILON) * gain


def after(value, *earlier):
    return lax.optimization_barrier((value, *earlier))[0]


def swap_x(value):
    return lax.ppermute(value, "ctx", [(0, 1), (1, 0)])


def swap_rep(value, offset):
    return lax.ppermute(value, "rep", [(i, i ^ offset) for i in range(4)])


def swap_z(value, offset):
    return lax.ppermute(value, "vocab", [(i, i ^ offset) for i in range(4)])


def pick(value, index, size, axis):
    return lax.dynamic_slice_in_dim(value, index * size, size, axis)


def split_relative(value, index, count, axis):
    size = value.shape[axis] // count
    return [pick(value, index ^ r, size, axis) for r in range(count)]


def join_absolute(blocks, index, axis):
    count = len(blocks)
    return jnp.concatenate(
        [
            lax.select_n(index, *[blocks[j ^ i] for i in range(count)])
            for j in range(count)
        ],
        axis=axis,
    )


def rep_gather(own, gate=lambda value: value):
    along_y = swap_rep(own, 2)
    return [own, swap_rep(own, 1), along_y, swap_rep(gate(along_y), 1)]


def line_gather(own, gate=lambda value: value):
    received = [own] + [gate(swap_z(own, r)) for r in (1, 2, 3)]
    return join_absolute(received, lax.axis_index("vocab"), 0)


def line_exchange(value):
    index = lax.axis_index("vocab")
    blocks = split_relative(value, index, 4, 0)
    received = [blocks[0]] + [swap_z(blocks[r], r) for r in (1, 2, 3)]
    return join_absolute(received, index, 0)


def line_sum(partial):
    index = lax.axis_index("vocab")
    size = partial.shape[0] // 4
    half = partial.shape[1] // 2
    blocks = split_relative(partial, index, 4, 0)
    kept = []
    for first in (0, half):
        mine, beside, far, farther = (block[:, first : first + half] for block in blocks)
        got = swap_z(jnp.concatenate([beside, farther], axis=0), 1).astype(F32)
        kept.append((mine.astype(F32) + got[:size], far.astype(F32) + got[size:]))
    return jnp.concatenate(
        [mine + swap_z(far.astype(BF16), 2).astype(F32) for mine, far in kept], axis=1
    )


def plane_rows(own):
    half = own.shape[0] // 2
    along_x = swap_x(own)
    along_y = swap_rep(own, 2)
    near = swap_x(along_y[:half])
    far = swap_rep(along_x[half:], 2)
    mine = jnp.concatenate([own, along_y, along_x, near, far], axis=0)
    return jnp.concatenate([mine, swap_rep(mine, 1)], axis=0), along_x


def plane_exchange(rows, gate_y, gate_core):
    plane = lax.axis_index("ctx") * 4 + lax.axis_index("rep")
    blocks = split_relative(rows, plane, 8, 1)
    count, size = blocks[0].shape
    there = swap_x(jnp.concatenate(blocks[4:], axis=1))
    here = jnp.concatenate([jnp.concatenate(blocks[:4], axis=1), there], axis=0)
    here = gate_y(here)
    there = swap_rep(here[:, 2 * size :], 2)
    here = here[:, : 2 * size]
    here = jnp.concatenate([here[:count], there[:count], here[count:], there[count:]], axis=0)
    return jnp.concatenate([here[:, :size], swap_rep(gate_core(here[:, size:]), 1)], axis=0)


HEADS_STEP = 4


def attend_kernel(facts, query, rows, out):
    pos_ctx = query.shape[1]
    keys = rows.shape[2]
    length = facts[pl.program_id(0)]
    query_pos = facts[pl.num_programs(0)] + lax.broadcasted_iota(jnp.int32, (pos_ctx, keys), 0)
    key_pos = facts[pl.num_programs(0) + 1] + lax.broadcasted_iota(jnp.int32, (pos_ctx, keys), 1)
    allowed = (key_pos <= query_pos) & (key_pos < length) & (key_pos >= 0)
    bias = jnp.where(allowed, 0.0, MASKED)
    for head in range(query.shape[2] // HD):
        cols = slice(head * HD, (head + 1) * HD)
        scores = matmul(query[0, :, cols], rows[0, 0], LAST) * HD ** (-0.5) + bias
        peak = jnp.max(scores, axis=-1, keepdims=True)
        exponent = jnp.exp(scores - peak)
        total = jnp.sum(exponent, axis=-1, keepdims=True)
        weighted = matmul(exponent.astype(BF16), rows[1, 0])
        out[:, cols] = (weighted / total).astype(BF16)


def attend(queries, key_value, lengths, earlier):
    seq_dev, pos_ctx, head_cols = queries.shape
    heads_dev = head_cols // HD
    ctx_index = lax.axis_index("ctx")
    shared_head = lax.axis_index("vocab") * heads_dev // (QH // KVH)
    own_rows = lax.dynamic_slice_in_dim(key_value, shared_head * HD, HD, 3)
    other = after(swap_x(own_rows), earlier)
    rows = jnp.concatenate([other, own_rows], axis=2)
    facts = jnp.concatenate([lengths, jnp.stack([ctx_index * pos_ctx, (ctx_index - 1) * pos_ctx])])
    step_cols = HEADS_STEP * HD
    heads_out = pl.pallas_call(
        attend_kernel,
        out_shape=jax.ShapeDtypeStruct((seq_dev * pos_ctx, head_cols), BF16),
        grid_spec=pltpu.PrefetchScalarGridSpec(
            num_scalar_prefetch=1,
            grid=(seq_dev, head_cols // step_cols),
            in_specs=[
                pl.BlockSpec((1, pos_ctx, step_cols), lambda s, h, facts: (s, 0, h)),
                pl.BlockSpec((2, 1, rows.shape[2], HD), lambda s, h, facts: (0, s, 0, 0)),
            ],
            out_specs=pl.BlockSpec((pos_ctx, step_cols), lambda s, h, facts: (s, h)),
        ),
        cost_estimate=pl.CostEstimate(flops=0, bytes_accessed=0, transcendentals=0),
        compiler_params=pltpu.CompilerParams(vmem_limit_bytes=32 * 2**20),
        name="attend",
    )(facts, queries, rows)
    return heads_out, other


def per_device(
    queries,
    key_value,
    residual,
    out_weight,
    moe_gain,
    expert_ids,
    route_gate,
    gate_weight,
    up_weight,
    down_weight,
    final_gain,
    teacher_head,
    learner_hidden,
    learner_head,
    lengths,
):
    seq_dev, pos_ctx, _ = queries.shape
    pos_dev, width = residual.shape[1:]
    own_count = seq_dev * pos_dev
    half = width // 2
    ctx_index = lax.axis_index("ctx")
    vocab_index = lax.axis_index("vocab")
    rep_index = lax.axis_index("rep")
    per_expert = own_count // 4
    vocab = 4 * teacher_head.shape[0]

    def column_blocks(value, ctx):
        size = value.shape[-1] // 8
        return [pick(value, ctx * 4 + (rep_index ^ r), size, value.ndim - 1) for r in range(4)]

    residual_rows = residual.reshape(own_count, width)
    other_residual = jnp.concatenate(column_blocks(residual_rows, 1 - ctx_index), axis=1)
    other_residual = swap_x(other_residual)
    heads_out, keys = attend(queries, key_value, lengths, other_residual)
    expert_ids = after(expert_ids, keys)

    route_ids = expert_ids.reshape(own_count, -1)
    inside = route_ids < 4
    chosen = jnp.sum(jnp.where(inside, route_ids, 0), axis=1)
    route_weight = jnp.sum(jnp.where(inside, route_gate.reshape(own_count, -1), 0.0), axis=1)
    member = (chosen[:, None] == jnp.arange(4)[None, :]).astype(jnp.int32)
    slot_rank = jnp.sum((jnp.cumsum(member, axis=0) - 1) * member, axis=1)
    target = chosen * per_expert + slot_rank
    placed = target[None, :] == jnp.arange(own_count)[:, None]
    placer = placed.astype(BF16)

    line_target = chosen * own_count + vocab_index * per_expert + slot_rank
    own_facts = jnp.stack([line_target.astype(F32), route_weight])[None]
    line_facts = line_gather(own_facts)

    weight_y = swap_rep(out_weight, 2)
    weight_blocks = [out_weight, swap_rep(out_weight, 1), weight_y]
    other_facts = swap_x(line_facts)
    line_facts = after(line_facts, heads_out)
    mine = vocab_index * own_count + jnp.arange(own_count)[:, None]

    def routed(facts):
        targets = facts[:, 0].astype(jnp.int32).reshape(1, -1)
        weights = jnp.where(targets == mine, facts[:, 1].reshape(1, -1), 0.0)
        return targets, jnp.sum(weights, axis=1, keepdims=True)

    line_target_all, my_weight = routed(line_facts)
    other_target_all, other_weight = routed(other_facts)
    other_target = pick(other_target_all, vocab_index, own_count, 1)

    line_rows = jnp.arange(seq_dev * pos_ctx)
    chunk = line_rows // own_count
    chunk = jnp.where(chunk < 2, 2 * chunk + 1, 2 * chunk - 4) ^ vocab_index
    line_rows = (chunk * own_count + line_rows % own_count)[:, None]
    line_tokens = jnp.swapaxes(line_target_all.reshape(4, seq_dev, pos_dev), 0, 1).reshape(1, -1)
    line_placer = (line_rows == line_tokens).astype(BF16)
    heads_sorted = matmul(line_placer, heads_out).astype(BF16)
    sent_count = 2 * own_count
    other_sent = swap_x(heads_sorted[:sent_count])

    own_residual = jnp.concatenate(column_blocks(after(residual_rows, heads_out), ctx_index), axis=1)
    own_added = matmul((line_rows == line_target[None, :]).astype(BF16), own_residual).astype(BF16)
    other_added = matmul(
        (line_rows == other_target).astype(BF16), other_residual
    ).astype(BF16)

    def projected(rows, added, members):
        size = added.shape[1] // 4
        return jnp.concatenate(
            [
                (
                    matmul(rows, weight_blocks[r])
                    + added[:, r * size : (r + 1) * size].astype(F32)
                ).astype(BF16)
                for r in members
            ],
            axis=1,
        )

    def beside_sum(kept, beside):
        return kept.astype(F32) + beside.astype(F32)

    def across_sum(kept, across):
        return kept[:own_count] + across.astype(F32)

    part_0 = projected(heads_sorted, own_added, (0, 1))
    beside_0 = swap_z(part_0[:sent_count], 1)
    weight_blocks.append(swap_rep(after(weight_y, part_0), 1))
    part_1 = projected(heads_sorted, own_added, (2, 3))
    beside_1 = swap_z(part_1[:sent_count], 1)
    other_kept = swap_x(after(heads_sorted[sent_count:], other_sent, part_1))
    kept_0 = beside_sum(part_0[sent_count:], after(beside_0, part_1))
    across_0 = swap_z(kept_0[own_count:].astype(BF16), 2)
    sent_2 = projected(after(other_sent, part_1), other_added[:sent_count], (0, 1, 2, 3))
    beside_2 = swap_z(sent_2, 1)
    kept_1 = beside_sum(part_1[sent_count:], after(beside_1, sent_2))
    across_1 = swap_z(kept_1[own_count:].astype(BF16), 2)
    other_kept = after(other_kept, kept_0, kept_1)
    kept_2 = projected(other_kept, other_added[sent_count:], (0, 1, 2, 3))
    hidden_0 = across_sum(kept_0, after(across_0, kept_2))
    hidden_1 = across_sum(kept_1, after(across_1, kept_2))
    kept_2 = beside_sum(kept_2, beside_2)
    across_2 = swap_z(kept_2[own_count:].astype(BF16), 2)
    hidden_2 = across_sum(kept_2, across_2)
    hidden_parts = [hidden_0, hidden_1, hidden_2]
    sent = [part.astype(BF16) for part in hidden_parts]
    got = [swap_x(part) for part in sent]

    plane_columns = plane_exchange(
        after(learner_hidden.reshape(own_count, width), part_1),
        lambda value: after(value, sent_2),
        lambda value: after(value, hidden_2),
    )
    teacher_slice = pick(teacher_head, ctx_index * 4 + rep_index, width // 8, 1)
    teacher_line = line_gather(teacher_slice, lambda value: after(value, part_1))
    teacher_line = after(teacher_line, weight_y)
    teacher_blocks = rep_gather(teacher_line, lambda value: after(value, hidden_2))
    learner_line = line_gather(after(learner_head, hidden_2))

    hidden_one = jnp.concatenate([jnp.concatenate(hidden_parts[:2], axis=1), hidden_2], axis=0)
    theirs = jnp.concatenate([got[2], jnp.concatenate(got[:2], axis=1)], axis=0)
    squares = jnp.sum(hidden_one * hidden_one, axis=1, keepdims=True) + jnp.sum(
        jnp.square(theirs.astype(F32)), axis=1, keepdims=True
    )
    scale = lax.rsqrt(squares / width + EPSILON)
    sides = [
        join_absolute(jnp.split(side, 4, axis=1), rep_index, 1)
        for side in (hidden_one.astype(BF16), theirs)
    ]
    rows = join_absolute(sides, ctx_index, 1)
    normed = (rows.astype(F32) * scale * moe_gain).astype(BF16)

    learner_own = after(learner_hidden, sent_2).reshape(own_count, width)
    learner_rows = matmul(placer, learner_own).astype(BF16)
    other_rows = jnp.concatenate(column_blocks(learner_rows, 1 - ctx_index), axis=1)
    other_rows = swap_x(after(other_rows, other_kept))
    own_rows = jnp.concatenate(column_blocks(learner_rows, ctx_index), axis=1)
    both_rows = jnp.concatenate([own_rows, other_rows], axis=0)
    gate_pre = matmul(normed, gate_weight[0], LAST)
    up_pre = matmul(normed, up_weight[0], LAST)
    activated = (jax.nn.silu(gate_pre) * up_pre).astype(BF16)
    down_other = column_blocks(after(down_weight, sent_2)[0], 1 - ctx_index)
    down_own = column_blocks(after(down_weight, sent_2)[0], ctx_index)
    expert_parts = []
    for r in (0, 2):
        terms = matmul(activated, jnp.concatenate(down_other[r : r + 2], axis=1)).astype(BF16)
        terms = swap_x(terms)
        terms = jnp.concatenate([terms[own_count:], terms[:own_count]], axis=0)
        ours = matmul(activated, jnp.concatenate(down_own[r : r + 2], axis=1)).astype(BF16)
        expert_parts.append((ours.astype(F32) + terms.astype(F32)).astype(BF16).astype(F32))
    expert_out = jnp.concatenate(expert_parts, axis=1)
    both_weight = jnp.concatenate([my_weight, other_weight], axis=0)
    hidden_two = hidden_one + both_weight * expert_out

    squares = jnp.sum(hidden_two * hidden_two, axis=1, keepdims=True)
    own_squares = squares[:own_count] + swap_x(squares[own_count:])
    scale = lax.rsqrt(own_squares / width + EPSILON)
    gain = jnp.concatenate(column_blocks(final_gain, ctx_index))
    final_rows = (hidden_two * gain).astype(BF16)
    final_blocks = jnp.split(final_rows, 4, axis=1)
    teacher_sides = [
        sum(
            matmul(rows, block[first : first + vocab // 2], LAST)
            for rows, block in zip(final_blocks, teacher_blocks)
        )
        for first in (0, vocab // 2)
    ]
    teacher_parts = [
        (side[:own_count] + swap_x(side[own_count:])) * scale for side in teacher_sides
    ]
    teacher_logits = jnp.concatenate([line_exchange(part) for part in teacher_parts], axis=1)
    learner_blocks = rep_gather(learner_line, lambda value: after(value, *teacher_sides))
    learner_part = sum(
        matmul(part, block, LAST)
        for part, block in zip(jnp.split(both_rows, 4, axis=1), learner_blocks)
    )
    learner_logits = learner_part[:own_count] + swap_x(after(learner_part[own_count:], *teacher_parts))
    learner_peak = jnp.max(learner_logits, axis=1, keepdims=True)
    learner_exp = jnp.exp(learner_logits - learner_peak)
    learner_total = jnp.sum(learner_exp, axis=1, keepdims=True)
    learner_lse = learner_peak + jnp.log(learner_total)

    teacher_peak = jnp.max(teacher_logits, axis=1, keepdims=True)
    teacher_lse = teacher_peak + jnp.log(
        jnp.sum(jnp.exp(teacher_logits - teacher_peak), axis=1, keepdims=True)
    )
    logit_gap = learner_logits - teacher_logits
    mean_gap = jnp.sum(learner_exp * logit_gap, axis=1, keepdims=True) / learner_total
    divergence = mean_gap - learner_lse + teacher_lse
    row_pos = ctx_index * pos_ctx + vocab_index * pos_dev + jnp.arange(pos_dev)
    live = row_pos[None, :] < lengths[:, None]
    live_sorted = jnp.any(placed & live.reshape(1, -1), axis=1)
    kl_rows = jnp.sum(jnp.where(placed, divergence, 0.0), axis=0).reshape(seq_dev, pos_dev)
    row_kl = jnp.where(live, kl_rows, 0.0)
    learner_prob = jnp.exp(learner_logits - learner_lse)
    dlogits = jnp.where(
        live_sorted[:, None], learner_prob * (logit_gap - mean_gap), 0.0
    ).astype(BF16)
    dlogits = matmul(placer, dlogits, FIRST).astype(BF16)

    plane_dlogits, other_dlogits = plane_rows(dlogits)
    head_part = matmul(plane_dlogits, plane_columns, FIRST).astype(BF16)
    head_grad = line_sum(head_part).astype(BF16)

    other_grad = swap_x(
        join_absolute(
            [matmul(other_dlogits, block).astype(BF16) for block in learner_blocks], rep_index, 1
        )
    )
    own_grad = join_absolute(
        [matmul(dlogits, block).astype(BF16) for block in learner_blocks], rep_index, 1
    )
    hidden_grad = join_absolute([own_grad, after(other_grad, head_grad)], ctx_index, 1)
    return (hidden_grad.reshape(seq_dev, pos_dev, width), head_grad, row_kl)


def per_device_general(
    queries,
    key_value,
    residual,
    out_weight,
    moe_gain,
    expert_ids,
    route_gate,
    gate_weight,
    up_weight,
    down_weight,
    final_gain,
    teacher_head,
    learner_hidden,
    learner_head,
    lengths,
):
    seq_dev, pos_ctx, head_cols = queries.shape
    pos_dev = residual.shape[1]
    width = residual.shape[2]
    vocab_count = lax.axis_size("vocab")
    ctx_index = lax.axis_index("ctx")
    vocab_index = lax.axis_index("vocab")
    heads_dev = head_cols // HD
    shared_head = vocab_index * heads_dev // (QH // KVH)
    key_rows = lax.dynamic_slice_in_dim(key_value, shared_head * HD, HD, 3)
    query_heads = queries.reshape(seq_dev, pos_ctx, heads_dev, HD)
    query_pos = ctx_index * pos_ctx + jnp.arange(pos_ctx)
    score_scale = HD ** (-0.5)
    shard_rows = lax.all_gather(key_rows, "ctx", axis=2, tiled=True)
    running_max = jnp.full((seq_dev, pos_ctx, heads_dev), MASKED, jnp.float32)
    key_pos = jnp.arange(shard_rows.shape[2])
    scores = (
        jnp.einsum("sqhd,skd->sqhk", query_heads, shard_rows[0], preferred_element_type=jnp.float32)
        * score_scale
    )
    allowed = (key_pos[None, None, :] <= query_pos[None, :, None]) & (
        key_pos[None, None, :] < lengths[:, None, None]
    )
    allowed = allowed[:, :, None, :]
    scores = jnp.where(allowed, scores, MASKED)
    new_max = jnp.maximum(running_max, jnp.max(scores, axis=-1))
    exponent = jnp.where(allowed, jnp.exp(scores - new_max[..., None]), 0.0)
    running_sum = jnp.sum(exponent, axis=-1)
    weighted = jnp.einsum(
        "sqhk,skd->sqhd",
        exponent.astype(jnp.bfloat16),
        shard_rows[1],
        preferred_element_type=jnp.float32,
    )
    final_max, final_sum, weighted = (new_max, running_sum, weighted)
    heads_out = (
        (weighted / final_sum[..., None]).astype(jnp.bfloat16).reshape(seq_dev * pos_ctx, head_cols)
    )
    mixed = jnp.dot(
        heads_out,
        lax.all_gather(out_weight, ("ctx", "rep"), axis=1, tiled=True),
        preferred_element_type=jnp.float32,
    )
    attn_rows = lax.psum_scatter(
        mixed.reshape(seq_dev, pos_ctx, width).astype(jnp.bfloat16),
        "vocab",
        scatter_dimension=1,
        tiled=True,
    ).astype(jnp.float32)
    hidden_one = residual.astype(jnp.float32) + attn_rows
    own_count = seq_dev * pos_dev
    normed = rms_scale(hidden_one, moe_gain).astype(jnp.bfloat16).reshape(own_count, width)
    route_ids = expert_ids.reshape(own_count, -1)
    inside = route_ids < vocab_count
    chosen = jnp.sum(jnp.where(inside, route_ids, 0), axis=1)
    route_weight = jnp.sum(jnp.where(inside, route_gate.reshape(own_count, -1), 0.0), axis=1)
    per_expert = own_count // vocab_count
    member = (chosen[:, None] == jnp.arange(vocab_count)[None, :]).astype(jnp.int32)
    slot_rank = jnp.sum((jnp.cumsum(member, axis=0) - 1) * member, axis=1)
    target = chosen * per_expert + slot_rank
    placer = (target[None, :] == jnp.arange(own_count)[:, None]).astype(jnp.bfloat16)
    outgoing = jnp.dot(placer, normed, preferred_element_type=jnp.float32).astype(jnp.bfloat16)
    arrived = lax.all_to_all(
        outgoing.reshape(vocab_count, per_expert, width),
        "vocab",
        split_axis=0,
        concat_axis=0,
        tiled=True,
    )
    arrived = arrived.reshape(own_count, width)
    gate_slice = gate_weight[0]
    up_slice = up_weight[0]
    down_slice = down_weight[0]
    contract_last = (((1,), (1,)), ((), ()))
    shard_rows = lax.all_gather(arrived, "ctx", axis=0, tiled=True)
    gate_pre = lax.dot_general(
        shard_rows, gate_slice, contract_last, preferred_element_type=jnp.float32
    )
    up_pre = lax.dot_general(
        shard_rows, up_slice, contract_last, preferred_element_type=jnp.float32
    )
    activated = (jax.nn.silu(gate_pre) * up_pre).astype(jnp.bfloat16)
    expert_terms = jnp.dot(activated, down_slice, preferred_element_type=jnp.float32)
    expert_out = lax.psum_scatter(
        expert_terms.astype(jnp.bfloat16), "ctx", scatter_dimension=0, tiled=True
    )
    returned_rows = lax.all_to_all(
        expert_out.reshape(vocab_count, per_expert, width),
        "vocab",
        split_axis=0,
        concat_axis=0,
        tiled=True,
    )
    restored = lax.dot_general(
        placer,
        returned_rows.reshape(own_count, width),
        (((0,), (0,)), ((), ())),
        preferred_element_type=jnp.float32,
    )
    hidden_two = hidden_one.reshape(own_count, width) + route_weight[:, None] * restored
    final_rows = (
        rms_scale(hidden_two, final_gain).astype(jnp.bfloat16).reshape(seq_dev, pos_dev, width)
    )
    teacher_rows, learner_rows = (
        lax.all_gather(final_rows, "vocab", axis=1, tiled=True),
        lax.all_gather(learner_hidden, "vocab", axis=1, tiled=True),
    )
    learner_full = lax.all_gather(learner_head, ("ctx", "rep"), axis=1, tiled=True)
    teacher_flat = teacher_rows.reshape(-1, width)
    learner_flat = learner_rows.reshape(-1, width)
    teacher_logits = lax.dot_general(
        teacher_flat, teacher_head, contract_last, preferred_element_type=jnp.float32
    )
    learner_logits = lax.dot_general(
        learner_flat, learner_full, contract_last, preferred_element_type=jnp.float32
    )
    logit_gap = learner_logits - teacher_logits
    learner_peak = jnp.max(learner_logits, axis=1)
    teacher_peak = jnp.max(teacher_logits, axis=1)
    learner_peak, teacher_peak = lax.pmax((learner_peak, teacher_peak), "vocab")
    learner_exp = jnp.exp(learner_logits - learner_peak[:, None])
    learner_total, cross_total, teacher_total = lax.psum(
        (
            jnp.sum(learner_exp, axis=1),
            jnp.sum(learner_exp * logit_gap, axis=1),
            jnp.sum(jnp.exp(teacher_logits - teacher_peak[:, None]), axis=1),
        ),
        "vocab",
    )
    learner_lse = learner_peak + jnp.log(learner_total)
    teacher_lse = teacher_peak + jnp.log(teacher_total)
    mean_gap = cross_total / learner_total
    divergence = mean_gap - learner_lse + teacher_lse
    row_pos = ctx_index * pos_ctx + jnp.arange(pos_ctx)
    live_rows = (row_pos[None, :] < lengths[:, None]).reshape(-1)
    learner_prob = jnp.exp(learner_logits - learner_lse[:, None])
    dlogits = jnp.where(
        live_rows[:, None], learner_prob * (logit_gap - mean_gap[:, None]), 0.0
    ).astype(jnp.bfloat16)
    kl_block = jnp.where(live_rows, divergence, 0.0).reshape(seq_dev, pos_ctx)
    row_kl = lax.dynamic_slice_in_dim(kl_block, vocab_index * pos_dev, pos_dev, 1)
    by_position = jnp.swapaxes(dlogits.reshape(seq_dev, pos_ctx, -1), 0, 1)
    shard_rows = by_position
    grad_rows = lax.psum_scatter(
        jnp.einsum(
            "psv,vd->psd", shard_rows, learner_full, preferred_element_type=jnp.float32
        ).astype(jnp.bfloat16),
        "vocab",
        scatter_dimension=0,
        tiled=True,
    ).astype(jnp.float32)
    hidden_grad = jnp.swapaxes(grad_rows, 0, 1).astype(jnp.bfloat16)
    head_sum = lax.psum_scatter(
        lax.dot_general(
            learner_flat, dlogits, (((0,), (0,)), ((), ())), preferred_element_type=jnp.float32
        ).astype(jnp.bfloat16),
        ("ctx", "rep"),
        scatter_dimension=0,
        tiled=True,
    ).astype(jnp.float32)
    head_grad = jnp.transpose(head_sum).astype(jnp.bfloat16)
    return (hidden_grad, head_grad, row_kl)


def solution(mesh):
    placed = (
        P("rep", "ctx", "vocab"),
        P(None, "rep", "ctx", None),
        P("rep", ("ctx", "vocab"), None),
        P("vocab", ("ctx", "rep")),
        P(),
        P("rep", ("ctx", "vocab"), None),
        P("rep", ("ctx", "vocab"), None),
        P("vocab", "ctx", None),
        P("vocab", "ctx", None),
        P("vocab", "ctx", None),
        P(),
        P("vocab", None),
        P("rep", ("ctx", "vocab"), None),
        P("vocab", ("ctx", "rep")),
        P("rep"),
    )
    shape = dict(mesh.shape)
    swaps = (shape["ctx"], shape["vocab"], shape["rep"]) == (2, 4, 4)
    return jax.shard_map(
        per_device if swaps else per_device_general,
        mesh=mesh,
        in_specs=placed,
        out_specs=(
            P("rep", ("ctx", "vocab"), None),
            P("vocab", ("ctx", "rep")),
            P("rep", ("ctx", "vocab")),
        ),
        check_vma=False,
    )
```

```python
import functools

import jax
import jax.numpy as jnp
from jax import lax
from jax.experimental import pallas as pl
from jax.experimental.pallas import tpu as pltpu
from jax.sharding import PartitionSpec as P

QH = 64
KVH = 4
HD = 128

EPSILON = 1e-06
MASKED = -1e30
PLANE = ("ctx", "rep")
LAST = (((1,), (1,)), ((), ()))
FIRST = (((0,), (0,)), ((), ()))
F32 = jnp.float32
BF16 = jnp.bfloat16


def matmul(left, right, dims=(((1,), (0,)), ((), ()))):
    return lax.dot_general(left, right, dims, preferred_element_type=F32)


def rms_scale(values, gain):
    mean_square = jnp.mean(values * values, axis=-1, keepdims=True)
    return values * lax.rsqrt(mean_square + EPSILON) * gain


class Order:
    def __init__(self):
        self.last = None

    def take(self, *values):
        if self.last is None:
            return values if len(values) > 1 else values[0]
        values = lax.optimization_barrier((*values, self.last))[:-1]
        return values if len(values) > 1 else values[0]

    def ends(self, value):
        self.last = value
        return value

    def waits(self, *values):
        values = lax.optimization_barrier((*values, self.last))[:-1]
        self.last = values[0]
        return values if len(values) > 1 else values[0]


def swap_x(value):
    return lax.ppermute(value, "ctx", [(0, 1), (1, 0)])


def swap_rep(value, offset):
    return lax.ppermute(value, "rep", [(i, i ^ offset) for i in range(4)])


def swap_z(value, offset):
    return lax.ppermute(value, "vocab", [(i, i ^ offset) for i in range(4)])


def pick(value, index, size, axis):
    return lax.dynamic_slice_in_dim(value, index * size, size, axis)


def split_relative(value, index, count, axis):
    size = value.shape[axis] // count
    return [pick(value, index ^ r, size, axis) for r in range(count)]


def join_absolute(blocks, index, axis):
    count = len(blocks)
    return jnp.concatenate(
        [
            lax.select_n(index, *[blocks[j ^ i] for i in range(count)])
            for j in range(count)
        ],
        axis=axis,
    )


def line_gather(own):
    return [own] + [swap_z(own, r) for r in (1, 2, 3)]


def line_exchange(value):
    blocks = split_relative(value, lax.axis_index("vocab"), 4, 0)
    return [blocks[0]] + [swap_z(blocks[r], r) for r in (1, 2, 3)]


def line_joined(received):
    return join_absolute(received, lax.axis_index("vocab"), 0)


HEADS_STEP = 4


def attend_kernel(facts, query, rows, out):
    pos_ctx = query.shape[1]
    keys = rows.shape[2]
    length = facts[pl.program_id(0)]
    query_pos = facts[pl.num_programs(0)] + lax.broadcasted_iota(jnp.int32, (pos_ctx, keys), 0)
    key_pos = facts[pl.num_programs(0) + 1] + lax.broadcasted_iota(jnp.int32, (pos_ctx, keys), 1)
    allowed = (key_pos <= query_pos) & (key_pos < length) & (key_pos >= 0)
    bias = jnp.where(allowed, 0.0, MASKED)
    for head in range(query.shape[2] // HD):
        cols = slice(head * HD, (head + 1) * HD)
        scores = matmul(query[0, :, cols], rows[0, 0], LAST) * HD ** (-0.5) + bias
        peak = jnp.max(scores, axis=-1, keepdims=True)
        exponent = jnp.exp(scores - peak)
        total = jnp.sum(exponent, axis=-1, keepdims=True)
        weighted = matmul(exponent.astype(BF16), rows[1, 0])
        out[:, cols] = (weighted / total).astype(BF16)


def attend(queries, rows, lengths):
    seq_dev, pos_ctx, head_cols = queries.shape
    ctx_index = lax.axis_index("ctx")
    facts = jnp.concatenate([lengths, jnp.stack([ctx_index * pos_ctx, (ctx_index - 1) * pos_ctx])])
    step_cols = HEADS_STEP * HD
    return pl.pallas_call(
        attend_kernel,
        out_shape=jax.ShapeDtypeStruct((seq_dev * pos_ctx, head_cols), BF16),
        grid_spec=pltpu.PrefetchScalarGridSpec(
            num_scalar_prefetch=1,
            grid=(seq_dev, head_cols // step_cols),
            in_specs=[
                pl.BlockSpec(
                    (1, pos_ctx, step_cols), lambda s, h, facts: (s, 0, h)
                ),
                pl.BlockSpec((2, 1, rows.shape[2], HD), lambda s, h, facts: (0, s, 0, 0)),
            ],
            out_specs=pl.BlockSpec((pos_ctx, step_cols), lambda s, h, facts: (s, h)),
        ),
        cost_estimate=pl.CostEstimate(flops=0, bytes_accessed=0, transcendentals=0),
        compiler_params=pltpu.CompilerParams(vmem_limit_bytes=32 * 2**20),
        name="attend",
    )(facts, queries, rows)


FREE = pl.CostEstimate(flops=0, bytes_accessed=0, transcendentals=0)
VMEM_BYTES = 48 * 2**20


def whole(shape):
    return pl.BlockSpec(shape, lambda *_: (0,) * len(shape))


def project_kernel(count, parts, *refs):
    groups = len(parts)
    rows, placers, refs = refs[:groups], refs[groups : 2 * groups], refs[2 * groups :]
    residual, weights, outs = refs[0], refs[1 : 1 + count], list(refs[1 + count :])
    for row, placer, part in zip(rows, placers, parts):
        targets = [outs.pop(0) for _ in part]
        for r in range(count):
            total = matmul(row[...], weights[r][...]) + matmul(placer[...], residual[r])
            first = 0
            for target, size in zip(targets, part):
                target[r] = total[first : first + size].astype(BF16)
                first += size


def project(rows, placers, residual, weights, parts):
    count = len(weights)
    size = weights[0].shape[1]
    tile = size // 2
    cuts = [part for group in parts for part in group]
    return pl.pallas_call(
        functools.partial(project_kernel, count, parts),
        out_shape=[jax.ShapeDtypeStruct((count, part, size), BF16) for part in cuts],
        grid=(2,),
        in_specs=[whole(value.shape) for value in (*rows, *placers)]
        + [pl.BlockSpec((count, residual.shape[1], tile), lambda j: (0, 0, j))]
        + [pl.BlockSpec((weights[0].shape[0], tile), lambda j: (0, j))] * count,
        out_specs=[pl.BlockSpec((count, part, tile), lambda j: (0, 0, j)) for part in cuts],
        cost_estimate=FREE,
        compiler_params=pltpu.CompilerParams(vmem_limit_bytes=VMEM_BYTES),
        name="project",
    )(*rows, *placers, residual, *weights)


def sort_kernel(placer, heads, sent, kept):
    half = sent.shape[0]
    sent[...] = matmul(placer[:half], heads[...]).astype(BF16)
    kept[...] = matmul(placer[half:], heads[...]).astype(BF16)


def sorted_rows(placer, heads):
    rows, width = heads.shape
    tile = width // 4
    return pl.pallas_call(
        sort_kernel,
        out_shape=[jax.ShapeDtypeStruct((rows // 2, width), BF16)] * 2,
        grid=(4,),
        in_specs=[whole(placer.shape), pl.BlockSpec((rows, tile), lambda j: (0, j))],
        out_specs=[pl.BlockSpec((rows // 2, tile), lambda j: (0, j))] * 2,
        cost_estimate=FREE,
        compiler_params=pltpu.CompilerParams(vmem_limit_bytes=VMEM_BYTES),
        name="sorted_rows",
    )(placer, heads)


def logits_kernel(rows, *refs):
    blocks, (own, other) = refs[:-2], refs[-2:]
    count = own.shape[0]
    total = 0.0
    for r, block in enumerate(blocks):
        total += matmul(rows[r], block[...].reshape(own.shape[1], -1), LAST)
    own[...] = total[:count]
    other[...] = total[count:]


def logits_part(rows, heads, part):
    vocab_count, entries, size = heads[0].shape
    tile = vocab_count // 2 * entries
    count = rows.shape[1] // 2
    block = (vocab_count // 2, entries, size)
    return pl.pallas_call(
        logits_kernel,
        out_shape=[jax.ShapeDtypeStruct((count, tile), F32)] * 2,
        grid=(1,),
        in_specs=[whole(rows.shape)] + [pl.BlockSpec(block, lambda j: (part, 0, 0))] * len(heads),
        out_specs=[whole((count, tile))] * 2,
        cost_estimate=FREE,
        compiler_params=pltpu.CompilerParams(vmem_limit_bytes=VMEM_BYTES),
        name="logits",
    )(rows, *heads)


def learner_logits_kernel(facts, rows, *refs):
    logits_kernel(rows, *[ref.at[:, 0] for ref in refs[:4]], *refs[4:])


def learner_logits_part(facts, rows, heads, part):
    vocab_count, rep_count, entries, size = heads.shape
    tile = vocab_count // 2 * entries
    count = rows.shape[1] // 2
    block = (vocab_count // 2, 1, entries, size)
    return pl.pallas_call(
        learner_logits_kernel,
        out_shape=[jax.ShapeDtypeStruct((count, tile), F32)] * 2,
        grid_spec=pltpu.PrefetchScalarGridSpec(
            num_scalar_prefetch=1,
            grid=(1,),
            in_specs=[whole(rows.shape)]
            + [
                pl.BlockSpec(block, lambda j, facts, r=r: (part, facts[r], 0, 0))
                for r in range(rep_count)
            ],
            out_specs=[whole((count, tile))] * 2,
        ),
        cost_estimate=FREE,
        compiler_params=pltpu.CompilerParams(vmem_limit_bytes=VMEM_BYTES),
        name="logits",
    )(facts, rows, *[heads] * rep_count)


def join_kernel(facts, *refs):
    sources, out = refs[:-1], refs[-1]
    for r, source in enumerate(sources):

        @pl.when((facts[0] ^ pl.program_id(0)) == r)
        def _():
            out[0] = source[...]


def joined(index, blocks):
    count = len(blocks)
    shape = blocks[0].shape
    return pl.pallas_call(
        join_kernel,
        out_shape=jax.ShapeDtypeStruct((count, *shape), blocks[0].dtype),
        grid_spec=pltpu.PrefetchScalarGridSpec(
            num_scalar_prefetch=1,
            grid=(count,),
            in_specs=[whole(shape)] * count,
            out_specs=pl.BlockSpec((1, *shape), lambda j, facts: (j, 0, 0)),
        ),
        cost_estimate=FREE,
        compiler_params=pltpu.CompilerParams(vmem_limit_bytes=VMEM_BYTES),
        name="joined",
    )(index.reshape(1).astype(jnp.int32), *blocks)


def learner_kernel(facts, placer, other_placer, own, other, rows, near, far):
    r = pl.program_id(0)
    count = own.shape[0]
    rows[0, :count] = matmul(placer[...], own[...]).astype(BF16)
    rows[0, count:] = matmul(other_placer[...], other[...]).astype(BF16)
    for out, here in ((near, r < 2), (far, r >= 2)):

        @pl.when(here)
        def _():
            out[0, :count] = own[...]
            out[0, count:] = other[...]


def learner_parts(facts, placer, other_placer, own, other):
    count = own.shape[0]
    size = own.shape[1] // 8
    shape = (1, 2 * count, size)
    return pl.pallas_call(
        learner_kernel,
        out_shape=[
            jax.ShapeDtypeStruct((blocks, 2 * count, size), BF16) for blocks in (4, 2, 2)
        ],
        grid_spec=pltpu.PrefetchScalarGridSpec(
            num_scalar_prefetch=1,
            grid=(4,),
            in_specs=[
                whole(placer.shape),
                whole(placer.shape),
                pl.BlockSpec((count, size), lambda r, facts: (0, facts[r])),
                pl.BlockSpec((count, size), lambda r, facts: (0, r)),
            ],
            out_specs=[
                pl.BlockSpec(shape, lambda r, facts: (r, 0, 0)),
                pl.BlockSpec(shape, lambda r, facts: (jnp.minimum(r, 1), 0, 0)),
                pl.BlockSpec(shape, lambda r, facts: (jnp.maximum(r - 2, 0), 0, 0)),
            ],
        ),
        cost_estimate=FREE,
        compiler_params=pltpu.CompilerParams(vmem_limit_bytes=VMEM_BYTES),
        name="learner_parts",
    )(facts, placer, other_placer, own, other)


def head_kernel(facts, mine, core, here, along_y, other, *outs):
    i = pl.program_id(0)
    count = here.shape[1]
    total = matmul(mine[:count], here[0], FIRST) + matmul(mine[count:], along_y[0], FIRST)
    total += matmul(core[:count], other[0], FIRST) + matmul(core[count:], other[1], FIRST)
    total = total.astype(BF16)
    size = total.shape[1] // 2
    for group, now in ((outs[:2], i < 2), (outs[2:], i >= 2)):

        @pl.when(now)
        def _():
            for k, out in enumerate(group):
                out[0] = total[:, k * size : (k + 1) * size]


def head_parts(facts, mine, core, here, along_y, other):
    rows, vocab = mine.shape
    tile, size = vocab // 4, here.shape[2] // 2
    shape = (1, tile, size)
    first = pl.BlockSpec(shape, lambda i, facts: (jnp.minimum(i, 1), 0, 0))
    rest = pl.BlockSpec(shape, lambda i, facts: (jnp.maximum(i - 2, 0), 0, 0))
    return pl.pallas_call(
        head_kernel,
        out_shape=[jax.ShapeDtypeStruct((2, tile, size), BF16)] * 4,
        grid_spec=pltpu.PrefetchScalarGridSpec(
            num_scalar_prefetch=1,
            grid=(4,),
            in_specs=[pl.BlockSpec((rows, tile), lambda i, facts: (0, facts[i]))] * 2
            + [whole(value.shape) for value in (here, along_y, other)],
            out_specs=[first, first, rest, rest],
        ),
        cost_estimate=FREE,
        compiler_params=pltpu.CompilerParams(vmem_limit_bytes=VMEM_BYTES),
        name="head_parts",
    )(facts, mine, core, here, along_y, other)


def grad_kernel(rows, block, out):
    out[...] = matmul(rows[...], block[:, 0].reshape(rows.shape[1], -1)).astype(BF16)


def grad_part(rows, heads):
    vocab_count, rep_count, entries, size = heads.shape
    return pl.pallas_call(
        grad_kernel,
        out_shape=jax.ShapeDtypeStruct((rows.shape[0], rep_count * size), BF16),
        grid=(rep_count,),
        in_specs=[
            whole(rows.shape),
            pl.BlockSpec((vocab_count, 1, entries, size), lambda r: (0, r, 0, 0)),
        ],
        out_specs=pl.BlockSpec((rows.shape[0], size), lambda r: (0, r)),
        cost_estimate=FREE,
        compiler_params=pltpu.CompilerParams(vmem_limit_bytes=VMEM_BYTES),
        name="hidden_grad",
    )(rows, heads)


def expert_kernel(facts, *refs):
    hidden, got, (gain, gate, up, out, normed) = refs[:4], refs[4:8], refs[8:]
    count, size = hidden[0].shape[1:]
    width = normed.shape[1]

    @pl.when(pl.program_id(0) == 0)
    def _():
        own = [part[r] for part in hidden[:2] for r in range(2)]
        own += [part[r].astype(F32) for part in got[2:] for r in range(2)]
        partner = [part[r] for part in hidden[2:] for r in range(2)]
        partner += [part[r].astype(F32) for part in got[:2] for r in range(2)]
        for first, blocks in ((0, own), (count, partner)):
            squares = sum(jnp.sum(block * block, axis=1, keepdims=True) for block in blocks)
            scale = lax.rsqrt(squares / width + EPSILON)
            for i, block in enumerate(blocks):
                column = pl.multiple_of(facts[i] * size, size)
                normed[first : first + count, pl.ds(column, size)] = (
                    block * scale * gain[:, pl.ds(column, size)]
                ).astype(BF16)

    rows = normed[...]
    gate_pre = matmul(rows, gate[0], LAST)
    up_pre = matmul(rows, up[0], LAST)
    out[...] = (gate_pre / (1.0 + jnp.exp(-gate_pre)) * up_pre).astype(BF16)


def expert_hidden(facts, hidden, got, gain, gate, up):
    count, size = hidden[0].shape[1:]
    units, width = gate.shape[1:]
    tile = units // 3
    return pl.pallas_call(
        expert_kernel,
        out_shape=jax.ShapeDtypeStruct((2 * count, units), BF16),
        grid_spec=pltpu.PrefetchScalarGridSpec(
            num_scalar_prefetch=1,
            grid=(3,),
            in_specs=[whole(part.shape) for part in (*hidden, *got)]
            + [whole((1, width))]
            + [pl.BlockSpec((1, tile, width), lambda j, facts: (0, j, 0))] * 2,
            out_specs=pl.BlockSpec((2 * count, tile), lambda j, facts: (0, j)),
            scratch_shapes=[pltpu.VMEM((2 * count, width), BF16)],
        ),
        cost_estimate=FREE,
        compiler_params=pltpu.CompilerParams(vmem_limit_bytes=VMEM_BYTES),
        name="expert_hidden",
    )(facts, *hidden, *got, gain[None], gate, up)


def down_kernel(turned, facts, rows, weight, out):
    total = matmul(rows[...], weight[0]).astype(BF16)
    half = total.shape[0] // 2
    if turned:
        out[0, :half] = total[half:]
        out[0, half:] = total[:half]
    else:
        out[0] = total


def expert_down(facts, rows, weight, turned):
    count = facts.shape[0]
    units = rows.shape[1]
    size = weight.shape[2] // 8
    return pl.pallas_call(
        functools.partial(down_kernel, turned),
        out_shape=jax.ShapeDtypeStruct((count, rows.shape[0], size), BF16),
        grid_spec=pltpu.PrefetchScalarGridSpec(
            num_scalar_prefetch=1,
            grid=(count,),
            in_specs=[
                whole(rows.shape),
                pl.BlockSpec((1, units, size), lambda r, facts: (0, 0, facts[r])),
            ],
            out_specs=pl.BlockSpec((1, rows.shape[0], size), lambda r, facts: (r, 0, 0)),
        ),
        cost_estimate=FREE,
        compiler_params=pltpu.CompilerParams(vmem_limit_bytes=VMEM_BYTES),
        name="expert_down",
    )(facts, rows, weight)


def final_kernel(*refs):
    hidden_parts, (ours, terms, weight, gain, rows, squares) = refs[:4], refs[4:]
    total = 0.0
    for r in range(4):
        parts = [part[r % 2] for part in hidden_parts[r // 2 :: 2]]
        hidden = jnp.concatenate(parts, axis=0)
        out = (ours[r].astype(F32) + terms[r].astype(F32)).astype(BF16).astype(F32)
        hidden = hidden + weight[...] * out
        total += jnp.sum(hidden * hidden, axis=1, keepdims=True)
        rows[r] = (hidden * gain[r]).astype(BF16)
    squares[...] = jnp.broadcast_to(total, squares.shape)


def final_hidden(hidden, ours, terms, weight, gain):
    values = (*hidden, ours, terms, weight, gain)
    return pl.pallas_call(
        final_kernel,
        grid=(1,),
        in_specs=[whole(value.shape) for value in values],
        out_specs=[whole(ours.shape), whole((ours.shape[1], 128))],
        out_shape=[
            jax.ShapeDtypeStruct(ours.shape, BF16),
            jax.ShapeDtypeStruct((ours.shape[1], 128), F32),
        ],
        cost_estimate=FREE,
        compiler_params=pltpu.CompilerParams(vmem_limit_bytes=VMEM_BYTES),
        name="final_hidden",
    )(*values)


def per_device(
    queries,
    key_value,
    residual,
    out_weight,
    moe_gain,
    expert_ids,
    route_gate,
    gate_weight,
    up_weight,
    down_weight,
    final_gain,
    teacher_head,
    learner_hidden,
    learner_head,
    lengths,
):
    seq_dev, pos_ctx, head_cols = queries.shape
    pos_dev, width = residual.shape[1:]
    own_count = seq_dev * pos_dev
    half = width // 2
    ctx_index = lax.axis_index("ctx")
    vocab_index = lax.axis_index("vocab")
    rep_index = lax.axis_index("rep")
    plane = ctx_index * 4 + rep_index
    per_expert = own_count // 4
    vocab = 4 * teacher_head.shape[0]
    order = Order()

    def column_blocks(value, ctx):
        size = value.shape[-1] // 8
        return [pick(value, ctx * 4 + (rep_index ^ r), size, value.ndim - 1) for r in range(4)]

    def columns(value, ctx):
        return jnp.concatenate(column_blocks(value, ctx), axis=-1)

    shared_head = vocab_index * (head_cols // HD) // (QH // KVH)
    own_keys = lax.dynamic_slice_in_dim(key_value, shared_head * HD, HD, 3)
    other_keys = swap_x(own_keys)
    weight_y = swap_rep(out_weight, 2)
    weight_core = swap_rep(out_weight, 1)
    teacher_slice = pick(teacher_head, plane, width // 8, 1)
    teacher = line_gather(teacher_slice[None])

    expert_ids = lax.optimization_barrier((expert_ids, own_keys))[0]
    route_ids = expert_ids.reshape(own_count, -1)
    inside = route_ids < 4
    chosen = jnp.sum(jnp.where(inside, route_ids, 0), axis=1)
    route_weight = jnp.sum(jnp.where(inside, route_gate.reshape(own_count, -1), 0.0), axis=1)
    member = (chosen[:, None] == jnp.arange(4)[None, :]).astype(jnp.int32)
    slot_rank = jnp.sum((jnp.cumsum(member, axis=0) - 1) * member, axis=1)
    target = chosen * per_expert + slot_rank
    placed = target[None, :] == jnp.arange(own_count)[:, None]
    placer = placed.astype(BF16)
    line_target = chosen * own_count + vocab_index * per_expert + slot_rank
    line_facts = line_joined(line_gather(jnp.stack([line_target.astype(F32), route_weight])[None]))
    other_facts = swap_x(line_facts)
    order.ends(line_facts)
    mine = vocab_index * own_count + jnp.arange(own_count)[:, None]

    def routed(facts):
        targets = facts[:, 0].astype(jnp.int32).reshape(1, -1)
        weights = jnp.where(targets == mine, facts[:, 1].reshape(1, -1), 0.0)
        return targets, jnp.sum(weights, axis=1, keepdims=True)

    line_rows = jnp.arange(seq_dev * pos_ctx)
    chunk = line_rows // own_count
    chunk = jnp.where(chunk < 2, 2 * chunk + 1, 2 * chunk - 4) ^ vocab_index
    line_rows = (chunk * own_count + line_rows % own_count)[:, None]
    line_targets, my_weight = routed(line_facts)
    line_tokens = jnp.swapaxes(line_targets.reshape(4, seq_dev, pos_dev), 0, 1).reshape(1, -1)
    line_placer = (line_rows == line_tokens).astype(BF16)
    sent_count = 2 * own_count

    residual_rows = order.take(residual).reshape(own_count, width)
    own_residual = column_blocks(residual_rows, ctx_index)
    own_blocks = [jnp.stack(own_residual[:2]), jnp.stack(own_residual[2:])]
    own_placer = (line_rows == line_target[None, :]).astype(BF16)
    own_placers = (own_placer[:sent_count], own_placer[sent_count:])
    other_blocks = swap_x(jnp.stack(column_blocks(residual_rows, 1 - ctx_index)))
    learner_own = order.take(learner_hidden).reshape(own_count, width)
    other_targets, other_weight = routed(other_facts)
    other_target = pick(other_targets, vocab_index, own_count, 1)
    other_placer = (line_rows == other_target).astype(BF16)
    both_weight = jnp.concatenate([my_weight, other_weight], axis=0)

    other_slot = other_target.reshape(-1)
    other_slot = other_slot // own_count * per_expert + other_slot % per_expert
    other_place = (other_slot[None, :] == jnp.arange(own_count)[:, None]).astype(BF16)
    places = (rep_index ^ jnp.arange(4)).astype(jnp.int32)
    here, there = ctx_index * 4 + places, (1 - ctx_index) * 4 + places

    rows = jnp.concatenate([other_keys, own_keys], axis=2)
    ready = (queries, rows, line_placer, *own_blocks, *own_placers, other_placer, both_weight)
    ready += (weight_core,)
    ready = lax.optimization_barrier(ready)
    queries, rows, line_placer, *own_blocks = ready[:5]
    own_placers, (other_placer, both_weight, weight_core) = ready[5:7], ready[7:]
    heads_out = order.ends(attend(queries, rows, lengths))

    cuts = ((sent_count,), (own_count, own_count))

    def halved(far, beside):
        return order.ends((far.astype(F32) + beside[:, own_count:].astype(F32)).astype(BF16))

    def summed(mine, beside, across):
        total = mine.astype(F32) + beside[:, :own_count].astype(F32)
        return order.ends(total + across.astype(F32))

    other_blocks = order.waits(other_blocks)
    sent_rows, kept_rows = sorted_rows(order.take(line_placer), heads_out)
    order.ends(kept_rows)
    other_sent = swap_x(sent_rows)
    sent_0, mine_0, far_0 = project(
        order.take(sent_rows, kept_rows),
        own_placers,
        own_blocks[0],
        (out_weight, weight_core),
        cuts,
    )
    order.ends(mine_0)
    teacher = order.ends(line_joined(order.waits(*teacher)))
    beside_0 = swap_z(order.take(sent_0), 1)
    other_sent = order.waits(other_sent)
    beside_0 = order.waits(beside_0)
    across_0 = swap_z(halved(far_0, beside_0), 2)
    weight_y = order.waits(weight_y)
    weight_y_core = swap_rep(weight_y, 1)
    teacher_y = swap_rep(order.take(teacher), 2)
    weight_y_core, across_0 = order.waits(weight_y_core, across_0)

    sent_1, mine_1, far_1 = project(
        order.take(sent_rows, kept_rows),
        own_placers,
        own_blocks[1],
        (weight_y, weight_y_core),
        cuts,
    )
    order.ends(mine_1)
    beside_1 = swap_z(sent_1, 1)

    weights = (out_weight, weight_core, weight_y, weight_y_core)

    def other_part(rows, placer, first, cuts):
        return project(
            (rows,), (placer,), other_blocks[first : first + 2], weights[first : first + 2], (cuts,)
        )

    (sent_2,) = other_part(order.take(other_sent), other_placer[:sent_count], 0, (sent_count,))
    order.ends(sent_2)
    beside_2 = swap_z(sent_2, 1)
    other_kept = swap_x(order.take(kept_rows))
    (sent_3,) = other_part(order.take(other_sent), other_placer[:sent_count], 2, (sent_count,))
    order.ends(sent_3)
    beside_3 = swap_z(sent_3, 1)

    beside_1, beside_2, other_kept, teacher_y = order.waits(
        beside_1, beside_2, other_kept, teacher_y
    )
    across_1 = swap_z(halved(far_1, beside_1), 2)
    mine_2, far_2 = other_part(
        order.take(other_kept), other_placer[sent_count:], 0, (own_count, own_count)
    )
    order.ends(mine_2)
    across_2 = swap_z(halved(far_2, beside_2), 2)
    mine_3, far_3 = other_part(
        order.take(other_kept), other_placer[sent_count:], 2, (own_count, own_count)
    )
    order.ends(mine_3)
    beside_3 = order.waits(beside_3)
    across_3 = swap_z(halved(far_3, beside_3), 2)
    hidden_0 = summed(mine_0, beside_0, across_0)
    got_0 = swap_x(hidden_0.astype(BF16))
    hidden_1 = summed(mine_1, beside_1, order.waits(across_1))
    got_0, across_2 = order.waits(got_0, across_2)
    hidden_2 = summed(mine_2, beside_2, across_2)
    got_1, got_2 = (swap_x(order.take(part.astype(BF16))) for part in (hidden_1, hidden_2))
    across_3, got_1, got_2 = order.waits(across_3, got_1, got_2)
    hidden_3 = summed(mine_3, beside_3, across_3)
    got_3 = swap_x(hidden_3.astype(BF16))
    heads = lax.all_gather(order.take(learner_head), ("vocab", "rep"))
    heads = heads.reshape(4, 4, *learner_head.shape)
    got_3 = order.waits(got_3)
    learner_x = swap_x(columns(order.take(learner_own), 1 - ctx_index))

    hidden = (hidden_0, hidden_1, hidden_2, hidden_3)
    activated = expert_hidden(
        jnp.concatenate([here, there]).astype(jnp.int32),
        hidden,
        (got_0, got_1, got_2, got_3),
        moe_gain,
        gate_weight,
        up_weight,
    )
    order.ends(activated)
    terms = order.ends(expert_down(there, order.take(activated), down_weight, True))
    learner_x = order.waits(learner_x)
    terms = swap_x(order.take(terms))
    ours = order.ends(expert_down(here, order.take(activated), down_weight, False))
    learner_rows, plane_here, plane_there = learner_parts(
        here, placer, other_place, order.take(learner_own), order.take(learner_x)
    )
    order.ends(learner_rows)
    plane_y = swap_rep(plane_there, 2)
    terms = order.waits(terms)

    places = places.astype(jnp.int32)
    final_rows, squares = final_hidden(
        hidden,
        ours,
        order.take(terms),
        both_weight,
        jnp.stack(column_blocks(final_gain, ctx_index))[:, None],
    )
    order.ends(final_rows)
    other_squares = swap_x(squares[own_count:])
    cores = [swap_rep(order.take(block), 1) for block in (teacher, teacher_y)]
    other_squares, *cores = order.waits(other_squares, *cores)
    teacher = (teacher, cores[0], teacher_y, cores[1])
    teacher_own, teacher_other = [None, None], [None, None]
    teacher_own[0], teacher_other[0] = logits_part(order.take(final_rows), teacher, 0)
    order.ends(teacher_other[0])
    teacher_got = swap_x(teacher_other[0])
    teacher_own[1], teacher_other[1] = logits_part(order.take(final_rows), teacher, 1)
    order.ends(teacher_own[1])
    scale = lax.rsqrt((squares[:own_count, :1] + other_squares[:, :1]) / width + EPSILON)
    teacher_got, plane_y = order.waits(teacher_got, plane_y)
    part = order.ends((teacher_own[0] + teacher_got) * scale)
    teacher_got = swap_x(order.take(teacher_other[1]))
    teacher_logits = [line_exchange(part)]

    heads = order.waits(heads)
    learner_own_part, learner_other = (
        jnp.concatenate(parts, axis=1)
        for parts in zip(*(learner_logits_part(places, order.take(learner_rows), heads, i) for i in (0, 1)))
    )
    order.ends(learner_own_part)
    part = order.ends((teacher_own[1] + order.waits(teacher_got)) * scale)
    learner_other = swap_x(order.take(learner_other))
    teacher_logits[0] = order.waits(*teacher_logits[0])
    teacher_logits.append(line_exchange(order.take(part)))
    teacher_logits = [line_joined(order.take(*received)) for received in teacher_logits]
    teacher_logits = order.ends(jnp.concatenate(teacher_logits, axis=1))
    teacher_peak = jnp.max(teacher_logits, axis=1, keepdims=True)
    teacher_lse = teacher_peak + jnp.log(
        jnp.sum(jnp.exp(teacher_logits - teacher_peak), axis=1, keepdims=True)
    )
    plane_core = swap_rep(jnp.stack([plane_here[1], plane_y[1]]), 1)
    learner_other, plane_core = order.waits(learner_other, plane_core)
    learner_logits = learner_own_part + learner_other
    learner_peak = jnp.max(learner_logits, axis=1, keepdims=True)
    learner_exp = jnp.exp(learner_logits - learner_peak)
    learner_total = jnp.sum(learner_exp, axis=1, keepdims=True)
    learner_lse = learner_peak + jnp.log(learner_total)

    logit_gap = learner_logits - teacher_logits
    mean_gap = jnp.sum(learner_exp * logit_gap, axis=1, keepdims=True) / learner_total
    divergence = mean_gap - learner_lse + teacher_lse
    row_pos = ctx_index * pos_ctx + vocab_index * pos_dev + jnp.arange(pos_dev)
    live = row_pos[None, :] < lengths[:, None]
    live_sorted = jnp.any(placed & live.reshape(1, -1), axis=1)
    learner_prob = jnp.exp(learner_logits - learner_lse)
    dlogits = jnp.where(
        live_sorted[:, None], learner_prob * (logit_gap - mean_gap), 0.0
    ).astype(BF16)
    dlogits = order.ends(matmul(placer, dlogits, FIRST).astype(BF16))

    rows = own_count // 2
    along_x, along_y = swap_x(dlogits), swap_rep(dlogits, 2)
    along_x, along_y = order.waits(along_x, along_y)
    near, far = swap_x(along_y[:rows]), swap_rep(along_x[rows:], 2)
    near, far = order.waits(near, far)
    mine = order.ends(jnp.concatenate([dlogits, along_x, along_y, near, far], axis=0))
    core = order.waits(swap_rep(mine, 1))
    blocks = (vocab_index ^ jnp.array([1, 3, 0, 2])).astype(jnp.int32)
    parts = head_parts(blocks, mine, core, plane_here, plane_y, plane_core)
    order.ends(parts[0])
    sums = [(kept, swap_z(sent, 1)) for sent, kept in zip(parts[:2], parts[2:])]
    other_grad = order.ends(grad_part(order.take(along_x), heads))
    other_grad = swap_x(other_grad)
    own_grad = order.ends(grad_part(order.take(dlogits), heads))
    for i, (kept, beside) in enumerate(sums):
        beside = order.waits(beside)
        far = order.ends((kept[1].astype(F32) + beside[1].astype(F32)).astype(BF16))
        sums[i] = (kept[0], beside[0], swap_z(far, 2))
    kl_rows = jnp.sum(jnp.where(placed, order.take(divergence), 0.0), axis=0)
    row_kl = order.ends(jnp.where(live, kl_rows.reshape(seq_dev, pos_dev), 0.0))
    other_grad = order.take(other_grad)
    hidden_grad = join_absolute([own_grad, other_grad], ctx_index, 1)
    order.ends(hidden_grad)
    head_grad = jnp.concatenate(
        [
            mine.astype(F32) + beside.astype(F32) + order.take(across).astype(F32)
            for mine, beside, across in sums
        ],
        axis=1,
    ).astype(BF16)
    return (hidden_grad.reshape(seq_dev, pos_dev, width), head_grad, row_kl)


def per_device_general(
    queries,
    key_value,
    residual,
    out_weight,
    moe_gain,
    expert_ids,
    route_gate,
    gate_weight,
    up_weight,
    down_weight,
    final_gain,
    teacher_head,
    learner_hidden,
    learner_head,
    lengths,
):
    seq_dev, pos_ctx, head_cols = queries.shape
    pos_dev = residual.shape[1]
    width = residual.shape[2]
    vocab_count = lax.axis_size("vocab")
    ctx_index = lax.axis_index("ctx")
    vocab_index = lax.axis_index("vocab")
    heads_dev = head_cols // HD
    shared_head = vocab_index * heads_dev // (QH // KVH)
    key_rows = lax.dynamic_slice_in_dim(key_value, shared_head * HD, HD, 3)
    query_heads = queries.reshape(seq_dev, pos_ctx, heads_dev, HD)
    query_pos = ctx_index * pos_ctx + jnp.arange(pos_ctx)
    score_scale = HD ** (-0.5)
    shard_rows = lax.all_gather(key_rows, "ctx", axis=2, tiled=True)
    running_max = jnp.full((seq_dev, pos_ctx, heads_dev), MASKED, jnp.float32)
    key_pos = jnp.arange(shard_rows.shape[2])
    scores = (
        jnp.einsum("sqhd,skd->sqhk", query_heads, shard_rows[0], preferred_element_type=jnp.float32)
        * score_scale
    )
    allowed = (key_pos[None, None, :] <= query_pos[None, :, None]) & (
        key_pos[None, None, :] < lengths[:, None, None]
    )
    allowed = allowed[:, :, None, :]
    scores = jnp.where(allowed, scores, MASKED)
    new_max = jnp.maximum(running_max, jnp.max(scores, axis=-1))
    exponent = jnp.where(allowed, jnp.exp(scores - new_max[..., None]), 0.0)
    running_sum = jnp.sum(exponent, axis=-1)
    weighted = jnp.einsum(
        "sqhk,skd->sqhd",
        exponent.astype(jnp.bfloat16),
        shard_rows[1],
        preferred_element_type=jnp.float32,
    )
    final_max, final_sum, weighted = (new_max, running_sum, weighted)
    heads_out = (
        (weighted / final_sum[..., None]).astype(jnp.bfloat16).reshape(seq_dev * pos_ctx, head_cols)
    )
    mixed = jnp.dot(
        heads_out,
        lax.all_gather(out_weight, ("ctx", "rep"), axis=1, tiled=True),
        preferred_element_type=jnp.float32,
    )
    attn_rows = lax.psum_scatter(
        mixed.reshape(seq_dev, pos_ctx, width).astype(jnp.bfloat16),
        "vocab",
        scatter_dimension=1,
        tiled=True,
    ).astype(jnp.float32)
    hidden_one = residual.astype(jnp.float32) + attn_rows
    own_count = seq_dev * pos_dev
    normed = rms_scale(hidden_one, moe_gain).astype(jnp.bfloat16).reshape(own_count, width)
    route_ids = expert_ids.reshape(own_count, -1)
    inside = route_ids < vocab_count
    chosen = jnp.sum(jnp.where(inside, route_ids, 0), axis=1)
    route_weight = jnp.sum(jnp.where(inside, route_gate.reshape(own_count, -1), 0.0), axis=1)
    per_expert = own_count // vocab_count
    member = (chosen[:, None] == jnp.arange(vocab_count)[None, :]).astype(jnp.int32)
    slot_rank = jnp.sum((jnp.cumsum(member, axis=0) - 1) * member, axis=1)
    target = chosen * per_expert + slot_rank
    placer = (target[None, :] == jnp.arange(own_count)[:, None]).astype(jnp.bfloat16)
    outgoing = jnp.dot(placer, normed, preferred_element_type=jnp.float32).astype(jnp.bfloat16)
    arrived = lax.all_to_all(
        outgoing.reshape(vocab_count, per_expert, width),
        "vocab",
        split_axis=0,
        concat_axis=0,
        tiled=True,
    )
    arrived = arrived.reshape(own_count, width)
    gate_slice = gate_weight[0]
    up_slice = up_weight[0]
    down_slice = down_weight[0]
    contract_last = (((1,), (1,)), ((), ()))
    shard_rows = lax.all_gather(arrived, "ctx", axis=0, tiled=True)
    gate_pre = lax.dot_general(
        shard_rows, gate_slice, contract_last, preferred_element_type=jnp.float32
    )
    up_pre = lax.dot_general(
        shard_rows, up_slice, contract_last, preferred_element_type=jnp.float32
    )
    activated = (jax.nn.silu(gate_pre) * up_pre).astype(jnp.bfloat16)
    expert_terms = jnp.dot(activated, down_slice, preferred_element_type=jnp.float32)
    expert_out = lax.psum_scatter(
        expert_terms.astype(jnp.bfloat16), "ctx", scatter_dimension=0, tiled=True
    )
    returned_rows = lax.all_to_all(
        expert_out.reshape(vocab_count, per_expert, width),
        "vocab",
        split_axis=0,
        concat_axis=0,
        tiled=True,
    )
    restored = lax.dot_general(
        placer,
        returned_rows.reshape(own_count, width),
        (((0,), (0,)), ((), ())),
        preferred_element_type=jnp.float32,
    )
    hidden_two = hidden_one.reshape(own_count, width) + route_weight[:, None] * restored
    final_rows = (
        rms_scale(hidden_two, final_gain).astype(jnp.bfloat16).reshape(seq_dev, pos_dev, width)
    )
    teacher_rows, learner_rows = (
        lax.all_gather(final_rows, "vocab", axis=1, tiled=True),
        lax.all_gather(learner_hidden, "vocab", axis=1, tiled=True),
    )
    learner_full = lax.all_gather(learner_head, ("ctx", "rep"), axis=1, tiled=True)
    teacher_flat = teacher_rows.reshape(-1, width)
    learner_flat = learner_rows.reshape(-1, width)
    teacher_logits = lax.dot_general(
        teacher_flat, teacher_head, contract_last, preferred_element_type=jnp.float32
    )
    learner_logits = lax.dot_general(
        learner_flat, learner_full, contract_last, preferred_element_type=jnp.float32
    )
    logit_gap = learner_logits - teacher_logits
    learner_peak = jnp.max(learner_logits, axis=1)
    teacher_peak = jnp.max(teacher_logits, axis=1)
    learner_peak, teacher_peak = lax.pmax((learner_peak, teacher_peak), "vocab")
    learner_exp = jnp.exp(learner_logits - learner_peak[:, None])
    learner_total, cross_total, teacher_total = lax.psum(
        (
            jnp.sum(learner_exp, axis=1),
            jnp.sum(learner_exp * logit_gap, axis=1),
            jnp.sum(jnp.exp(teacher_logits - teacher_peak[:, None]), axis=1),
        ),
        "vocab",
    )
    learner_lse = learner_peak + jnp.log(learner_total)
    teacher_lse = teacher_peak + jnp.log(teacher_total)
    mean_gap = cross_total / learner_total
    divergence = mean_gap - learner_lse + teacher_lse
    row_pos = ctx_index * pos_ctx + jnp.arange(pos_ctx)
    live_rows = (row_pos[None, :] < lengths[:, None]).reshape(-1)
    learner_prob = jnp.exp(learner_logits - learner_lse[:, None])
    dlogits = jnp.where(
        live_rows[:, None], learner_prob * (logit_gap - mean_gap[:, None]), 0.0
    ).astype(jnp.bfloat16)
    kl_block = jnp.where(live_rows, divergence, 0.0).reshape(seq_dev, pos_ctx)
    row_kl = lax.dynamic_slice_in_dim(kl_block, vocab_index * pos_dev, pos_dev, 1)
    by_position = jnp.swapaxes(dlogits.reshape(seq_dev, pos_ctx, -1), 0, 1)
    shard_rows = by_position
    grad_rows = lax.psum_scatter(
        jnp.einsum(
            "psv,vd->psd", shard_rows, learner_full, preferred_element_type=jnp.float32
        ).astype(jnp.bfloat16),
        "vocab",
        scatter_dimension=0,
        tiled=True,
    ).astype(jnp.float32)
    hidden_grad = jnp.swapaxes(grad_rows, 0, 1).astype(jnp.bfloat16)
    head_sum = lax.psum_scatter(
        lax.dot_general(
            learner_flat, dlogits, (((0,), (0,)), ((), ())), preferred_element_type=jnp.float32
        ).astype(jnp.bfloat16),
        ("ctx", "rep"),
        scatter_dimension=0,
        tiled=True,
    ).astype(jnp.float32)
    head_grad = jnp.transpose(head_sum).astype(jnp.bfloat16)
    return (hidden_grad, head_grad, row_kl)


def solution(mesh):
    placed = (
        P("rep", "ctx", "vocab"),
        P(None, "rep", "ctx", None),
        P("rep", ("ctx", "vocab"), None),
        P("vocab", ("ctx", "rep")),
        P(),
        P("rep", ("ctx", "vocab"), None),
        P("rep", ("ctx", "vocab"), None),
        P("vocab", "ctx", None),
        P("vocab", "ctx", None),
        P("vocab", "ctx", None),
        P(),
        P("vocab", None),
        P("rep", ("ctx", "vocab"), None),
        P("vocab", ("ctx", "rep")),
        P("rep"),
    )
    shape = dict(mesh.shape)
    swaps = (shape["ctx"], shape["vocab"], shape["rep"]) == (2, 4, 4)
    return jax.shard_map(
        per_device if swaps else per_device_general,
        mesh=mesh,
        in_specs=placed,
        out_specs=(
            P("rep", ("ctx", "vocab"), None),
            P("vocab", ("ctx", "rep")),
            P("rep", ("ctx", "vocab")),
        ),
        check_vma=False,
    )
```

```python
import functools

import jax
import jax.numpy as jnp
from jax import lax
from jax.experimental import pallas as pl
from jax.experimental.pallas import tpu as pltpu
from jax.sharding import PartitionSpec as P

QH = 64
KVH = 4
HD = 128

EPSILON = 1e-06
MASKED = -1e30
PLANE = ("ctx", "rep")
LAST = (((1,), (1,)), ((), ()))
FIRST = (((0,), (0,)), ((), ()))
F32 = jnp.float32
BF16 = jnp.bfloat16


def matmul(left, right, dims=(((1,), (0,)), ((), ()))):
    return lax.dot_general(left, right, dims, preferred_element_type=F32)


def rms_scale(values, gain):
    mean_square = jnp.mean(values * values, axis=-1, keepdims=True)
    return values * lax.rsqrt(mean_square + EPSILON) * gain


class Order:
    def __init__(self):
        self.last = None

    def take(self, *values):
        if self.last is None:
            return values if len(values) > 1 else values[0]
        values = lax.optimization_barrier((*values, self.last))[:-1]
        return values if len(values) > 1 else values[0]

    def ends(self, value):
        self.last = value
        return value

    def waits(self, *values):
        values = lax.optimization_barrier((*values, self.last))[:-1]
        self.last = values[0]
        return values if len(values) > 1 else values[0]


def swap_x(value):
    return lax.ppermute(value, "ctx", [(0, 1), (1, 0)])


def swap_rep(value, offset):
    return lax.ppermute(value, "rep", [(i, i ^ offset) for i in range(4)])


def swap_z(value, offset):
    return lax.ppermute(value, "vocab", [(i, i ^ offset) for i in range(4)])


def pick(value, index, size, axis):
    return lax.dynamic_slice_in_dim(value, index * size, size, axis)


def split_relative(value, index, count, axis):
    size = value.shape[axis] // count
    return [pick(value, index ^ r, size, axis) for r in range(count)]


def join_absolute(blocks, index, axis):
    count = len(blocks)
    return jnp.concatenate(
        [
            lax.select_n(index, *[blocks[j ^ i] for i in range(count)])
            for j in range(count)
        ],
        axis=axis,
    )


def line_gather(own):
    return [own] + [swap_z(own, r) for r in (1, 2, 3)]


def line_exchange(value):
    blocks = split_relative(value, lax.axis_index("vocab"), 4, 0)
    return [blocks[0]] + [swap_z(blocks[r], r) for r in (1, 2, 3)]


def line_joined(received):
    return join_absolute(received, lax.axis_index("vocab"), 0)


HEADS_STEP = 4


def attend_kernel(facts, query, rows, out):
    pos_ctx = query.shape[1]
    keys = rows.shape[2]
    length = facts[pl.program_id(0)]
    query_pos = facts[pl.num_programs(0)] + lax.broadcasted_iota(jnp.int32, (pos_ctx, keys), 0)
    key_pos = facts[pl.num_programs(0) + 1] + lax.broadcasted_iota(jnp.int32, (pos_ctx, keys), 1)
    allowed = (key_pos <= query_pos) & (key_pos < length) & (key_pos >= 0)
    bias = jnp.where(allowed, 0.0, MASKED)
    for head in range(query.shape[2] // HD):
        cols = slice(head * HD, (head + 1) * HD)
        scores = matmul(query[0, :, cols], rows[0, 0], LAST) * HD ** (-0.5) + bias
        peak = jnp.max(scores, axis=-1, keepdims=True)
        exponent = jnp.exp(scores - peak)
        total = jnp.sum(exponent, axis=-1, keepdims=True)
        weighted = matmul(exponent.astype(BF16), rows[1, 0])
        out[:, cols] = (weighted / total).astype(BF16)


def attend(queries, rows, lengths):
    seq_dev, pos_ctx, head_cols = queries.shape
    ctx_index = lax.axis_index("ctx")
    facts = jnp.concatenate([lengths, jnp.stack([ctx_index * pos_ctx, (ctx_index - 1) * pos_ctx])])
    step_cols = HEADS_STEP * HD
    return pl.pallas_call(
        attend_kernel,
        out_shape=jax.ShapeDtypeStruct((seq_dev * pos_ctx, head_cols), BF16),
        grid_spec=pltpu.PrefetchScalarGridSpec(
            num_scalar_prefetch=1,
            grid=(seq_dev, head_cols // step_cols),
            in_specs=[
                pl.BlockSpec(
                    (1, pos_ctx, step_cols), lambda s, h, facts: (s, 0, h)
                ),
                pl.BlockSpec((2, 1, rows.shape[2], HD), lambda s, h, facts: (0, s, 0, 0)),
            ],
            out_specs=pl.BlockSpec((pos_ctx, step_cols), lambda s, h, facts: (s, h)),
        ),
        cost_estimate=pl.CostEstimate(flops=0, bytes_accessed=0, transcendentals=0),
        compiler_params=pltpu.CompilerParams(vmem_limit_bytes=32 * 2**20),
        name="attend",
    )(facts, queries, rows)


FREE = pl.CostEstimate(flops=0, bytes_accessed=0, transcendentals=0)
VMEM_BYTES = 32 * 2**20


def whole(shape):
    return pl.BlockSpec(shape, lambda *_: (0,) * len(shape))


def project_kernel(count, parts, *refs):
    groups = len(parts)
    rows, placers, refs = refs[:groups], refs[groups : 2 * groups], refs[2 * groups :]
    residual, weights, outs = refs[0], refs[1 : 1 + count], list(refs[1 + count :])
    for row, placer, part in zip(rows, placers, parts):
        targets = [outs.pop(0) for _ in part]
        for r in range(count):
            total = matmul(row[...], weights[r][...]) + matmul(placer[...], residual[r])
            first = 0
            for target, size in zip(targets, part):
                target[r] = total[first : first + size].astype(BF16)
                first += size


def project(rows, placers, residual, weights, parts):
    count = len(weights)
    size = weights[0].shape[1]
    tile = size // 2
    cuts = [part for group in parts for part in group]
    return pl.pallas_call(
        functools.partial(project_kernel, count, parts),
        out_shape=[jax.ShapeDtypeStruct((count, part, size), BF16) for part in cuts],
        grid=(2,),
        in_specs=[whole(value.shape) for value in (*rows, *placers)]
        + [pl.BlockSpec((count, residual.shape[1], tile), lambda j: (0, 0, j))]
        + [pl.BlockSpec((weights[0].shape[0], tile), lambda j: (0, j))] * count,
        out_specs=[pl.BlockSpec((count, part, tile), lambda j: (0, 0, j)) for part in cuts],
        cost_estimate=FREE,
        compiler_params=pltpu.CompilerParams(vmem_limit_bytes=VMEM_BYTES),
        name="project",
    )(*rows, *placers, residual, *weights)


def sort_kernel(placer, heads, sent, kept):
    half = sent.shape[0]
    sent[...] = matmul(placer[:half], heads[...]).astype(BF16)
    kept[...] = matmul(placer[half:], heads[...]).astype(BF16)


def sorted_rows(placer, heads):
    rows, width = heads.shape
    tile = width // 4
    return pl.pallas_call(
        sort_kernel,
        out_shape=[jax.ShapeDtypeStruct((rows // 2, width), BF16)] * 2,
        grid=(4,),
        in_specs=[whole(placer.shape), pl.BlockSpec((rows, tile), lambda j: (0, j))],
        out_specs=[pl.BlockSpec((rows // 2, tile), lambda j: (0, j))] * 2,
        cost_estimate=FREE,
        compiler_params=pltpu.CompilerParams(vmem_limit_bytes=VMEM_BYTES),
        name="sorted_rows",
    )(placer, heads)


def logits_kernel(rows, *refs):
    blocks, (own, other) = refs[:-2], refs[-2:]
    count = own.shape[0]
    total = 0.0
    for r, block in enumerate(blocks):
        total += matmul(rows[r], block[...].reshape(own.shape[1], -1), LAST)
    own[...] = total[:count]
    other[...] = total[count:]


def logits_part(rows, heads, part):
    vocab_count, entries, size = heads[0].shape
    tile = vocab_count // 2 * entries
    count = rows.shape[1] // 2
    block = (vocab_count // 2, entries, size)
    return pl.pallas_call(
        logits_kernel,
        out_shape=[jax.ShapeDtypeStruct((count, tile), F32)] * 2,
        grid=(1,),
        in_specs=[whole(rows.shape)] + [pl.BlockSpec(block, lambda j: (part, 0, 0))] * len(heads),
        out_specs=[whole((count, tile))] * 2,
        cost_estimate=FREE,
        compiler_params=pltpu.CompilerParams(vmem_limit_bytes=VMEM_BYTES),
        name="logits",
    )(rows, *heads)


def learner_logits_kernel(facts, rows, *refs):
    logits_kernel(rows, *[ref.at[:, 0] for ref in refs[:4]], *refs[4:])


def learner_logits_part(facts, rows, heads, part):
    vocab_count, rep_count, entries, size = heads.shape
    tile = vocab_count // 2 * entries
    count = rows.shape[1] // 2
    block = (vocab_count // 2, 1, entries, size)
    return pl.pallas_call(
        learner_logits_kernel,
        out_shape=[jax.ShapeDtypeStruct((count, tile), F32)] * 2,
        grid_spec=pltpu.PrefetchScalarGridSpec(
            num_scalar_prefetch=1,
            grid=(1,),
            in_specs=[whole(rows.shape)]
            + [
                pl.BlockSpec(block, lambda j, facts, r=r: (part, facts[r], 0, 0))
                for r in range(rep_count)
            ],
            out_specs=[whole((count, tile))] * 2,
        ),
        cost_estimate=FREE,
        compiler_params=pltpu.CompilerParams(vmem_limit_bytes=VMEM_BYTES),
        name="logits",
    )(facts, rows, *[heads] * rep_count)


def join_kernel(facts, *refs):
    sources, out = refs[:-1], refs[-1]
    for r, source in enumerate(sources):

        @pl.when((facts[0] ^ pl.program_id(0)) == r)
        def _():
            out[0] = source[...]


def joined(index, blocks):
    count = len(blocks)
    shape = blocks[0].shape
    return pl.pallas_call(
        join_kernel,
        out_shape=jax.ShapeDtypeStruct((count, *shape), blocks[0].dtype),
        grid_spec=pltpu.PrefetchScalarGridSpec(
            num_scalar_prefetch=1,
            grid=(count,),
            in_specs=[whole(shape)] * count,
            out_specs=pl.BlockSpec((1, *shape), lambda j, facts: (j, 0, 0)),
        ),
        cost_estimate=FREE,
        compiler_params=pltpu.CompilerParams(vmem_limit_bytes=VMEM_BYTES),
        name="joined",
    )(index.reshape(1).astype(jnp.int32), *blocks)


def learner_kernel(facts, placer, other_placer, own, other, rows, near, far):
    r = pl.program_id(0)
    count = own.shape[0]
    rows[0, :count] = matmul(placer[...], own[...]).astype(BF16)
    rows[0, count:] = matmul(other_placer[...], other[...]).astype(BF16)
    for out, here in ((near, r < 2), (far, r >= 2)):

        @pl.when(here)
        def _():
            out[0, :count] = own[...]
            out[0, count:] = other[...]


def learner_parts(facts, placer, other_placer, own, other):
    count = own.shape[0]
    size = own.shape[1] // 8
    shape = (1, 2 * count, size)
    return pl.pallas_call(
        learner_kernel,
        out_shape=[
            jax.ShapeDtypeStruct((blocks, 2 * count, size), BF16) for blocks in (4, 2, 2)
        ],
        grid_spec=pltpu.PrefetchScalarGridSpec(
            num_scalar_prefetch=1,
            grid=(4,),
            in_specs=[
                whole(placer.shape),
                whole(placer.shape),
                pl.BlockSpec((count, size), lambda r, facts: (0, facts[r])),
                pl.BlockSpec((count, size), lambda r, facts: (0, r)),
            ],
            out_specs=[
                pl.BlockSpec(shape, lambda r, facts: (r, 0, 0)),
                pl.BlockSpec(shape, lambda r, facts: (jnp.minimum(r, 1), 0, 0)),
                pl.BlockSpec(shape, lambda r, facts: (jnp.maximum(r - 2, 0), 0, 0)),
            ],
        ),
        cost_estimate=FREE,
        compiler_params=pltpu.CompilerParams(vmem_limit_bytes=VMEM_BYTES),
        name="learner_parts",
    )(facts, placer, other_placer, own, other)


def head_kernel(facts, mine, core, here, along_y, other, *outs):
    i = pl.program_id(0)
    count = here.shape[1]
    total = matmul(mine[:count], here[0], FIRST) + matmul(mine[count:], along_y[0], FIRST)
    total += matmul(core[:count], other[0], FIRST) + matmul(core[count:], other[1], FIRST)
    total = total.astype(BF16)
    size = total.shape[1] // 2
    for group, now in ((outs[:2], i < 2), (outs[2:], i >= 2)):

        @pl.when(now)
        def _():
            for k, out in enumerate(group):
                out[0] = total[:, k * size : (k + 1) * size]


def head_parts(facts, mine, core, here, along_y, other):
    rows, vocab = mine.shape
    tile, size = vocab // 4, here.shape[2] // 2
    shape = (1, tile, size)
    first = pl.BlockSpec(shape, lambda i, facts: (jnp.minimum(i, 1), 0, 0))
    rest = pl.BlockSpec(shape, lambda i, facts: (jnp.maximum(i - 2, 0), 0, 0))
    return pl.pallas_call(
        head_kernel,
        out_shape=[jax.ShapeDtypeStruct((2, tile, size), BF16)] * 4,
        grid_spec=pltpu.PrefetchScalarGridSpec(
            num_scalar_prefetch=1,
            grid=(4,),
            in_specs=[pl.BlockSpec((rows, tile), lambda i, facts: (0, facts[i]))] * 2
            + [whole(value.shape) for value in (here, along_y, other)],
            out_specs=[first, first, rest, rest],
        ),
        cost_estimate=FREE,
        compiler_params=pltpu.CompilerParams(vmem_limit_bytes=VMEM_BYTES),
        name="head_parts",
    )(facts, mine, core, here, along_y, other)


def grad_kernel(rows, block, out):
    out[...] = matmul(rows[...], block[:, 0].reshape(rows.shape[1], -1)).astype(BF16)


def grad_part(rows, heads):
    vocab_count, rep_count, entries, size = heads.shape
    return pl.pallas_call(
        grad_kernel,
        out_shape=jax.ShapeDtypeStruct((rows.shape[0], rep_count * size), BF16),
        grid=(rep_count,),
        in_specs=[
            whole(rows.shape),
            pl.BlockSpec((vocab_count, 1, entries, size), lambda r: (0, r, 0, 0)),
        ],
        out_specs=pl.BlockSpec((rows.shape[0], size), lambda r: (0, r)),
        cost_estimate=FREE,
        compiler_params=pltpu.CompilerParams(vmem_limit_bytes=VMEM_BYTES),
        name="hidden_grad",
    )(rows, heads)


def expert_kernel(facts, *refs):
    hidden, got, (gain, gate, up, out, normed) = refs[:4], refs[4:8], refs[8:]
    count, size = hidden[0].shape[1:]
    width = normed.shape[1]

    @pl.when(pl.program_id(0) == 0)
    def _():
        own = [part[r] for part in hidden[:2] for r in range(2)]
        own += [part[r].astype(F32) for part in got[2:] for r in range(2)]
        partner = [part[r] for part in hidden[2:] for r in range(2)]
        partner += [part[r].astype(F32) for part in got[:2] for r in range(2)]
        for first, blocks in ((0, own), (count, partner)):
            squares = sum(jnp.sum(block * block, axis=1, keepdims=True) for block in blocks)
            scale = lax.rsqrt(squares / width + EPSILON)
            for i, block in enumerate(blocks):
                column = pl.multiple_of(facts[i] * size, size)
                normed[first : first + count, pl.ds(column, size)] = (
                    block * scale * gain[:, pl.ds(column, size)]
                ).astype(BF16)

    rows = normed[...]
    gate_pre = matmul(rows, gate[0], LAST)
    up_pre = matmul(rows, up[0], LAST)
    out[...] = (gate_pre / (1.0 + jnp.exp(-gate_pre)) * up_pre).astype(BF16)


def expert_hidden(facts, hidden, got, gain, gate, up):
    count, size = hidden[0].shape[1:]
    units, width = gate.shape[1:]
    tile = units // 3
    return pl.pallas_call(
        expert_kernel,
        out_shape=jax.ShapeDtypeStruct((2 * count, units), BF16),
        grid_spec=pltpu.PrefetchScalarGridSpec(
            num_scalar_prefetch=1,
            grid=(3,),
            in_specs=[whole(part.shape) for part in (*hidden, *got)]
            + [whole((1, width))]
            + [pl.BlockSpec((1, tile, width), lambda j, facts: (0, j, 0))] * 2,
            out_specs=pl.BlockSpec((2 * count, tile), lambda j, facts: (0, j)),
            scratch_shapes=[pltpu.VMEM((2 * count, width), BF16)],
        ),
        cost_estimate=FREE,
        compiler_params=pltpu.CompilerParams(vmem_limit_bytes=48 * 2**20),
        name="expert_hidden",
    )(facts, *hidden, *got, gain[None], gate, up)


def down_kernel(turned, facts, rows, weight, out):
    total = matmul(rows[...], weight[0]).astype(BF16)
    half = total.shape[0] // 2
    if turned:
        out[0, :half] = total[half:]
        out[0, half:] = total[:half]
    else:
        out[0] = total


def expert_down(facts, rows, weight, turned):
    count = facts.shape[0]
    units = rows.shape[1]
    size = weight.shape[2] // 8
    return pl.pallas_call(
        functools.partial(down_kernel, turned),
        out_shape=jax.ShapeDtypeStruct((count, rows.shape[0], size), BF16),
        grid_spec=pltpu.PrefetchScalarGridSpec(
            num_scalar_prefetch=1,
            grid=(count,),
            in_specs=[
                whole(rows.shape),
                pl.BlockSpec((1, units, size), lambda r, facts: (0, 0, facts[r])),
            ],
            out_specs=pl.BlockSpec((1, rows.shape[0], size), lambda r, facts: (r, 0, 0)),
        ),
        cost_estimate=FREE,
        compiler_params=pltpu.CompilerParams(vmem_limit_bytes=48 * 2**20),
        name="expert_down",
    )(facts, rows, weight)


def final_kernel(*refs):
    hidden_parts, (ours, terms, weight, gain, rows, squares) = refs[:4], refs[4:]
    total = 0.0
    for r in range(4):
        parts = [part[r % 2] for part in hidden_parts[r // 2 :: 2]]
        hidden = jnp.concatenate(parts, axis=0)
        out = (ours[r].astype(F32) + terms[r].astype(F32)).astype(BF16).astype(F32)
        hidden = hidden + weight[...] * out
        total += jnp.sum(hidden * hidden, axis=1, keepdims=True)
        rows[r] = (hidden * gain[r]).astype(BF16)
    squares[...] = jnp.broadcast_to(total, squares.shape)


def final_hidden(hidden, ours, terms, weight, gain):
    values = (*hidden, ours, terms, weight, gain)
    return pl.pallas_call(
        final_kernel,
        grid=(1,),
        in_specs=[whole(value.shape) for value in values],
        out_specs=[whole(ours.shape), whole((ours.shape[1], 128))],
        out_shape=[
            jax.ShapeDtypeStruct(ours.shape, BF16),
            jax.ShapeDtypeStruct((ours.shape[1], 128), F32),
        ],
        cost_estimate=FREE,
        compiler_params=pltpu.CompilerParams(vmem_limit_bytes=VMEM_BYTES),
        name="final_hidden",
    )(*values)


def per_device(
    queries,
    key_value,
    residual,
    out_weight,
    moe_gain,
    expert_ids,
    route_gate,
    gate_weight,
    up_weight,
    down_weight,
    final_gain,
    teacher_head,
    learner_hidden,
    learner_head,
    lengths,
):
    seq_dev, pos_ctx, head_cols = queries.shape
    pos_dev, width = residual.shape[1:]
    own_count = seq_dev * pos_dev
    half = width // 2
    ctx_index = lax.axis_index("ctx")
    vocab_index = lax.axis_index("vocab")
    rep_index = lax.axis_index("rep")
    plane = ctx_index * 4 + rep_index
    per_expert = own_count // 4
    vocab = 4 * teacher_head.shape[0]
    order = Order()

    def column_blocks(value, ctx):
        size = value.shape[-1] // 8
        return [pick(value, ctx * 4 + (rep_index ^ r), size, value.ndim - 1) for r in range(4)]

    def columns(value, ctx):
        return jnp.concatenate(column_blocks(value, ctx), axis=-1)

    shared_head = vocab_index * (head_cols // HD) // (QH // KVH)
    own_keys = lax.dynamic_slice_in_dim(key_value, shared_head * HD, HD, 3)
    other_keys = swap_x(own_keys)
    weight_y = swap_rep(out_weight, 2)
    weight_core = swap_rep(out_weight, 1)
    teacher_slice = pick(teacher_head, plane, width // 8, 1)
    teacher = line_gather(teacher_slice[None])

    expert_ids = lax.optimization_barrier((expert_ids, own_keys))[0]
    route_ids = expert_ids.reshape(own_count, -1)
    inside = route_ids < 4
    chosen = jnp.sum(jnp.where(inside, route_ids, 0), axis=1)
    route_weight = jnp.sum(jnp.where(inside, route_gate.reshape(own_count, -1), 0.0), axis=1)
    member = (chosen[:, None] == jnp.arange(4)[None, :]).astype(jnp.int32)
    slot_rank = jnp.sum((jnp.cumsum(member, axis=0) - 1) * member, axis=1)
    target = chosen * per_expert + slot_rank
    placed = target[None, :] == jnp.arange(own_count)[:, None]
    placer = placed.astype(BF16)
    line_target = chosen * own_count + vocab_index * per_expert + slot_rank
    line_facts = line_joined(line_gather(jnp.stack([line_target.astype(F32), route_weight])[None]))
    other_facts = swap_x(line_facts)
    order.ends(line_facts)
    mine = vocab_index * own_count + jnp.arange(own_count)[:, None]

    def routed(facts):
        targets = facts[:, 0].astype(jnp.int32).reshape(1, -1)
        weights = jnp.where(targets == mine, facts[:, 1].reshape(1, -1), 0.0)
        return targets, jnp.sum(weights, axis=1, keepdims=True)

    line_rows = jnp.arange(seq_dev * pos_ctx)
    chunk = line_rows // own_count
    chunk = jnp.where(chunk < 2, 2 * chunk + 1, 2 * chunk - 4) ^ vocab_index
    line_rows = (chunk * own_count + line_rows % own_count)[:, None]
    line_targets, my_weight = routed(line_facts)
    line_tokens = jnp.swapaxes(line_targets.reshape(4, seq_dev, pos_dev), 0, 1).reshape(1, -1)
    line_placer = (line_rows == line_tokens).astype(BF16)
    sent_count = 2 * own_count

    residual_rows = order.take(residual).reshape(own_count, width)
    own_residual = column_blocks(residual_rows, ctx_index)
    own_blocks = [jnp.stack(own_residual[:2]), jnp.stack(own_residual[2:])]
    own_placer = (line_rows == line_target[None, :]).astype(BF16)
    own_placers = (own_placer[:sent_count], own_placer[sent_count:])
    other_blocks = swap_x(jnp.stack(column_blocks(residual_rows, 1 - ctx_index)))
    learner_own = order.take(learner_hidden).reshape(own_count, width)
    other_targets, other_weight = routed(other_facts)
    other_target = pick(other_targets, vocab_index, own_count, 1)
    other_placer = (line_rows == other_target).astype(BF16)
    both_weight = jnp.concatenate([my_weight, other_weight], axis=0)

    other_slot = other_target.reshape(-1)
    other_slot = other_slot // own_count * per_expert + other_slot % per_expert
    other_place = (other_slot[None, :] == jnp.arange(own_count)[:, None]).astype(BF16)
    places = (rep_index ^ jnp.arange(4)).astype(jnp.int32)
    here, there = ctx_index * 4 + places, (1 - ctx_index) * 4 + places

    rows = jnp.concatenate([other_keys, own_keys], axis=2)
    ready = (queries, rows, line_placer, *own_blocks, *own_placers, other_placer, both_weight)
    ready += (weight_core,)
    ready = lax.optimization_barrier(ready)
    queries, rows, line_placer, *own_blocks = ready[:5]
    own_placers, (other_placer, both_weight, weight_core) = ready[5:7], ready[7:]
    heads_out = order.ends(attend(queries, rows, lengths))

    cuts = ((sent_count,), (own_count, own_count))

    def halved(far, beside):
        return order.ends((far.astype(F32) + beside[:, own_count:].astype(F32)).astype(BF16))

    def summed(mine, beside, across):
        total = mine.astype(F32) + beside[:, :own_count].astype(F32)
        return order.ends(total + across.astype(F32))

    other_blocks = order.waits(other_blocks)
    sent_rows, kept_rows = sorted_rows(order.take(line_placer), heads_out)
    order.ends(kept_rows)
    other_sent = swap_x(sent_rows)
    sent_0, mine_0, far_0 = project(
        order.take(sent_rows, kept_rows),
        own_placers,
        own_blocks[0],
        (out_weight, weight_core),
        cuts,
    )
    order.ends(mine_0)
    teacher = order.ends(line_joined(order.waits(*teacher)))
    beside_0 = swap_z(order.take(sent_0), 1)
    other_sent = order.waits(other_sent)
    beside_0 = order.waits(beside_0)
    across_0 = swap_z(halved(far_0, beside_0), 2)
    weight_y = order.waits(weight_y)
    weight_y_core = swap_rep(weight_y, 1)
    teacher_y = swap_rep(order.take(teacher), 2)
    weight_y_core = order.waits(weight_y_core)

    sent_1, mine_1, far_1 = project(
        order.take(sent_rows, kept_rows),
        own_placers,
        own_blocks[1],
        (weight_y, weight_y_core),
        cuts,
    )
    order.ends(mine_1)
    beside_1 = swap_z(sent_1, 1)

    weights = (out_weight, weight_core, weight_y, weight_y_core)

    def other_part(rows, placer, first, cuts):
        return project(
            (rows,), (placer,), other_blocks[first : first + 2], weights[first : first + 2], (cuts,)
        )

    (sent_2,) = other_part(order.take(other_sent), other_placer[:sent_count], 0, (sent_count,))
    order.ends(sent_2)
    beside_2 = swap_z(sent_2, 1)
    across_0 = order.waits(across_0)
    other_kept = swap_x(order.take(kept_rows))
    (sent_3,) = other_part(order.take(other_sent), other_placer[:sent_count], 2, (sent_count,))
    order.ends(sent_3)
    beside_3 = swap_z(sent_3, 1)

    beside_1, beside_2, other_kept, teacher_y = order.waits(
        beside_1, beside_2, other_kept, teacher_y
    )
    across_1 = swap_z(halved(far_1, beside_1), 2)
    mine_2, far_2 = other_part(
        order.take(other_kept), other_placer[sent_count:], 0, (own_count, own_count)
    )
    order.ends(mine_2)
    across_2 = swap_z(halved(far_2, beside_2), 2)
    mine_3, far_3 = other_part(
        order.take(other_kept), other_placer[sent_count:], 2, (own_count, own_count)
    )
    order.ends(mine_3)
    beside_3, across_1 = order.waits(beside_3, across_1)
    across_3 = swap_z(halved(far_3, beside_3), 2)
    hidden_0 = summed(mine_0, beside_0, across_0)
    hidden_1 = summed(mine_1, beside_1, across_1)
    got_0, got_1 = (swap_x(order.take(part.astype(BF16))) for part in (hidden_0, hidden_1))
    across_2, got_0, got_1 = order.waits(across_2, got_0, got_1)
    hidden_2 = summed(mine_2, beside_2, across_2)
    got_2 = swap_x(hidden_2.astype(BF16))
    heads = lax.all_gather(order.take(learner_head), ("vocab", "rep"))
    heads = heads.reshape(4, 4, *learner_head.shape)
    across_3, got_2 = order.waits(across_3, got_2)
    hidden_3 = summed(mine_3, beside_3, across_3)
    got_3 = swap_x(hidden_3.astype(BF16))
    got_3 = order.waits(got_3)
    learner_x = swap_x(columns(order.take(learner_own), 1 - ctx_index))

    hidden = (hidden_0, hidden_1, hidden_2, hidden_3)
    activated = expert_hidden(
        jnp.concatenate([here, there]).astype(jnp.int32),
        hidden,
        (got_0, got_1, got_2, got_3),
        moe_gain,
        gate_weight,
        up_weight,
    )
    order.ends(activated)
    terms = order.ends(expert_down(there, order.take(activated), down_weight, True))
    learner_x = order.waits(learner_x)
    terms = swap_x(order.take(terms))
    ours = order.ends(expert_down(here, order.take(activated), down_weight, False))
    learner_rows, plane_here, plane_there = learner_parts(
        here, placer, other_place, order.take(learner_own), order.take(learner_x)
    )
    order.ends(learner_rows)
    plane_y = swap_rep(plane_there, 2)
    terms = order.waits(terms)

    places = places.astype(jnp.int32)
    final_rows, squares = final_hidden(
        hidden,
        ours,
        order.take(terms),
        both_weight,
        jnp.stack(column_blocks(final_gain, ctx_index))[:, None],
    )
    order.ends(final_rows)
    other_squares = swap_x(squares[own_count:])
    cores = [swap_rep(order.take(block), 1) for block in (teacher, teacher_y)]
    other_squares, *cores = order.waits(other_squares, *cores)
    teacher = (teacher, cores[0], teacher_y, cores[1])
    teacher_own, teacher_other = [None, None], [None, None]
    teacher_own[0], teacher_other[0] = logits_part(order.take(final_rows), teacher, 0)
    order.ends(teacher_other[0])
    teacher_got = swap_x(teacher_other[0])
    teacher_own[1], teacher_other[1] = logits_part(order.take(final_rows), teacher, 1)
    order.ends(teacher_own[1])
    scale = lax.rsqrt((squares[:own_count, :1] + other_squares[:, :1]) / width + EPSILON)
    teacher_got = order.waits(teacher_got)
    part = order.ends((teacher_own[0] + teacher_got) * scale)
    teacher_got = swap_x(order.take(teacher_other[1]))
    teacher_logits = [line_exchange(part)]

    heads = order.waits(heads)
    learner_own_part, learner_other = (
        jnp.concatenate(parts, axis=1)
        for parts in zip(*(learner_logits_part(places, order.take(learner_rows), heads, i) for i in (0, 1)))
    )
    order.ends(learner_own_part)
    part = order.ends((teacher_own[1] + order.waits(teacher_got)) * scale)
    learner_other = swap_x(order.take(learner_other))
    teacher_logits[0] = order.waits(*teacher_logits[0])
    teacher_logits.append(line_exchange(order.take(part)))
    teacher_logits = [line_joined(order.take(*received)) for received in teacher_logits]
    teacher_logits = order.ends(jnp.concatenate(teacher_logits, axis=1))
    teacher_peak = jnp.max(teacher_logits, axis=1, keepdims=True)
    teacher_lse = teacher_peak + jnp.log(
        jnp.sum(jnp.exp(teacher_logits - teacher_peak), axis=1, keepdims=True)
    )
    plane_y = order.waits(plane_y)
    plane_core = swap_rep(jnp.stack([plane_here[1], plane_y[1]]), 1)
    learner_other, plane_core = order.waits(learner_other, plane_core)
    learner_logits = learner_own_part + learner_other
    learner_peak = jnp.max(learner_logits, axis=1, keepdims=True)
    learner_exp = jnp.exp(learner_logits - learner_peak)
    learner_total = jnp.sum(learner_exp, axis=1, keepdims=True)
    learner_lse = learner_peak + jnp.log(learner_total)

    logit_gap = learner_logits - teacher_logits
    mean_gap = jnp.sum(learner_exp * logit_gap, axis=1, keepdims=True) / learner_total
    divergence = mean_gap - learner_lse + teacher_lse
    row_pos = ctx_index * pos_ctx + vocab_index * pos_dev + jnp.arange(pos_dev)
    live = row_pos[None, :] < lengths[:, None]
    live_sorted = jnp.any(placed & live.reshape(1, -1), axis=1)
    learner_prob = jnp.exp(learner_logits - learner_lse)
    dlogits = jnp.where(
        live_sorted[:, None], learner_prob * (logit_gap - mean_gap), 0.0
    ).astype(BF16)
    dlogits = order.ends(matmul(placer, dlogits, FIRST).astype(BF16))

    rows = own_count // 2
    along_x, along_y = swap_x(dlogits), swap_rep(dlogits, 2)
    along_x, along_y = order.waits(along_x, along_y)
    near, far = swap_x(along_y[:rows]), swap_rep(along_x[rows:], 2)
    near, far = order.waits(near, far)
    mine = order.ends(jnp.concatenate([dlogits, along_x, along_y, near, far], axis=0))
    core = order.waits(swap_rep(mine, 1))
    blocks = (vocab_index ^ jnp.array([1, 3, 0, 2])).astype(jnp.int32)
    parts = head_parts(blocks, mine, core, plane_here, plane_y, plane_core)
    order.ends(parts[0])
    sums = [(kept, swap_z(sent, 1)) for sent, kept in zip(parts[:2], parts[2:])]
    other_grad = order.ends(grad_part(order.take(along_x), heads))
    other_grad = swap_x(other_grad)
    own_grad = order.ends(grad_part(order.take(dlogits), heads))
    for i, (kept, beside) in enumerate(sums):
        beside = order.waits(beside)
        far = order.ends((kept[1].astype(F32) + beside[1].astype(F32)).astype(BF16))
        sums[i] = (kept[0], beside[0], swap_z(far, 2))
    kl_rows = jnp.sum(jnp.where(placed, order.take(divergence), 0.0), axis=0)
    row_kl = order.ends(jnp.where(live, kl_rows.reshape(seq_dev, pos_dev), 0.0))
    other_grad = order.take(other_grad)
    hidden_grad = join_absolute([own_grad, other_grad], ctx_index, 1)
    order.ends(hidden_grad)
    head_grad = jnp.concatenate(
        [
            mine.astype(F32) + beside.astype(F32) + order.take(across).astype(F32)
            for mine, beside, across in sums
        ],
        axis=1,
    ).astype(BF16)
    return (hidden_grad.reshape(seq_dev, pos_dev, width), head_grad, row_kl)


def per_device_general(
    queries,
    key_value,
    residual,
    out_weight,
    moe_gain,
    expert_ids,
    route_gate,
    gate_weight,
    up_weight,
    down_weight,
    final_gain,
    teacher_head,
    learner_hidden,
    learner_head,
    lengths,
):
    seq_dev, pos_ctx, head_cols = queries.shape
    pos_dev = residual.shape[1]
    width = residual.shape[2]
    vocab_count = lax.axis_size("vocab")
    ctx_index = lax.axis_index("ctx")
    vocab_index = lax.axis_index("vocab")
    heads_dev = head_cols // HD
    shared_head = vocab_index * heads_dev // (QH // KVH)
    key_rows = lax.dynamic_slice_in_dim(key_value, shared_head * HD, HD, 3)
    query_heads = queries.reshape(seq_dev, pos_ctx, heads_dev, HD)
    query_pos = ctx_index * pos_ctx + jnp.arange(pos_ctx)
    score_scale = HD ** (-0.5)
    shard_rows = lax.all_gather(key_rows, "ctx", axis=2, tiled=True)
    running_max = jnp.full((seq_dev, pos_ctx, heads_dev), MASKED, jnp.float32)
    key_pos = jnp.arange(shard_rows.shape[2])
    scores = (
        jnp.einsum("sqhd,skd->sqhk", query_heads, shard_rows[0], preferred_element_type=jnp.float32)
        * score_scale
    )
    allowed = (key_pos[None, None, :] <= query_pos[None, :, None]) & (
        key_pos[None, None, :] < lengths[:, None, None]
    )
    allowed = allowed[:, :, None, :]
    scores = jnp.where(allowed, scores, MASKED)
    new_max = jnp.maximum(running_max, jnp.max(scores, axis=-1))
    exponent = jnp.where(allowed, jnp.exp(scores - new_max[..., None]), 0.0)
    running_sum = jnp.sum(exponent, axis=-1)
    weighted = jnp.einsum(
        "sqhk,skd->sqhd",
        exponent.astype(jnp.bfloat16),
        shard_rows[1],
        preferred_element_type=jnp.float32,
    )
    final_max, final_sum, weighted = (new_max, running_sum, weighted)
    heads_out = (
        (weighted / final_sum[..., None]).astype(jnp.bfloat16).reshape(seq_dev * pos_ctx, head_cols)
    )
    mixed = jnp.dot(
        heads_out,
        lax.all_gather(out_weight, ("ctx", "rep"), axis=1, tiled=True),
        preferred_element_type=jnp.float32,
    )
    attn_rows = lax.psum_scatter(
        mixed.reshape(seq_dev, pos_ctx, width).astype(jnp.bfloat16),
        "vocab",
        scatter_dimension=1,
        tiled=True,
    ).astype(jnp.float32)
    hidden_one = residual.astype(jnp.float32) + attn_rows
    own_count = seq_dev * pos_dev
    normed = rms_scale(hidden_one, moe_gain).astype(jnp.bfloat16).reshape(own_count, width)
    route_ids = expert_ids.reshape(own_count, -1)
    inside = route_ids < vocab_count
    chosen = jnp.sum(jnp.where(inside, route_ids, 0), axis=1)
    route_weight = jnp.sum(jnp.where(inside, route_gate.reshape(own_count, -1), 0.0), axis=1)
    per_expert = own_count // vocab_count
    member = (chosen[:, None] == jnp.arange(vocab_count)[None, :]).astype(jnp.int32)
    slot_rank = jnp.sum((jnp.cumsum(member, axis=0) - 1) * member, axis=1)
    target = chosen * per_expert + slot_rank
    placer = (target[None, :] == jnp.arange(own_count)[:, None]).astype(jnp.bfloat16)
    outgoing = jnp.dot(placer, normed, preferred_element_type=jnp.float32).astype(jnp.bfloat16)
    arrived = lax.all_to_all(
        outgoing.reshape(vocab_count, per_expert, width),
        "vocab",
        split_axis=0,
        concat_axis=0,
        tiled=True,
    )
    arrived = arrived.reshape(own_count, width)
    gate_slice = gate_weight[0]
    up_slice = up_weight[0]
    down_slice = down_weight[0]
    contract_last = (((1,), (1,)), ((), ()))
    shard_rows = lax.all_gather(arrived, "ctx", axis=0, tiled=True)
    gate_pre = lax.dot_general(
        shard_rows, gate_slice, contract_last, preferred_element_type=jnp.float32
    )
    up_pre = lax.dot_general(
        shard_rows, up_slice, contract_last, preferred_element_type=jnp.float32
    )
    activated = (jax.nn.silu(gate_pre) * up_pre).astype(jnp.bfloat16)
    expert_terms = jnp.dot(activated, down_slice, preferred_element_type=jnp.float32)
    expert_out = lax.psum_scatter(
        expert_terms.astype(jnp.bfloat16), "ctx", scatter_dimension=0, tiled=True
    )
    returned_rows = lax.all_to_all(
        expert_out.reshape(vocab_count, per_expert, width),
        "vocab",
        split_axis=0,
        concat_axis=0,
        tiled=True,
    )
    restored = lax.dot_general(
        placer,
        returned_rows.reshape(own_count, width),
        (((0,), (0,)), ((), ())),
        preferred_element_type=jnp.float32,
    )
    hidden_two = hidden_one.reshape(own_count, width) + route_weight[:, None] * restored
    final_rows = (
        rms_scale(hidden_two, final_gain).astype(jnp.bfloat16).reshape(seq_dev, pos_dev, width)
    )
    teacher_rows, learner_rows = (
        lax.all_gather(final_rows, "vocab", axis=1, tiled=True),
        lax.all_gather(learner_hidden, "vocab", axis=1, tiled=True),
    )
    learner_full = lax.all_gather(learner_head, ("ctx", "rep"), axis=1, tiled=True)
    teacher_flat = teacher_rows.reshape(-1, width)
    learner_flat = learner_rows.reshape(-1, width)
    teacher_logits = lax.dot_general(
        teacher_flat, teacher_head, contract_last, preferred_element_type=jnp.float32
    )
    learner_logits = lax.dot_general(
        learner_flat, learner_full, contract_last, preferred_element_type=jnp.float32
    )
    logit_gap = learner_logits - teacher_logits
    learner_peak = jnp.max(learner_logits, axis=1)
    teacher_peak = jnp.max(teacher_logits, axis=1)
    learner_peak, teacher_peak = lax.pmax((learner_peak, teacher_peak), "vocab")
    learner_exp = jnp.exp(learner_logits - learner_peak[:, None])
    learner_total, cross_total, teacher_total = lax.psum(
        (
            jnp.sum(learner_exp, axis=1),
            jnp.sum(learner_exp * logit_gap, axis=1),
            jnp.sum(jnp.exp(teacher_logits - teacher_peak[:, None]), axis=1),
        ),
        "vocab",
    )
    learner_lse = learner_peak + jnp.log(learner_total)
    teacher_lse = teacher_peak + jnp.log(teacher_total)
    mean_gap = cross_total / learner_total
    divergence = mean_gap - learner_lse + teacher_lse
    row_pos = ctx_index * pos_ctx + jnp.arange(pos_ctx)
    live_rows = (row_pos[None, :] < lengths[:, None]).reshape(-1)
    learner_prob = jnp.exp(learner_logits - learner_lse[:, None])
    dlogits = jnp.where(
        live_rows[:, None], learner_prob * (logit_gap - mean_gap[:, None]), 0.0
    ).astype(jnp.bfloat16)
    kl_block = jnp.where(live_rows, divergence, 0.0).reshape(seq_dev, pos_ctx)
    row_kl = lax.dynamic_slice_in_dim(kl_block, vocab_index * pos_dev, pos_dev, 1)
    by_position = jnp.swapaxes(dlogits.reshape(seq_dev, pos_ctx, -1), 0, 1)
    shard_rows = by_position
    grad_rows = lax.psum_scatter(
        jnp.einsum(
            "psv,vd->psd", shard_rows, learner_full, preferred_element_type=jnp.float32
        ).astype(jnp.bfloat16),
        "vocab",
        scatter_dimension=0,
        tiled=True,
    ).astype(jnp.float32)
    hidden_grad = jnp.swapaxes(grad_rows, 0, 1).astype(jnp.bfloat16)
    head_sum = lax.psum_scatter(
        lax.dot_general(
            learner_flat, dlogits, (((0,), (0,)), ((), ())), preferred_element_type=jnp.float32
        ).astype(jnp.bfloat16),
        ("ctx", "rep"),
        scatter_dimension=0,
        tiled=True,
    ).astype(jnp.float32)
    head_grad = jnp.transpose(head_sum).astype(jnp.bfloat16)
    return (hidden_grad, head_grad, row_kl)


def solution(mesh):
    placed = (
        P("rep", "ctx", "vocab"),
        P(None, "rep", "ctx", None),
        P("rep", ("ctx", "vocab"), None),
        P("vocab", ("ctx", "rep")),
        P(),
        P("rep", ("ctx", "vocab"), None),
        P("rep", ("ctx", "vocab"), None),
        P("vocab", "ctx", None),
        P("vocab", "ctx", None),
        P("vocab", "ctx", None),
        P(),
        P("vocab", None),
        P("rep", ("ctx", "vocab"), None),
        P("vocab", ("ctx", "rep")),
        P("rep"),
    )
    shape = dict(mesh.shape)
    swaps = (shape["ctx"], shape["vocab"], shape["rep"]) == (2, 4, 4)
    return jax.shard_map(
        per_device if swaps else per_device_general,
        mesh=mesh,
        in_specs=placed,
        out_specs=(
            P("rep", ("ctx", "vocab"), None),
            P("vocab", ("ctx", "rep")),
            P("rep", ("ctx", "vocab")),
        ),
        check_vma=False,
    )
```

```python
import functools

import jax
import jax.numpy as jnp
from jax import lax
from jax.experimental import pallas as pl
from jax.experimental.pallas import tpu as pltpu
from jax.sharding import PartitionSpec as P

QH = 64
KVH = 4
HD = 128

EPSILON = 1e-06
MASKED = -1e30
PLANE = ("ctx", "rep")
LAST = (((1,), (1,)), ((), ()))
FIRST = (((0,), (0,)), ((), ()))
F32 = jnp.float32
BF16 = jnp.bfloat16


def matmul(left, right, dims=(((1,), (0,)), ((), ()))):
    return lax.dot_general(left, right, dims, preferred_element_type=F32)


def rms_scale(values, gain):
    mean_square = jnp.mean(values * values, axis=-1, keepdims=True)
    return values * lax.rsqrt(mean_square + EPSILON) * gain


class Order:
    def __init__(self):
        self.last = None

    def take(self, *values):
        if self.last is None:
            return values if len(values) > 1 else values[0]
        values = lax.optimization_barrier((*values, self.last))[:-1]
        return values if len(values) > 1 else values[0]

    def ends(self, value):
        self.last = value
        return value

    def waits(self, *values):
        values = lax.optimization_barrier((*values, self.last))[:-1]
        self.last = values[0]
        return values if len(values) > 1 else values[0]


def swap_x(value):
    return lax.ppermute(value, "ctx", [(0, 1), (1, 0)])


def swap_rep(value, offset):
    return lax.ppermute(value, "rep", [(i, i ^ offset) for i in range(4)])


def swap_z(value, offset):
    return lax.ppermute(value, "vocab", [(i, i ^ offset) for i in range(4)])


def pick(value, index, size, axis):
    return lax.dynamic_slice_in_dim(value, index * size, size, axis)


def split_relative(value, index, count, axis):
    size = value.shape[axis] // count
    return [pick(value, index ^ r, size, axis) for r in range(count)]


def join_absolute(blocks, index, axis):
    count = len(blocks)
    return jnp.concatenate(
        [
            lax.select_n(index, *[blocks[j ^ i] for i in range(count)])
            for j in range(count)
        ],
        axis=axis,
    )


def line_gather(own):
    return [own] + [swap_z(own, r) for r in (1, 2, 3)]


def line_exchange(value):
    blocks = split_relative(value, lax.axis_index("vocab"), 4, 0)
    return [blocks[0]] + [swap_z(blocks[r], r) for r in (1, 2, 3)]


def line_joined(received):
    return join_absolute(received, lax.axis_index("vocab"), 0)


HEADS_STEP = 4


def attend_kernel(facts, query, rows, out):
    pos_ctx = query.shape[1]
    keys = rows.shape[2]
    length = facts[pl.program_id(0)]
    query_pos = facts[pl.num_programs(0)] + lax.broadcasted_iota(jnp.int32, (pos_ctx, keys), 0)
    key_pos = facts[pl.num_programs(0) + 1] + lax.broadcasted_iota(jnp.int32, (pos_ctx, keys), 1)
    allowed = (key_pos <= query_pos) & (key_pos < length) & (key_pos >= 0)
    bias = jnp.where(allowed, 0.0, MASKED)
    for head in range(query.shape[2] // HD):
        cols = slice(head * HD, (head + 1) * HD)
        scores = matmul(query[0, :, cols], rows[0, 0], LAST) * HD ** (-0.5) + bias
        peak = jnp.max(scores, axis=-1, keepdims=True)
        exponent = jnp.exp(scores - peak)
        total = jnp.sum(exponent, axis=-1, keepdims=True)
        weighted = matmul(exponent.astype(BF16), rows[1, 0])
        out[:, cols] = (weighted / total).astype(BF16)


def attend(queries, rows, lengths):
    seq_dev, pos_ctx, head_cols = queries.shape
    ctx_index = lax.axis_index("ctx")
    facts = jnp.concatenate([lengths, jnp.stack([ctx_index * pos_ctx, (ctx_index - 1) * pos_ctx])])
    step_cols = HEADS_STEP * HD
    return pl.pallas_call(
        attend_kernel,
        out_shape=jax.ShapeDtypeStruct((seq_dev * pos_ctx, head_cols), BF16),
        grid_spec=pltpu.PrefetchScalarGridSpec(
            num_scalar_prefetch=1,
            grid=(seq_dev, head_cols // step_cols),
            in_specs=[
                pl.BlockSpec(
                    (1, pos_ctx, step_cols), lambda s, h, facts: (s, 0, h)
                ),
                pl.BlockSpec((2, 1, rows.shape[2], HD), lambda s, h, facts: (0, s, 0, 0)),
            ],
            out_specs=pl.BlockSpec((pos_ctx, step_cols), lambda s, h, facts: (s, h)),
        ),
        cost_estimate=pl.CostEstimate(flops=0, bytes_accessed=0, transcendentals=0),
        compiler_params=pltpu.CompilerParams(vmem_limit_bytes=32 * 2**20),
        name="attend",
    )(facts, queries, rows)


FREE = pl.CostEstimate(flops=0, bytes_accessed=0, transcendentals=0)
VMEM_BYTES = 32 * 2**20


def whole(shape):
    return pl.BlockSpec(shape, lambda *_: (0,) * len(shape))


def project_kernel(count, parts, *refs):
    groups = len(parts)
    rows, placers, refs = refs[:groups], refs[groups : 2 * groups], refs[2 * groups :]
    residual, weights, outs = refs[0], refs[1 : 1 + count], list(refs[1 + count :])
    for row, placer, part in zip(rows, placers, parts):
        targets = [outs.pop(0) for _ in part]
        for r in range(count):
            total = matmul(row[...], weights[r][...]) + matmul(placer[...], residual[r])
            first = 0
            for target, size in zip(targets, part):
                target[r] = total[first : first + size].astype(BF16)
                first += size


def project(rows, placers, residual, weights, parts):
    count = len(weights)
    size = weights[0].shape[1]
    tile = size // 2
    cuts = [part for group in parts for part in group]
    return pl.pallas_call(
        functools.partial(project_kernel, count, parts),
        out_shape=[jax.ShapeDtypeStruct((count, part, size), BF16) for part in cuts],
        grid=(2,),
        in_specs=[whole(value.shape) for value in (*rows, *placers)]
        + [pl.BlockSpec((count, residual.shape[1], tile), lambda j: (0, 0, j))]
        + [pl.BlockSpec((weights[0].shape[0], tile), lambda j: (0, j))] * count,
        out_specs=[pl.BlockSpec((count, part, tile), lambda j: (0, 0, j)) for part in cuts],
        cost_estimate=FREE,
        compiler_params=pltpu.CompilerParams(vmem_limit_bytes=VMEM_BYTES),
        name="project",
    )(*rows, *placers, residual, *weights)


def sort_kernel(placer, heads, sent, kept):
    half = sent.shape[0]
    sent[...] = matmul(placer[:half], heads[...]).astype(BF16)
    kept[...] = matmul(placer[half:], heads[...]).astype(BF16)


def sorted_rows(placer, heads):
    rows, width = heads.shape
    tile = width // 4
    return pl.pallas_call(
        sort_kernel,
        out_shape=[jax.ShapeDtypeStruct((rows // 2, width), BF16)] * 2,
        grid=(4,),
        in_specs=[whole(placer.shape), pl.BlockSpec((rows, tile), lambda j: (0, j))],
        out_specs=[pl.BlockSpec((rows // 2, tile), lambda j: (0, j))] * 2,
        cost_estimate=FREE,
        compiler_params=pltpu.CompilerParams(vmem_limit_bytes=VMEM_BYTES),
        name="sorted_rows",
    )(placer, heads)


def logits_kernel(rows, *refs):
    blocks, (own, other) = refs[:-2], refs[-2:]
    count = own.shape[0]
    total = 0.0
    for r, block in enumerate(blocks):
        total += matmul(rows[r], block[...].reshape(own.shape[1], -1), LAST)
    own[...] = total[:count]
    other[...] = total[count:]


def logits_part(rows, heads, part):
    vocab_count, entries, size = heads[0].shape
    tile = vocab_count // 2 * entries
    count = rows.shape[1] // 2
    block = (vocab_count // 2, entries, size)
    return pl.pallas_call(
        logits_kernel,
        out_shape=[jax.ShapeDtypeStruct((count, tile), F32)] * 2,
        grid=(1,),
        in_specs=[whole(rows.shape)] + [pl.BlockSpec(block, lambda j: (part, 0, 0))] * len(heads),
        out_specs=[whole((count, tile))] * 2,
        cost_estimate=FREE,
        compiler_params=pltpu.CompilerParams(vmem_limit_bytes=VMEM_BYTES),
        name="logits",
    )(rows, *heads)


def learner_logits_kernel(facts, rows, *refs):
    logits_kernel(rows, *[ref.at[:, 0] for ref in refs[:4]], *refs[4:])


def learner_logits_part(facts, rows, heads, part):
    vocab_count, rep_count, entries, size = heads.shape
    tile = vocab_count // 2 * entries
    count = rows.shape[1] // 2
    block = (vocab_count // 2, 1, entries, size)
    return pl.pallas_call(
        learner_logits_kernel,
        out_shape=[jax.ShapeDtypeStruct((count, tile), F32)] * 2,
        grid_spec=pltpu.PrefetchScalarGridSpec(
            num_scalar_prefetch=1,
            grid=(1,),
            in_specs=[whole(rows.shape)]
            + [
                pl.BlockSpec(block, lambda j, facts, r=r: (part, facts[r], 0, 0))
                for r in range(rep_count)
            ],
            out_specs=[whole((count, tile))] * 2,
        ),
        cost_estimate=FREE,
        compiler_params=pltpu.CompilerParams(vmem_limit_bytes=48 * 2**20),
        name="logits",
    )(facts, rows, *[heads] * rep_count)


def join_kernel(facts, *refs):
    sources, out = refs[:-1], refs[-1]
    for r, source in enumerate(sources):

        @pl.when((facts[0] ^ pl.program_id(0)) == r)
        def _():
            out[0] = source[...]


def joined(index, blocks):
    count = len(blocks)
    shape = blocks[0].shape
    return pl.pallas_call(
        join_kernel,
        out_shape=jax.ShapeDtypeStruct((count, *shape), blocks[0].dtype),
        grid_spec=pltpu.PrefetchScalarGridSpec(
            num_scalar_prefetch=1,
            grid=(count,),
            in_specs=[whole(shape)] * count,
            out_specs=pl.BlockSpec((1, *shape), lambda j, facts: (j, 0, 0)),
        ),
        cost_estimate=FREE,
        compiler_params=pltpu.CompilerParams(vmem_limit_bytes=VMEM_BYTES),
        name="joined",
    )(index.reshape(1).astype(jnp.int32), *blocks)


def learner_kernel(facts, placer, other_placer, own, other, rows, near, far):
    r = pl.program_id(0)
    count = own.shape[0]
    rows[0, :count] = matmul(placer[...], own[...]).astype(BF16)
    rows[0, count:] = matmul(other_placer[...], other[...]).astype(BF16)
    for out, here in ((near, r < 2), (far, r >= 2)):

        @pl.when(here)
        def _():
            out[0, :count] = own[...]
            out[0, count:] = other[...]


def learner_parts(facts, placer, other_placer, own, other):
    count = own.shape[0]
    size = own.shape[1] // 8
    shape = (1, 2 * count, size)
    return pl.pallas_call(
        learner_kernel,
        out_shape=[
            jax.ShapeDtypeStruct((blocks, 2 * count, size), BF16) for blocks in (4, 2, 2)
        ],
        grid_spec=pltpu.PrefetchScalarGridSpec(
            num_scalar_prefetch=1,
            grid=(4,),
            in_specs=[
                whole(placer.shape),
                whole(placer.shape),
                pl.BlockSpec((count, size), lambda r, facts: (0, facts[r])),
                pl.BlockSpec((count, size), lambda r, facts: (0, r)),
            ],
            out_specs=[
                pl.BlockSpec(shape, lambda r, facts: (r, 0, 0)),
                pl.BlockSpec(shape, lambda r, facts: (jnp.minimum(r, 1), 0, 0)),
                pl.BlockSpec(shape, lambda r, facts: (jnp.maximum(r - 2, 0), 0, 0)),
            ],
        ),
        cost_estimate=FREE,
        compiler_params=pltpu.CompilerParams(vmem_limit_bytes=VMEM_BYTES),
        name="learner_parts",
    )(facts, placer, other_placer, own, other)


def head_kernel(facts, mine, core, here, along_y, other, *outs):
    i = pl.program_id(0)
    count = here.shape[1]
    total = matmul(mine[:count], here[0], FIRST) + matmul(mine[count:], along_y[0], FIRST)
    total += matmul(core[:count], other[0], FIRST) + matmul(core[count:], other[1], FIRST)
    total = total.astype(BF16)
    size = total.shape[1] // 2
    for group, now in ((outs[:2], i < 2), (outs[2:], i >= 2)):

        @pl.when(now)
        def _():
            for k, out in enumerate(group):
                out[0] = total[:, k * size : (k + 1) * size]


def head_parts(facts, mine, core, here, along_y, other):
    rows, vocab = mine.shape
    tile, size = vocab // 4, here.shape[2] // 2
    shape = (1, tile, size)
    first = pl.BlockSpec(shape, lambda i, facts: (jnp.minimum(i, 1), 0, 0))
    rest = pl.BlockSpec(shape, lambda i, facts: (jnp.maximum(i - 2, 0), 0, 0))
    return pl.pallas_call(
        head_kernel,
        out_shape=[jax.ShapeDtypeStruct((2, tile, size), BF16)] * 4,
        grid_spec=pltpu.PrefetchScalarGridSpec(
            num_scalar_prefetch=1,
            grid=(4,),
            in_specs=[pl.BlockSpec((rows, tile), lambda i, facts: (0, facts[i]))] * 2
            + [whole(value.shape) for value in (here, along_y, other)],
            out_specs=[first, first, rest, rest],
        ),
        cost_estimate=FREE,
        compiler_params=pltpu.CompilerParams(vmem_limit_bytes=VMEM_BYTES),
        name="head_parts",
    )(facts, mine, core, here, along_y, other)


def grad_kernel(rows, block, out):
    out[...] = matmul(rows[...], block[:, 0].reshape(rows.shape[1], -1)).astype(BF16)


def grad_part(rows, heads):
    vocab_count, rep_count, entries, size = heads.shape
    return pl.pallas_call(
        grad_kernel,
        out_shape=jax.ShapeDtypeStruct((rows.shape[0], rep_count * size), BF16),
        grid=(rep_count,),
        in_specs=[
            whole(rows.shape),
            pl.BlockSpec((vocab_count, 1, entries, size), lambda r: (0, r, 0, 0)),
        ],
        out_specs=pl.BlockSpec((rows.shape[0], size), lambda r: (0, r)),
        cost_estimate=FREE,
        compiler_params=pltpu.CompilerParams(vmem_limit_bytes=48 * 2**20),
        name="hidden_grad",
    )(rows, heads)


def expert_kernel(facts, *refs):
    hidden, got, (gain, gate, up, out, normed) = refs[:4], refs[4:8], refs[8:]
    count, size = hidden[0].shape[1:]
    width = normed.shape[1]

    @pl.when(pl.program_id(0) == 0)
    def _():
        own = [part[r] for part in hidden[:2] for r in range(2)]
        own += [part[r].astype(F32) for part in got[2:] for r in range(2)]
        partner = [part[r] for part in hidden[2:] for r in range(2)]
        partner += [part[r].astype(F32) for part in got[:2] for r in range(2)]
        for first, blocks in ((0, own), (count, partner)):
            squares = sum(jnp.sum(block * block, axis=1, keepdims=True) for block in blocks)
            scale = lax.rsqrt(squares / width + EPSILON)
            for i, block in enumerate(blocks):
                column = pl.multiple_of(facts[i] * size, size)
                normed[first : first + count, pl.ds(column, size)] = (
                    block * scale * gain[:, pl.ds(column, size)]
                ).astype(BF16)

    rows = normed[...]
    gate_pre = matmul(rows, gate[0], LAST)
    up_pre = matmul(rows, up[0], LAST)
    out[...] = (gate_pre / (1.0 + jnp.exp(-gate_pre)) * up_pre).astype(BF16)


def expert_hidden(facts, hidden, got, gain, gate, up):
    count, size = hidden[0].shape[1:]
    units, width = gate.shape[1:]
    tile = units // 3
    return pl.pallas_call(
        expert_kernel,
        out_shape=jax.ShapeDtypeStruct((2 * count, units), BF16),
        grid_spec=pltpu.PrefetchScalarGridSpec(
            num_scalar_prefetch=1,
            grid=(3,),
            in_specs=[whole(part.shape) for part in (*hidden, *got)]
            + [whole((1, width))]
            + [pl.BlockSpec((1, tile, width), lambda j, facts: (0, j, 0))] * 2,
            out_specs=pl.BlockSpec((2 * count, tile), lambda j, facts: (0, j)),
            scratch_shapes=[pltpu.VMEM((2 * count, width), BF16)],
        ),
        cost_estimate=FREE,
        compiler_params=pltpu.CompilerParams(vmem_limit_bytes=48 * 2**20),
        name="expert_hidden",
    )(facts, *hidden, *got, gain[None], gate, up)


def down_kernel(turned, facts, rows, weight, out):
    total = matmul(rows[...], weight[0]).astype(BF16)
    half = total.shape[0] // 2
    if turned:
        out[0, :half] = total[half:]
        out[0, half:] = total[:half]
    else:
        out[0] = total


def expert_down(facts, rows, weight, turned):
    count = facts.shape[0]
    units = rows.shape[1]
    size = weight.shape[2] // 8
    return pl.pallas_call(
        functools.partial(down_kernel, turned),
        out_shape=jax.ShapeDtypeStruct((count, rows.shape[0], size), BF16),
        grid_spec=pltpu.PrefetchScalarGridSpec(
            num_scalar_prefetch=1,
            grid=(count,),
            in_specs=[
                whole(rows.shape),
                pl.BlockSpec((1, units, size), lambda r, facts: (0, 0, facts[r])),
            ],
            out_specs=pl.BlockSpec((1, rows.shape[0], size), lambda r, facts: (r, 0, 0)),
        ),
        cost_estimate=FREE,
        compiler_params=pltpu.CompilerParams(vmem_limit_bytes=48 * 2**20),
        name="expert_down",
    )(facts, rows, weight)


def final_kernel(*refs):
    hidden_parts, (ours, terms, weight, gain, rows, squares) = refs[:4], refs[4:]
    total = 0.0
    for r in range(4):
        parts = [part[r % 2] for part in hidden_parts[r // 2 :: 2]]
        hidden = jnp.concatenate(parts, axis=0)
        out = (ours[r].astype(F32) + terms[r].astype(F32)).astype(BF16).astype(F32)
        hidden = hidden + weight[...] * out
        total += jnp.sum(hidden * hidden, axis=1, keepdims=True)
        rows[r] = (hidden * gain[r]).astype(BF16)
    squares[...] = jnp.broadcast_to(total, squares.shape)


def final_hidden(hidden, ours, terms, weight, gain):
    values = (*hidden, ours, terms, weight, gain)
    return pl.pallas_call(
        final_kernel,
        grid=(1,),
        in_specs=[whole(value.shape) for value in values],
        out_specs=[whole(ours.shape), whole((ours.shape[1], 128))],
        out_shape=[
            jax.ShapeDtypeStruct(ours.shape, BF16),
            jax.ShapeDtypeStruct((ours.shape[1], 128), F32),
        ],
        cost_estimate=FREE,
        compiler_params=pltpu.CompilerParams(vmem_limit_bytes=VMEM_BYTES),
        name="final_hidden",
    )(*values)


def per_device(
    queries,
    key_value,
    residual,
    out_weight,
    moe_gain,
    expert_ids,
    route_gate,
    gate_weight,
    up_weight,
    down_weight,
    final_gain,
    teacher_head,
    learner_hidden,
    learner_head,
    lengths,
):
    seq_dev, pos_ctx, head_cols = queries.shape
    pos_dev, width = residual.shape[1:]
    own_count = seq_dev * pos_dev
    half = width // 2
    ctx_index = lax.axis_index("ctx")
    vocab_index = lax.axis_index("vocab")
    rep_index = lax.axis_index("rep")
    plane = ctx_index * 4 + rep_index
    per_expert = own_count // 4
    vocab = 4 * teacher_head.shape[0]
    order = Order()

    def column_blocks(value, ctx):
        size = value.shape[-1] // 8
        return [pick(value, ctx * 4 + (rep_index ^ r), size, value.ndim - 1) for r in range(4)]

    def columns(value, ctx):
        return jnp.concatenate(column_blocks(value, ctx), axis=-1)

    shared_head = vocab_index * (head_cols // HD) // (QH // KVH)
    own_keys = lax.dynamic_slice_in_dim(key_value, shared_head * HD, HD, 3)
    other_keys = swap_x(own_keys)
    weight_y = swap_rep(out_weight, 2)
    weight_core = swap_rep(out_weight, 1)
    teacher_slice = pick(teacher_head, plane, width // 8, 1)
    teacher = line_gather(teacher_slice[None])

    expert_ids = lax.optimization_barrier((expert_ids, own_keys))[0]
    route_ids = expert_ids.reshape(own_count, -1)
    inside = route_ids < 4
    chosen = jnp.sum(jnp.where(inside, route_ids, 0), axis=1)
    route_weight = jnp.sum(jnp.where(inside, route_gate.reshape(own_count, -1), 0.0), axis=1)
    member = (chosen[:, None] == jnp.arange(4)[None, :]).astype(jnp.int32)
    slot_rank = jnp.sum((jnp.cumsum(member, axis=0) - 1) * member, axis=1)
    target = chosen * per_expert + slot_rank
    placed = target[None, :] == jnp.arange(own_count)[:, None]
    placer = placed.astype(BF16)
    line_target = chosen * own_count + vocab_index * per_expert + slot_rank
    line_facts = line_joined(line_gather(jnp.stack([line_target.astype(F32), route_weight])[None]))
    other_facts = swap_x(line_facts)
    order.ends(line_facts)
    mine = vocab_index * own_count + jnp.arange(own_count)[:, None]

    def routed(facts):
        targets = facts[:, 0].astype(jnp.int32).reshape(1, -1)
        weights = jnp.where(targets == mine, facts[:, 1].reshape(1, -1), 0.0)
        return targets, jnp.sum(weights, axis=1, keepdims=True)

    line_rows = jnp.arange(seq_dev * pos_ctx)
    chunk = line_rows // own_count
    chunk = jnp.where(chunk < 2, 2 * chunk + 1, 2 * chunk - 4) ^ vocab_index
    line_rows = (chunk * own_count + line_rows % own_count)[:, None]
    line_targets, my_weight = routed(line_facts)
    line_tokens = jnp.swapaxes(line_targets.reshape(4, seq_dev, pos_dev), 0, 1).reshape(1, -1)
    line_placer = (line_rows == line_tokens).astype(BF16)
    sent_count = 2 * own_count

    residual_rows = order.take(residual).reshape(own_count, width)
    own_residual = column_blocks(residual_rows, ctx_index)
    own_blocks = [jnp.stack(own_residual[:2]), jnp.stack(own_residual[2:])]
    own_placer = (line_rows == line_target[None, :]).astype(BF16)
    own_placers = (own_placer[:sent_count], own_placer[sent_count:])
    other_blocks = swap_x(jnp.stack(column_blocks(residual_rows, 1 - ctx_index)))
    learner_own = order.take(learner_hidden).reshape(own_count, width)
    other_targets, other_weight = routed(other_facts)
    other_target = pick(other_targets, vocab_index, own_count, 1)
    other_placer = (line_rows == other_target).astype(BF16)
    both_weight = jnp.concatenate([my_weight, other_weight], axis=0)

    other_slot = other_target.reshape(-1)
    other_slot = other_slot // own_count * per_expert + other_slot % per_expert
    other_place = (other_slot[None, :] == jnp.arange(own_count)[:, None]).astype(BF16)
    places = (rep_index ^ jnp.arange(4)).astype(jnp.int32)
    here, there = ctx_index * 4 + places, (1 - ctx_index) * 4 + places

    rows = jnp.concatenate([other_keys, own_keys], axis=2)
    ready = (queries, rows, line_placer, *own_blocks, *own_placers, other_placer, both_weight)
    ready += (weight_core,)
    ready = lax.optimization_barrier(ready)
    queries, rows, line_placer, *own_blocks = ready[:5]
    own_placers, (other_placer, both_weight, weight_core) = ready[5:7], ready[7:]
    heads_out = order.ends(attend(queries, rows, lengths))

    cuts = ((sent_count,), (own_count, own_count))

    def halved(far, beside):
        return order.ends((far.astype(F32) + beside[:, own_count:].astype(F32)).astype(BF16))

    def summed(mine, beside, across):
        total = mine.astype(F32) + beside[:, :own_count].astype(F32)
        return order.ends(total + across.astype(F32))

    other_blocks = order.waits(other_blocks)
    sent_rows, kept_rows = sorted_rows(order.take(line_placer), heads_out)
    order.ends(kept_rows)
    other_sent = swap_x(sent_rows)
    sent_0, mine_0, far_0 = project(
        order.take(sent_rows, kept_rows),
        own_placers,
        own_blocks[0],
        (out_weight, weight_core),
        cuts,
    )
    order.ends(mine_0)
    teacher = order.ends(line_joined(order.waits(*teacher)))
    beside_0 = swap_z(order.take(sent_0), 1)
    other_sent = order.waits(other_sent)
    beside_0 = order.waits(beside_0)
    across_0 = swap_z(halved(far_0, beside_0), 2)
    weight_y = order.waits(weight_y)
    weight_y_core = swap_rep(weight_y, 1)
    teacher_y = swap_rep(order.take(teacher), 2)
    weight_y_core = order.waits(weight_y_core)

    sent_1, mine_1, far_1 = project(
        order.take(sent_rows, kept_rows),
        own_placers,
        own_blocks[1],
        (weight_y, weight_y_core),
        cuts,
    )
    order.ends(mine_1)
    beside_1 = swap_z(sent_1, 1)

    weights = (out_weight, weight_core, weight_y, weight_y_core)

    def other_part(rows, placer, first, cuts):
        return project(
            (rows,), (placer,), other_blocks[first : first + 2], weights[first : first + 2], (cuts,)
        )

    (sent_2,) = other_part(order.take(other_sent), other_placer[:sent_count], 0, (sent_count,))
    order.ends(sent_2)
    beside_2 = swap_z(sent_2, 1)
    across_0 = order.waits(across_0)
    other_kept = swap_x(order.take(kept_rows))
    (sent_3,) = other_part(order.take(other_sent), other_placer[:sent_count], 2, (sent_count,))
    order.ends(sent_3)
    beside_3 = swap_z(sent_3, 1)

    beside_1, beside_2, other_kept, teacher_y = order.waits(
        beside_1, beside_2, other_kept, teacher_y
    )
    across_1 = swap_z(halved(far_1, beside_1), 2)
    mine_2, far_2 = other_part(
        order.take(other_kept), other_placer[sent_count:], 0, (own_count, own_count)
    )
    order.ends(mine_2)
    across_2 = swap_z(halved(far_2, beside_2), 2)
    mine_3, far_3 = other_part(
        order.take(other_kept), other_placer[sent_count:], 2, (own_count, own_count)
    )
    order.ends(mine_3)
    beside_3, across_1 = order.waits(beside_3, across_1)
    across_3 = swap_z(halved(far_3, beside_3), 2)
    hidden_0 = summed(mine_0, beside_0, across_0)
    hidden_1 = summed(mine_1, beside_1, across_1)
    got_0, got_1 = (swap_x(order.take(part.astype(BF16))) for part in (hidden_0, hidden_1))
    across_2, got_0, got_1 = order.waits(across_2, got_0, got_1)
    hidden_2 = summed(mine_2, beside_2, across_2)
    got_2 = swap_x(hidden_2.astype(BF16))
    heads = lax.all_gather(order.take(learner_head), ("vocab", "rep"))
    heads = heads.reshape(4, 4, *learner_head.shape)
    across_3, got_2 = order.waits(across_3, got_2)
    hidden_3 = summed(mine_3, beside_3, across_3)
    got_3 = swap_x(hidden_3.astype(BF16))
    got_3 = order.waits(got_3)
    learner_x = swap_x(columns(order.take(learner_own), 1 - ctx_index))

    hidden = (hidden_0, hidden_1, hidden_2, hidden_3)
    activated = expert_hidden(
        jnp.concatenate([here, there]).astype(jnp.int32),
        hidden,
        (got_0, got_1, got_2, got_3),
        moe_gain,
        gate_weight,
        up_weight,
    )
    order.ends(activated)
    terms = order.ends(expert_down(there, order.take(activated), down_weight, True))
    learner_x = order.waits(learner_x)
    terms = swap_x(order.take(terms))
    ours = order.ends(expert_down(here, order.take(activated), down_weight, False))
    learner_rows, plane_here, plane_there = learner_parts(
        here, placer, other_place, order.take(learner_own), order.take(learner_x)
    )
    order.ends(learner_rows)
    plane_y = swap_rep(plane_there, 2)
    terms = order.waits(terms)

    places = places.astype(jnp.int32)
    final_rows, squares = final_hidden(
        hidden,
        ours,
        order.take(terms),
        both_weight,
        jnp.stack(column_blocks(final_gain, ctx_index))[:, None],
    )
    order.ends(final_rows)
    other_squares = swap_x(squares[own_count:])
    cores = [swap_rep(order.take(block), 1) for block in (teacher, teacher_y)]
    other_squares, *cores = order.waits(other_squares, *cores)
    teacher = (teacher, cores[0], teacher_y, cores[1])
    teacher_own, teacher_other = [None, None], [None, None]
    teacher_own[0], teacher_other[0] = logits_part(order.take(final_rows), teacher, 0)
    order.ends(teacher_other[0])
    teacher_got = swap_x(teacher_other[0])
    teacher_own[1], teacher_other[1] = logits_part(order.take(final_rows), teacher, 1)
    order.ends(teacher_own[1])
    scale = lax.rsqrt((squares[:own_count, :1] + other_squares[:, :1]) / width + EPSILON)
    teacher_got = order.waits(teacher_got)
    part = order.ends((teacher_own[0] + teacher_got) * scale)
    teacher_got = swap_x(order.take(teacher_other[1]))
    teacher_logits = [line_exchange(part)]

    heads = order.waits(heads)
    learner_own_part, learner_other = (
        jnp.concatenate(parts, axis=1)
        for parts in zip(*(learner_logits_part(places, order.take(learner_rows), heads, i) for i in (0, 1)))
    )
    order.ends(learner_own_part)
    part = order.ends((teacher_own[1] + order.waits(teacher_got)) * scale)
    learner_other = swap_x(order.take(learner_other))
    teacher_logits[0] = order.waits(*teacher_logits[0])
    teacher_logits.append(line_exchange(order.take(part)))
    teacher_logits = [line_joined(order.take(*received)) for received in teacher_logits]
    teacher_logits = order.ends(jnp.concatenate(teacher_logits, axis=1))
    teacher_peak = jnp.max(teacher_logits, axis=1, keepdims=True)
    teacher_lse = teacher_peak + jnp.log(
        jnp.sum(jnp.exp(teacher_logits - teacher_peak), axis=1, keepdims=True)
    )
    plane_y = order.waits(plane_y)
    plane_core = swap_rep(jnp.stack([plane_here[1], plane_y[1]]), 1)
    learner_other, plane_core = order.waits(learner_other, plane_core)
    learner_logits = learner_own_part + learner_other
    learner_peak = jnp.max(learner_logits, axis=1, keepdims=True)
    learner_exp = jnp.exp(learner_logits - learner_peak)
    learner_total = jnp.sum(learner_exp, axis=1, keepdims=True)
    learner_lse = learner_peak + jnp.log(learner_total)

    logit_gap = learner_logits - teacher_logits
    mean_gap = jnp.sum(learner_exp * logit_gap, axis=1, keepdims=True) / learner_total
    divergence = mean_gap - learner_lse + teacher_lse
    row_pos = ctx_index * pos_ctx + vocab_index * pos_dev + jnp.arange(pos_dev)
    live = row_pos[None, :] < lengths[:, None]
    live_sorted = jnp.any(placed & live.reshape(1, -1), axis=1)
    learner_prob = jnp.exp(learner_logits - learner_lse)
    dlogits = jnp.where(
        live_sorted[:, None], learner_prob * (logit_gap - mean_gap), 0.0
    ).astype(BF16)
    dlogits = order.ends(matmul(placer, dlogits, FIRST).astype(BF16))

    rows = own_count // 2
    along_x, along_y = swap_x(dlogits), swap_rep(dlogits, 2)
    along_x, along_y = order.waits(along_x, along_y)
    near, far = swap_x(along_y[:rows]), swap_rep(along_x[rows:], 2)
    near, far = order.waits(near, far)
    mine = order.ends(jnp.concatenate([dlogits, along_x, along_y, near, far], axis=0))
    core = order.waits(swap_rep(mine, 1))
    blocks = (vocab_index ^ jnp.array([1, 3, 0, 2])).astype(jnp.int32)
    parts = head_parts(blocks, mine, core, plane_here, plane_y, plane_core)
    order.ends(parts[0])
    sums = [(kept, swap_z(sent, 1)) for sent, kept in zip(parts[:2], parts[2:])]
    other_grad = order.ends(grad_part(order.take(along_x), heads))
    other_grad = swap_x(other_grad)
    own_grad = order.ends(grad_part(order.take(dlogits), heads))
    for i, (kept, beside) in enumerate(sums):
        beside = order.waits(beside)
        far = order.ends((kept[1].astype(F32) + beside[1].astype(F32)).astype(BF16))
        sums[i] = (kept[0], beside[0], swap_z(far, 2))
    kl_rows = jnp.sum(jnp.where(placed, order.take(divergence), 0.0), axis=0)
    row_kl = order.ends(jnp.where(live, kl_rows.reshape(seq_dev, pos_dev), 0.0))
    other_grad = order.take(other_grad)
    hidden_grad = join_absolute([own_grad, other_grad], ctx_index, 1)
    order.ends(hidden_grad)
    head_grad = jnp.concatenate(
        [
            mine.astype(F32) + beside.astype(F32) + order.take(across).astype(F32)
            for mine, beside, across in sums
        ],
        axis=1,
    ).astype(BF16)
    return (hidden_grad.reshape(seq_dev, pos_dev, width), head_grad, row_kl)


def per_device_general(
    queries,
    key_value,
    residual,
    out_weight,
    moe_gain,
    expert_ids,
    route_gate,
    gate_weight,
    up_weight,
    down_weight,
    final_gain,
    teacher_head,
    learner_hidden,
    learner_head,
    lengths,
):
    seq_dev, pos_ctx, head_cols = queries.shape
    pos_dev = residual.shape[1]
    width = residual.shape[2]
    vocab_count = lax.axis_size("vocab")
    ctx_index = lax.axis_index("ctx")
    vocab_index = lax.axis_index("vocab")
    heads_dev = head_cols // HD
    shared_head = vocab_index * heads_dev // (QH // KVH)
    key_rows = lax.dynamic_slice_in_dim(key_value, shared_head * HD, HD, 3)
    query_heads = queries.reshape(seq_dev, pos_ctx, heads_dev, HD)
    query_pos = ctx_index * pos_ctx + jnp.arange(pos_ctx)
    score_scale = HD ** (-0.5)
    shard_rows = lax.all_gather(key_rows, "ctx", axis=2, tiled=True)
    running_max = jnp.full((seq_dev, pos_ctx, heads_dev), MASKED, jnp.float32)
    key_pos = jnp.arange(shard_rows.shape[2])
    scores = (
        jnp.einsum("sqhd,skd->sqhk", query_heads, shard_rows[0], preferred_element_type=jnp.float32)
        * score_scale
    )
    allowed = (key_pos[None, None, :] <= query_pos[None, :, None]) & (
        key_pos[None, None, :] < lengths[:, None, None]
    )
    allowed = allowed[:, :, None, :]
    scores = jnp.where(allowed, scores, MASKED)
    new_max = jnp.maximum(running_max, jnp.max(scores, axis=-1))
    exponent = jnp.where(allowed, jnp.exp(scores - new_max[..., None]), 0.0)
    running_sum = jnp.sum(exponent, axis=-1)
    weighted = jnp.einsum(
        "sqhk,skd->sqhd",
        exponent.astype(jnp.bfloat16),
        shard_rows[1],
        preferred_element_type=jnp.float32,
    )
    final_max, final_sum, weighted = (new_max, running_sum, weighted)
    heads_out = (
        (weighted / final_sum[..., None]).astype(jnp.bfloat16).reshape(seq_dev * pos_ctx, head_cols)
    )
    mixed = jnp.dot(
        heads_out,
        lax.all_gather(out_weight, ("ctx", "rep"), axis=1, tiled=True),
        preferred_element_type=jnp.float32,
    )
    attn_rows = lax.psum_scatter(
        mixed.reshape(seq_dev, pos_ctx, width).astype(jnp.bfloat16),
        "vocab",
        scatter_dimension=1,
        tiled=True,
    ).astype(jnp.float32)
    hidden_one = residual.astype(jnp.float32) + attn_rows
    own_count = seq_dev * pos_dev
    normed = rms_scale(hidden_one, moe_gain).astype(jnp.bfloat16).reshape(own_count, width)
    route_ids = expert_ids.reshape(own_count, -1)
    inside = route_ids < vocab_count
    chosen = jnp.sum(jnp.where(inside, route_ids, 0), axis=1)
    route_weight = jnp.sum(jnp.where(inside, route_gate.reshape(own_count, -1), 0.0), axis=1)
    per_expert = own_count // vocab_count
    member = (chosen[:, None] == jnp.arange(vocab_count)[None, :]).astype(jnp.int32)
    slot_rank = jnp.sum((jnp.cumsum(member, axis=0) - 1) * member, axis=1)
    target = chosen * per_expert + slot_rank
    placer = (target[None, :] == jnp.arange(own_count)[:, None]).astype(jnp.bfloat16)
    outgoing = jnp.dot(placer, normed, preferred_element_type=jnp.float32).astype(jnp.bfloat16)
    arrived = lax.all_to_all(
        outgoing.reshape(vocab_count, per_expert, width),
        "vocab",
        split_axis=0,
        concat_axis=0,
        tiled=True,
    )
    arrived = arrived.reshape(own_count, width)
    gate_slice = gate_weight[0]
    up_slice = up_weight[0]
    down_slice = down_weight[0]
    contract_last = (((1,), (1,)), ((), ()))
    shard_rows = lax.all_gather(arrived, "ctx", axis=0, tiled=True)
    gate_pre = lax.dot_general(
        shard_rows, gate_slice, contract_last, preferred_element_type=jnp.float32
    )
    up_pre = lax.dot_general(
        shard_rows, up_slice, contract_last, preferred_element_type=jnp.float32
    )
    activated = (jax.nn.silu(gate_pre) * up_pre).astype(jnp.bfloat16)
    expert_terms = jnp.dot(activated, down_slice, preferred_element_type=jnp.float32)
    expert_out = lax.psum_scatter(
        expert_terms.astype(jnp.bfloat16), "ctx", scatter_dimension=0, tiled=True
    )
    returned_rows = lax.all_to_all(
        expert_out.reshape(vocab_count, per_expert, width),
        "vocab",
        split_axis=0,
        concat_axis=0,
        tiled=True,
    )
    restored = lax.dot_general(
        placer,
        returned_rows.reshape(own_count, width),
        (((0,), (0,)), ((), ())),
        preferred_element_type=jnp.float32,
    )
    hidden_two = hidden_one.reshape(own_count, width) + route_weight[:, None] * restored
    final_rows = (
        rms_scale(hidden_two, final_gain).astype(jnp.bfloat16).reshape(seq_dev, pos_dev, width)
    )
    teacher_rows, learner_rows = (
        lax.all_gather(final_rows, "vocab", axis=1, tiled=True),
        lax.all_gather(learner_hidden, "vocab", axis=1, tiled=True),
    )
    learner_full = lax.all_gather(learner_head, ("ctx", "rep"), axis=1, tiled=True)
    teacher_flat = teacher_rows.reshape(-1, width)
    learner_flat = learner_rows.reshape(-1, width)
    teacher_logits = lax.dot_general(
        teacher_flat, teacher_head, contract_last, preferred_element_type=jnp.float32
    )
    learner_logits = lax.dot_general(
        learner_flat, learner_full, contract_last, preferred_element_type=jnp.float32
    )
    logit_gap = learner_logits - teacher_logits
    learner_peak = jnp.max(learner_logits, axis=1)
    teacher_peak = jnp.max(teacher_logits, axis=1)
    learner_peak, teacher_peak = lax.pmax((learner_peak, teacher_peak), "vocab")
    learner_exp = jnp.exp(learner_logits - learner_peak[:, None])
    learner_total, cross_total, teacher_total = lax.psum(
        (
            jnp.sum(learner_exp, axis=1),
            jnp.sum(learner_exp * logit_gap, axis=1),
            jnp.sum(jnp.exp(teacher_logits - teacher_peak[:, None]), axis=1),
        ),
        "vocab",
    )
    learner_lse = learner_peak + jnp.log(learner_total)
    teacher_lse = teacher_peak + jnp.log(teacher_total)
    mean_gap = cross_total / learner_total
    divergence = mean_gap - learner_lse + teacher_lse
    row_pos = ctx_index * pos_ctx + jnp.arange(pos_ctx)
    live_rows = (row_pos[None, :] < lengths[:, None]).reshape(-1)
    learner_prob = jnp.exp(learner_logits - learner_lse[:, None])
    dlogits = jnp.where(
        live_rows[:, None], learner_prob * (logit_gap - mean_gap[:, None]), 0.0
    ).astype(jnp.bfloat16)
    kl_block = jnp.where(live_rows, divergence, 0.0).reshape(seq_dev, pos_ctx)
    row_kl = lax.dynamic_slice_in_dim(kl_block, vocab_index * pos_dev, pos_dev, 1)
    by_position = jnp.swapaxes(dlogits.reshape(seq_dev, pos_ctx, -1), 0, 1)
    shard_rows = by_position
    grad_rows = lax.psum_scatter(
        jnp.einsum(
            "psv,vd->psd", shard_rows, learner_full, preferred_element_type=jnp.float32
        ).astype(jnp.bfloat16),
        "vocab",
        scatter_dimension=0,
        tiled=True,
    ).astype(jnp.float32)
    hidden_grad = jnp.swapaxes(grad_rows, 0, 1).astype(jnp.bfloat16)
    head_sum = lax.psum_scatter(
        lax.dot_general(
            learner_flat, dlogits, (((0,), (0,)), ((), ())), preferred_element_type=jnp.float32
        ).astype(jnp.bfloat16),
        ("ctx", "rep"),
        scatter_dimension=0,
        tiled=True,
    ).astype(jnp.float32)
    head_grad = jnp.transpose(head_sum).astype(jnp.bfloat16)
    return (hidden_grad, head_grad, row_kl)


def solution(mesh):
    placed = (
        P("rep", "ctx", "vocab"),
        P(None, "rep", "ctx", None),
        P("rep", ("ctx", "vocab"), None),
        P("vocab", ("ctx", "rep")),
        P(),
        P("rep", ("ctx", "vocab"), None),
        P("rep", ("ctx", "vocab"), None),
        P("vocab", "ctx", None),
        P("vocab", "ctx", None),
        P("vocab", "ctx", None),
        P(),
        P("vocab", None),
        P("rep", ("ctx", "vocab"), None),
        P("vocab", ("ctx", "rep")),
        P("rep"),
    )
    shape = dict(mesh.shape)
    swaps = (shape["ctx"], shape["vocab"], shape["rep"]) == (2, 4, 4)
    return jax.shard_map(
        per_device if swaps else per_device_general,
        mesh=mesh,
        in_specs=placed,
        out_specs=(
            P("rep", ("ctx", "vocab"), None),
            P("vocab", ("ctx", "rep")),
            P("rep", ("ctx", "vocab")),
        ),
        check_vma=False,
    )
```
